32 devices in a mesh: dp: 16 (over z, x, core), mp: 2 (over y).
Axes of the slice: x: 2, y: 2, z: 4, core: 2. Of those that a mesh axis runs over, the one named last changes fastest.
Arguments:
- tokens: bfloat16 [49152, 640], P('dp'), may hold values from -6 to 6
- lengths: int32 [16, 6], P('dp'), may hold values from 0 to 1024, as said below
- gain_one: bfloat16 [640], replicated, may hold values from 0.5 to 1.5
- shift_one: bfloat16 [640], replicated, may hold values from -1 to 1
- w_qkv: bfloat16 [3, 640, 640], P(None, None, 'mp'), may hold values from -0.3125 to 0.3125
- b_qkv: bfloat16 [3, 640], P(None, 'mp'), may hold values from -1.5 to 1.5
- w_out: bfloat16 [640, 640], P('mp'), may hold values from -1 to 1
- b_out: bfloat16 [640], replicated, may hold values from -1 to 1
- gain_two: bfloat16 [640], replicated, may hold values from 0.5 to 1.5
- shift_two: bfloat16 [640], replicated, may hold values from -1 to 1
- w_up: bfloat16 [640, 2560], P(None, 'mp'), may hold values from -0.25 to 0.25
- b_up: bfloat16 [2560], P('mp'), may hold values from -1.5 to 1.5
- w_down: bfloat16 [2560, 640], P('mp'), may hold values from -0.125 to 0.125
- b_down: bfloat16 [640], replicated, may hold values from -1 to 1
- cotangent: bfloat16 [49152, 640], P('dp'), may hold values from -6 to 6
Outputs:
- out_tokens: bfloat16 [49152, 640], P('dp')
- grad_tokens: bfloat16 [49152, 640], P('dp')
- grad_gain_one: float32 [640], replicated
- grad_shift_one: float32 [640], replicated
- grad_w_qkv: float32 [3, 640, 640], P(None, 'dp', 'mp')
- grad_b_qkv: float32 [3, 640], P(None, 'mp')
- grad_w_out: float32 [640, 640], P('mp', 'dp')
- grad_b_out: float32 [640], replicated
- grad_gain_two: float32 [640], replicated
- grad_shift_two: float32 [640], replicated
- grad_w_up: float32 [640, 2560], P('dp', 'mp')
- grad_b_up: float32 [2560], P('mp')
- grad_w_down: float32 [2560, 640], P('mp', 'dp')
- grad_b_down: float32 [640], replicated
The draws below stay inside these ranges and needn't reach their ends.
Inputs may be any that keep to these rules, and one draw needn't show every extreme that they name: `lengths`: each window's pair of entries is either (1024, 0), one sequence filling the window, or (512, 512), two sequences; exactly half of all windows hold one sequence.
All inputs are finite; a program needn't handle non-finite values.
Results may differ from the reference program's by a relative error of at most 0.017.
Values may be sent and summed in bfloat16 or wider, within the bound.
A program may use at most 320 MiB of HBM per device.

```python
import jax
import jax.numpy as jnp
from jax import lax

D = 640
HEADS = 20
HD = 32
FF = 2560
LONG = 1024
SHORT = 512
TOK_DEV = 3072
WINDOWS = 3
TOKENS = 49152
N_DP = 16
N_MP = 2


def draw_lengths(key, part):
    key = jax.random.fold_in(key, 5)
    window_count = N_DP * WINDOWS
    order = jax.random.permutation(key, window_count)
    single = (order < window_count // 2).astype(jnp.int32).reshape(N_DP, WINDOWS)
    first_len = single * LONG + (1 - single) * SHORT
    second_len = (1 - single) * SHORT
    return jnp.stack([first_len, second_len], -1).reshape(N_DP, 2 * WINDOWS).astype(jnp.int32)


def raised(entries, stream_key, source, target, parts, factor):
    def block_of(axis_at):
        return (jnp.arange(entries.shape[axis_at]) // (entries.shape[axis_at] // parts)).reshape((-1,) + (1,) * (entries.ndim - 1 - axis_at))

    first = jax.random.permutation(stream_key, parts)[block_of(target)]
    far = (block_of(target) + parts // 2) % parts
    return jnp.where((block_of(source) == first) | (block_of(source) == far), factor * entries, entries)


def shard_levels(key, shape, shards, low, largest):
    gain, own = 1.0, jax.random.fold_in(key, 6)
    for dim, shards_of in shards:
        heights = jnp.exp(jax.random.uniform(jax.random.fold_in(own, dim), (shards_of,), jnp.float32, low / len(shards), largest / len(shards)))
        gain = gain * jnp.repeat(heights, shape[dim] // shards_of).reshape([-1 if axis == dim else 1 for axis in range(len(shape))])
    return gain


def normal_values(own_key, dims, scale, bound, pieces=(), kind=jnp.bfloat16):
    gain = shard_levels(own_key, dims, pieces, -0.22, 0.18) if pieces else 1.0
    values = jax.random.normal(own_key, dims, jnp.float32) * scale * gain
    return jnp.minimum(jnp.maximum(values, -bound), bound).astype(kind)


def heavy_noise(rng, extent, scale, most, pieces, heavy, held_as=jnp.bfloat16):
    drawn = scale * jax.random.normal(rng, extent, jnp.float32)
    if pieces:
        drawn = drawn * shard_levels(rng, extent, pieces, -0.22, 0.18)
    return jnp.clip(raised(drawn, jax.random.fold_in(rng, 3), *heavy), -most, most).astype(held_as)


def setup_inputs(seed: int = 0) -> dict:
    streams_of = jax.random.split(jax.random.key(seed), 16)
    return {
        "tokens": normal_values(streams_of[0], (TOKENS, D), 1.0, 6.0, ((0, 16),)),
        "lengths": draw_lengths(jax.random.fold_in(streams_of[15], 71), 0),
        "gain_one": jnp.clip(1.0 + 0.1 * jax.random.normal(streams_of[2], (D,), jnp.float32), 0.5, 1.5).astype(jnp.bfloat16),
        "shift_one": normal_values(streams_of[3], (D,), 0.2, 1.0),
        "w_qkv": normal_values(streams_of[4], (3, D, D), (D // 2) ** -0.5, 0.3125, ((2, 2),)),
        "b_qkv": normal_values(streams_of[5], (3, D), 0.3, 1.5, ((1, 2),)),
        "w_out": normal_values(streams_of[6], (D, D), (D // 16) ** -0.5, 1.0, ((0, 2),)),
        "b_out": normal_values(streams_of[7], (D,), 0.2, 1.0),
        "gain_two": jnp.clip(1.0 + 0.1 * jax.random.normal(streams_of[8], (D,), jnp.float32), 0.5, 1.5).astype(jnp.bfloat16),
        "shift_two": normal_values(streams_of[9], (D,), 0.2, 1.0),
        "w_up": normal_values(streams_of[10], (D, FF), D ** -0.5, 0.25, ((1, 2),)),
        "b_up": normal_values(streams_of[11], (FF,), 0.3, 1.5, ((0, 2),)),
        "w_down": normal_values(streams_of[12], (FF, D), FF ** -0.5, 0.125, ((0, 2),)),
        "b_down": normal_values(streams_of[13], (D,), 0.2, 1.0),
        "cotangent": heavy_noise(streams_of[14], (TOKENS, D), 1.0, 6.0, ((0, 16),), (0, 1, 16, 2.0)),
    }


@jax.custom_vjp
def low(v):
    return lax.optimization_barrier(v.astype(jnp.bfloat16)).astype(jnp.float32)

@jax.custom_vjp
def low_back(v):
    return v

def low_keep(v):
    return (low(v), None)

def low_pass(kept, grad):
    return (grad,)

def back_keep(v):
    return (v, None)

def back_low(kept, grad):
    return (low(grad),)
low.defvjp(low_keep, low_pass)
low_back.defvjp(back_keep, back_low)
epsilon = 1e-05
rotary_base = 10000.0
highest = lax.Precision.HIGHEST

def normalize(values, scale_vec, shift_vec):
    centred = values - lax.optimization_barrier(jnp.mean(values, -1, keepdims=True))
    spread = lax.optimization_barrier(jnp.mean(centred * centred, -1, keepdims=True))
    return centred * lax.rsqrt(spread + epsilon) * scale_vec + shift_vec

def rotate(values, cosines, sines):
    half_width = values.shape[-1] // 2
    first_half = values[..., :half_width]
    second_half = values[..., half_width:]
    return jnp.concatenate([first_half * cosines - second_half * sines, second_half * cosines + first_half * sines], -1)

def documents(starts):
    inside = jnp.arange(LONG, dtype=jnp.int32)
    later_doc = (inside[None, :] >= starts[:, None]).astype(jnp.int32)
    place_in = inside[None, :] - starts[:, None] * later_doc
    return (later_doc, place_in)

def attend_window(queries, keys_rot, values, later_doc):
    scores = low_back(jnp.einsum('qhe,khe->hqk', queries, keys_rot, precision=highest))
    same_doc = later_doc[:, None] == later_doc[None, :]
    scores = jnp.where(same_doc[None], scores, -1e+30)
    row_max = lax.optimization_barrier(jnp.max(scores, -1, keepdims=True))
    expo_vals = jnp.exp(scores - row_max)
    probs = expo_vals / lax.optimization_barrier(jnp.sum(expo_vals, -1, keepdims=True))
    return jnp.einsum('hqk,khe->qhe', low(probs), values, precision=highest)

def window_step(packed):
    return jax.checkpoint(attend_window)(*packed)

def forward(residual, params, later_doc, cosines, sines):
    gain_one, shift_one, w_qkv, b_qkv, w_out, b_out, gain_two, shift_two, w_up, b_up, w_down, b_down = params
    row_count = residual.shape[0]
    per_shard = D // N_MP
    ff_shard = FF // N_MP
    normed_one = low(normalize(residual, gain_one, shift_one))
    spread_one = low_back(jnp.broadcast_to(normed_one[:, None, :], (row_count, N_MP, D)))
    projected = jnp.einsum('tgd,sdgc->tsgc', spread_one, w_qkv.reshape(3, D, N_MP, per_shard), precision=highest)
    projected = low_back(projected + b_qkv.reshape(3, N_MP, per_shard)[None])
    projected = projected.reshape(row_count, 3, HEADS, HD)
    queries = low(rotate(projected[:, 0], cosines, sines) * HD ** (-0.5))
    keys_rot = low(rotate(projected[:, 1], cosines, sines))
    values = low(projected[:, 2])
    shape_win = (row_count // LONG, LONG, HEADS, HD)
    attended = lax.map(window_step, (queries.reshape(shape_win), keys_rot.reshape(shape_win), values.reshape(shape_win), later_doc))
    attended = low_back(low(attended.reshape(row_count, N_MP, per_shard)))
    heads_out = jnp.einsum('tgc,gcd->tgd', attended, w_out.reshape(N_MP, per_shard, D), precision=highest)
    mixed = lax.optimization_barrier(jnp.sum(low(low_back(heads_out)), 1)) + b_out + residual
    normed_two = low(normalize(mixed, gain_two, shift_two))
    spread_two = low_back(jnp.broadcast_to(normed_two[:, None, :], (row_count, N_MP, D)))
    pre_act = jnp.einsum('tgd,dgf->tgf', spread_two, w_up.reshape(D, N_MP, ff_shard), precision=highest)
    pre_act = low_back(pre_act + b_up.reshape(N_MP, ff_shard))
    active = low(jax.nn.gelu(pre_act, approximate=False))
    down_out = jnp.einsum('tgf,gfd->tgd', active, w_down.reshape(N_MP, ff_shard, D), precision=highest)
    return lax.optimization_barrier(jnp.sum(low(low_back(down_out)), 1)) + b_down + mixed

def reference(tokens, lengths, gain_one, shift_one, w_qkv, b_qkv, w_out, b_out, gain_two, shift_two, w_up, b_up, w_down, b_down, cotangent):
    params = tuple((item.astype(jnp.float32) for item in (gain_one, shift_one, w_qkv, b_qkv, w_out, b_out, gain_two, shift_two, w_up, b_up, w_down, b_down)))
    starts_all = lengths[:, 0::2]
    frequency = rotary_base ** (-jnp.arange(HD // 2, dtype=jnp.float32) * 2.0 / HD)

    def block_step(totals, packed):
        block_in, starts, block_grad = packed
        later_doc, place_in = documents(starts)
        angles = place_in.reshape(-1).astype(jnp.float32)[:, None] * frequency[None, :]
        cosines = jnp.cos(angles)[:, None, :]
        sines = jnp.sin(angles)[:, None, :]

        def apply_layer(residual, weights):
            return forward(residual, weights, later_doc, cosines, sines)
        result, pullback = jax.vjp(apply_layer, block_in.astype(jnp.float32), params)
        grad_in, grad_params = pullback(block_grad.astype(jnp.float32))
        totals = jax.tree.map(jnp.add, totals, grad_params)
        return (totals, (result.astype(jnp.bfloat16), grad_in.astype(jnp.bfloat16)))
    zero_grads = jax.tree.map(jnp.zeros_like, params)
    inputs = (tokens.reshape(N_DP, TOK_DEV, D), starts_all, cotangent.reshape(N_DP, TOK_DEV, D))
    totals, (out_blocks, grad_blocks) = lax.scan(block_step, zero_grads, inputs)
    out_tokens = out_blocks.reshape(TOKENS, D)
    grad_tokens = grad_blocks.reshape(TOKENS, D)
    return (out_tokens, grad_tokens, totals[0], totals[1], totals[2], totals[3], totals[4], totals[5], totals[6], totals[7], totals[8], totals[9], totals[10], totals[11])
```

```python
import functools

import jax
import jax.numpy as jnp
import numpy as np
from jax import lax
from jax.experimental import pallas as pl
from jax.experimental.pallas import tpu as pltpu
from jax.sharding import PartitionSpec as P

HD = 32
LONG = 1024
BLK = 512
GROUP = 128
epsilon = 1e-05
rotary_base = 10000.0
log2_e = 1.4426950408889634
ln_2 = 0.6931471805599453

f32 = jnp.float32
bf16 = jnp.bfloat16
NT = (((1,), (1,)), ((), ()))
NN = (((1,), (0,)), ((), ()))
TN = (((0,), (0,)), ((), ()))
VMEM_LIMIT = 60 << 20


def dot(a, b, dims=NN):
    return lax.dot_general(a, b, dims, preferred_element_type=f32)


def rope_tables():
    place = np.arange(LONG, dtype=np.float64)[:, None]
    frequency = rotary_base ** (-np.arange(HD // 2, dtype=np.float64) * 2.0 / HD)
    angles = place * frequency[None, :]
    cosines = np.concatenate([np.cos(angles), np.cos(angles)], 1)
    sines = np.concatenate([-np.sin(angles), np.sin(angles)], 1)
    repeat = GROUP // HD
    return (
        np.tile(cosines, (1, repeat)).astype(np.float32),
        np.tile(sines, (1, repeat)).astype(np.float32),
    )


def swap_halves(x):
    lane = lax.broadcasted_iota(jnp.int32, (1, GROUP), 1)
    low = (lane // (HD // 2)) % 2 == 0
    return jnp.where(low, pltpu.roll(x, GROUP - HD // 2, 1), pltpu.roll(x, HD // 2, 1))


def rotate(x, cosines, sines):
    return x * cosines + swap_halves(x) * sines


def rotate_back(x, cosines, sines):
    return x * cosines - swap_halves(x) * sines


def normalize(values):
    centred = values - jnp.mean(values, -1, keepdims=True)
    inverse = lax.rsqrt(jnp.mean(centred * centred, -1, keepdims=True) + epsilon)
    return (centred * inverse, inverse)


def normalize_back(normed, inverse, grad_normed):
    mean_grad = jnp.mean(grad_normed, -1, keepdims=True)
    mean_proj = jnp.mean(grad_normed * normed, -1, keepdims=True)
    return inverse * (grad_normed - mean_grad - normed * mean_proj)


FLAG, BLOCK, TABLE, PLACE = 0, 3, 7, 11


def project_kernel(sc, x_ref, gain, shift, w_ref, b_ref, cos, sin, q_ref, k_ref, v_ref):
    normed, _ = normalize(x_ref[...].astype(f32))
    hidden = (normed * gain[...] + shift[...]).astype(bf16)
    scale = HD ** (-0.5) * log2_e
    width = w_ref.shape[2]
    for s in range(3):
        out = dot(hidden, w_ref[s]) + b_ref[s : s + 1, :]
        if s == 2:
            v_ref[...] = out.astype(bf16)
            continue
        for j in range(width // GROUP):
            cols = slice(j * GROUP, (j + 1) * GROUP)
            part = rotate(out[:, cols], cos[...], sin[...])
            if s == 0:
                q_ref[:, cols] = (part * scale).astype(bf16)
            else:
                k_ref[:, cols] = part.astype(bf16)


def project(sc, tokens, gain, shift, w, b, cos, sin):
    d = tokens.shape[1]
    rows = 4 * BLK
    whole = lambda *shape: pl.BlockSpec(shape, lambda i, s: (0,) * len(shape))
    table = pl.BlockSpec((BLK, GROUP), lambda i, s: (s[TABLE + i], 0))
    out = pl.BlockSpec((BLK, d), lambda i, s: (i, 0))
    return pl.pallas_call(
        project_kernel,
        grid_spec=pltpu.PrefetchScalarGridSpec(
            num_scalar_prefetch=1,
            grid=(4,),
            in_specs=[
                pl.BlockSpec((BLK, d), lambda i, s: (s[BLOCK + i], 0)),
                whole(1, d),
                whole(1, d),
                whole(3, d, d),
                whole(3, d),
                table,
                table,
            ],
            out_specs=[out, out, out],
        ),
        out_shape=[jax.ShapeDtypeStruct((rows, d), bf16)] * 3,
        compiler_params=pltpu.CompilerParams(vmem_limit_bytes=VMEM_LIMIT),
        cost_estimate=pl.CostEstimate(
            flops=2 * rows * d * 3 * d, bytes_accessed=rows * d * 8, transcendentals=0
        ),
        name="project",
    )(sc, tokens, gain, shift, w, b, cos, sin)


def attend_body(q, k_ref, v_ref, o_ref, l_ref, e_ref, store, start, count):
    lane = lax.broadcasted_iota(jnp.int32, (1, GROUP), 1) // HD
    heads = GROUP // HD
    chunks = count // BLK
    values_t = v_ref[pl.ds(start, count), :].T
    ones = jnp.ones((16, count), bf16)
    outs, inverses = [], []

    def score(h, c):
        keys = k_ref[pl.ds(start + c * BLK, BLK), :]
        scores = dot(jnp.where(lane == h, keys, jnp.zeros_like(keys)), q, NT)
        store[h % 2, c * BLK : (c + 1) * BLK, :] = scores
        return jnp.max(scores.reshape(BLK // 8, 8, BLK), axis=0)

    def score_max(h, c, so_far):
        found = score(h, c)
        return found if so_far is None else jnp.maximum(so_far, found)

    top = None
    for c in range(chunks):
        top = score_max(0, c, top)
    row_max = jnp.max(top, axis=0, keepdims=True)
    for h in range(heads):
        top = None
        total = None
        stacked = jnp.concatenate([values_t[HD * h : HD * (h + 1)], ones], 0)
        for c in range(chunks):
            if h + 1 < heads:
                top = score_max(h + 1, c, top)
            rows = slice(c * BLK, (c + 1) * BLK)
            expo = jnp.exp2(store[h % 2, rows, :] - row_max).astype(bf16)
            e_ref[h, pl.ds(start + c * BLK, BLK), :] = expo
            part = dot(stacked[:, rows], expo)
            total = part if total is None else total + part
        inverse = 1.0 / total[HD : HD + 1]
        outs.append(total[:HD] * inverse)
        inverses.append(jnp.broadcast_to(inverse, (HD, BLK)))
        if h + 1 < heads:
            row_max = jnp.max(top, axis=0, keepdims=True)
    o_ref[...] = jnp.concatenate(outs, 0).T.astype(bf16)
    l_ref[...] = jnp.concatenate(inverses, 0).T


def attend_kernel(sc, q_ref, k_ref, v_ref, o_ref, l_ref, e_ref, store):
    b = pl.program_id(1)
    refs = (k_ref, v_ref, o_ref, l_ref, e_ref, store)

    @pl.when(sc[FLAG + b] == 1)
    def _():
        attend_body(q_ref[...], *refs, 0, LONG)

    @pl.when(sc[FLAG + b] == 0)
    def _():
        start = pl.multiple_of(jnp.where(b == 1, BLK, 0), BLK)
        attend_body(q_ref[...], *refs, start, BLK)


def attend(sc, q, k, v):
    d = q.shape[1]
    groups = d // GROUP
    heads = GROUP // HD
    own = 3 * BLK
    qs = pl.BlockSpec((BLK, GROUP), lambda g, b, s: (b, g))
    ks = pl.BlockSpec((LONG, GROUP), lambda g, b, s: (b // 2, g))
    es = pl.BlockSpec((heads, LONG, BLK), lambda g, b, s: (g * 3 + b, 0, 0))
    return pl.pallas_call(
        attend_kernel,
        grid_spec=pltpu.PrefetchScalarGridSpec(
            num_scalar_prefetch=1,
            grid=(groups, 3),
            in_specs=[qs, ks, ks],
            out_specs=[qs, qs, es],
            scratch_shapes=[pltpu.VMEM((2, LONG, BLK), f32)],
        ),
        out_shape=[
            jax.ShapeDtypeStruct((own, d), bf16),
            jax.ShapeDtypeStruct((own, d), f32),
            jax.ShapeDtypeStruct((groups * 3 * heads, LONG, BLK), bf16),
        ],
        compiler_params=pltpu.CompilerParams(vmem_limit_bytes=VMEM_LIMIT),
        cost_estimate=pl.CostEstimate(
            flops=25_000_000_000, bytes_accessed=80_000_000, transcendentals=31_000_000
        ),
        name="attend",
    )(sc, q, k, v)


def attend_back_body(
    q_ref, k_ref, v_ref, do_ref, o_ref, l_ref, e_ref, cos, sin, dq_ref, prod, dk_sum, dv_sum, start, count
):
    lane = lax.broadcasted_iota(jnp.int32, (1, GROUP), 1) // HD
    heads = GROUP // HD
    q = q_ref[...]
    do = (do_ref[...].astype(f32) * l_ref[...]).astype(bf16)
    both = do.astype(f32) * o_ref[...].astype(f32)
    upper = both.astype(bf16)
    lower = (both - upper.astype(f32)).astype(bf16)
    pick = (
        lax.broadcasted_iota(jnp.int32, (8, GROUP), 0)
        == lax.broadcasted_iota(jnp.int32, (8, GROUP), 1) // HD
    )
    pick = pick.astype(f32).astype(bf16)
    delta = dot(pick, upper, NT) + dot(pick, lower, NT)
    keys_t = k_ref[pl.ds(start, count), :].T
    chunks = count // BLK
    tiles = [(h, c) for h in range(heads) for c in range(chunks)]

    def grad_probs(i):
        h, c = tiles[i]
        values = v_ref[pl.ds(start + c * BLK, BLK), :]
        prod[i % 2] = dot(jnp.where(lane == h, values, jnp.zeros_like(values)), do, NT)

    grad_probs(0)
    dq_t = [None] * heads
    for i, (h, c) in enumerate(tiles):
        if i + 1 < len(tiles):
            grad_probs(i + 1)
        rows = pl.ds(start + c * BLK, BLK)
        expo = e_ref[h, rows, :]
        ds = (expo.astype(f32) * (prod[i % 2] - delta[h : h + 1])).astype(bf16)
        dv_sum[rows, :] += dot(expo, jnp.where(lane == h, do, jnp.zeros_like(do)))
        dk_sum[rows, :] += dot(ds, jnp.where(lane == h, q, jnp.zeros_like(q)))
        part = dot(keys_t[HD * h : HD * (h + 1), c * BLK : (c + 1) * BLK], ds)
        dq_t[h] = part if dq_t[h] is None else dq_t[h] + part
    dq = jnp.concatenate(dq_t, 0).T * (HD ** (-0.5))
    dq_ref[...] = rotate_back(dq, cos[...], sin[...]).astype(bf16)


def attend_back_kernel(
    sc, q_ref, k_ref, v_ref, do_ref, o_ref, l_ref, e_ref, cos, sin, cos0, sin0, cos1, sin1,
    dq_ref, dk_ref, dv_ref, prod, dk_sum, dv_sum,
):
    b = pl.program_id(1)
    refs = (q_ref, k_ref, v_ref, do_ref, o_ref, l_ref, e_ref, cos, sin, dq_ref, prod, dk_sum, dv_sum)

    @pl.when(b != 1)
    def _():
        dk_sum[...] = jnp.zeros_like(dk_sum)
        dv_sum[...] = jnp.zeros_like(dv_sum)

    @pl.when(sc[FLAG + b] == 1)
    def _():
        attend_back_body(*refs, 0, LONG)

    @pl.when(sc[FLAG + b] == 0)
    def _():
        start = pl.multiple_of(jnp.where(b == 1, BLK, 0), BLK)
        attend_back_body(*refs, start, BLK)

    @pl.when(b != 0)
    def _():
        for j, (c, s) in enumerate(((cos0, sin0), (cos1, sin1))):
            rows = slice(j * BLK, (j + 1) * BLK)
            dk = dk_sum[rows, :] * ln_2
            dk_ref[rows, :] = rotate_back(dk, c[...], s[...]).astype(bf16)
            dv_ref[rows, :] = dv_sum[rows, :].astype(bf16)


def attend_back(sc, q, k, v, do, o, inverse, expo, cos, sin):
    d = q.shape[1]
    groups = d // GROUP
    heads = GROUP // HD
    own = 3 * BLK
    rows = 4 * BLK
    qs = pl.BlockSpec((BLK, GROUP), lambda g, b, s: (b, g))
    ks = pl.BlockSpec((LONG, GROUP), lambda g, b, s: (b // 2, g))
    es = pl.BlockSpec((heads, LONG, BLK), lambda g, b, s: (g * 3 + b, 0, 0))
    tq = pl.BlockSpec((BLK, GROUP), lambda g, b, s: (s[TABLE + b], 0))
    t0 = pl.BlockSpec((BLK, GROUP), lambda g, b, s: (s[TABLE + 2 * (b // 2)], 0))
    t1 = pl.BlockSpec((BLK, GROUP), lambda g, b, s: (s[TABLE + 2 * (b // 2) + 1], 0))
    return pl.pallas_call(
        attend_back_kernel,
        grid_spec=pltpu.PrefetchScalarGridSpec(
            num_scalar_prefetch=1,
            grid=(groups, 3),
            in_specs=[qs, ks, ks, qs, qs, qs, es, tq, tq, t0, t0, t1, t1],
            out_specs=[qs, ks, ks],
            scratch_shapes=[
                pltpu.VMEM((2, BLK, BLK), f32),
                pltpu.VMEM((LONG, GROUP), f32),
                pltpu.VMEM((LONG, GROUP), f32),
            ],
        ),
        out_shape=[
            jax.ShapeDtypeStruct((own, d), bf16),
            jax.ShapeDtypeStruct((rows, d), bf16),
            jax.ShapeDtypeStruct((rows, d), bf16),
        ],
        compiler_params=pltpu.CompilerParams(vmem_limit_bytes=VMEM_LIMIT),
        cost_estimate=pl.CostEstimate(
            flops=60_000_000_000, bytes_accessed=100_000_000, transcendentals=0
        ),
        name="attend_back",
    )(sc, q, k, v, do, o, inverse, expo, cos, sin, cos, sin, cos, sin)


def gelu_parts(z):
    density = jnp.exp2(z * z * (-0.5 * log2_e)) * 0.3989422804014327
    t = 1.0 / (1.0 + 0.2316419 * jnp.abs(z))
    poly = t * (
        0.319381530
        + t * (-0.356563782 + t * (1.781477937 + t * (-1.821255978 + t * 1.330274429)))
    )
    tail = density * poly
    cdf = jnp.where(z >= 0, 1.0 - tail, tail)
    return z * cdf, cdf + z * density


def middle_kernel(
    sc, x0, x1, x2, y0, y1, y2, o_ref, w_out, b_out, gain, shift, up_own, up_other, b_up, down_own, down_other, b_down,
    out_ref, mid_ref, do_ref, g_up, g_down, g_out, g_bup, g_small,
    r1, h2, h2t, dyt, acc, back,
):
    i = pl.program_id(0)
    last = pl.num_programs(0) - 1
    xs, ys = (x0, x1, x2), (y0, y1, y2)
    blocks = [slice(j * BLK, (j + 1) * BLK) for j in range(3)]

    @pl.when(i == 0)
    def _():
        for j, rows in enumerate(blocks):
            mixed = dot(o_ref[rows, :], w_out[...]) + b_out[...] + xs[j][...].astype(f32)
            r1[rows, :] = mixed
            normed, _ = normalize(mixed)
            hidden = (normed * gain[...] + shift[...]).astype(bf16)
            h2[rows, :] = hidden
            h2t[:, rows] = hidden.T
            dyt[:, rows] = ys[j][...].T
            acc[rows, :] = jnp.zeros_like(mixed)
            back[rows, :] = jnp.zeros_like(mixed)

    first = i <= last // 2
    w_up = jnp.where(first, up_own[...], up_other[...])
    w_down = jnp.where(first, down_own[...], down_other[...])
    actives, grads = [], []
    col_sum = None
    for j, rows in enumerate(blocks):
        pre = dot(h2[rows, :], w_up) + b_up[...]
        active, slope = gelu_parts(pre)
        active = active.astype(bf16)
        actives.append(active)
        acc[rows, :] += dot(active, w_down)
        grad = (dot(ys[j][...], w_down, NT) * slope).astype(bf16)
        grads.append(grad)
        back[rows, :] += dot(grad, w_up, NT)
        s = jnp.sum(grad.astype(f32), 0, keepdims=True)
        col_sum = s if col_sum is None else col_sum + s
    g_bup[...] = col_sum
    g_up[...] = dot(h2t[...], jnp.concatenate(grads, 0)).astype(g_up.dtype)
    g_down[...] = dot(dyt[...], jnp.concatenate(actives, 0)).astype(g_down.dtype)

    @pl.when(i == last)
    def _():
        sums = [None] * 4
        lows = []
        for j, rows in enumerate(blocks):
            mixed = r1[rows, :]
            place = pl.multiple_of(sc[PLACE + j] * BLK, BLK)
            out_ref[pl.ds(place, BLK), :] = (acc[rows, :] + b_down[...] + mixed).astype(bf16)
            normed, inverse = normalize(mixed)
            top = ys[j][...].astype(f32)
            dh = back[rows, :]
            dr = top + normalize_back(normed, inverse, dh * gain[...])
            mid_ref[rows, :] = dr
            low = dr.astype(bf16)
            lows.append(low)
            do_ref[rows, :] = dot(low, w_out[...], NT).astype(bf16)
            for n, term in enumerate((dh * normed, dh, dr, top)):
                s = jnp.sum(term, 0, keepdims=True)
                sums[n] = s if sums[n] is None else sums[n] + s
        g_out[...] = dot(jnp.concatenate(lows, 0).T, o_ref[...]).astype(g_out.dtype)
        g_small[...] = jnp.concatenate(sums + [jnp.zeros_like(sums[0])] * 4, 0)


def middle(sc, tokens, cotangent, o, w_out, b_out, gain, shift, up_own, up_other, b_up, down_own, down_other, b_down):
    d = tokens.shape[1]
    own = 3 * BLK
    half = up_own.shape[1]
    chunk = 256
    per = half // chunk
    one = pl.Buffered(buffer_count=1)
    whole = lambda *shape: pl.BlockSpec(shape, lambda i, s: (0,) * len(shape), pipeline_mode=one)
    rows_of = lambda j: pl.BlockSpec((BLK, d), lambda i, s: (s[BLOCK + j], 0), pipeline_mode=one)
    fixed = lambda *shape: pl.BlockSpec(shape, lambda i, s: (0,) * len(shape))
    low = lambda i: jnp.minimum(i, per - 1)
    high = lambda i: jnp.maximum(i - per, 0)
    return pl.pallas_call(
        middle_kernel,
        grid_spec=pltpu.PrefetchScalarGridSpec(
            num_scalar_prefetch=1,
            grid=(2 * per,),
            in_specs=[rows_of(0), rows_of(1), rows_of(2)] * 2
            + [
                whole(own, d),
                whole(d, d),
                whole(1, d),
                whole(1, d),
                whole(1, d),
                pl.BlockSpec((d, chunk), lambda i, s: (0, low(i))),
                pl.BlockSpec((d, chunk), lambda i, s: (0, high(i))),
                pl.BlockSpec((1, chunk), lambda i, s: (0, i)),
                pl.BlockSpec((chunk, d), lambda i, s: (low(i), 0)),
                pl.BlockSpec((chunk, d), lambda i, s: (high(i), 0)),
                whole(1, d),
            ],
            out_specs=[
                fixed(own, d),
                fixed(own, d),
                fixed(own, d),
                pl.BlockSpec((d, chunk), lambda i, s: (0, i)),
                pl.BlockSpec((d, chunk), lambda i, s: (0, i)),
                fixed(d, d),
                pl.BlockSpec((1, chunk), lambda i, s: (0, i)),
                fixed(8, d),
            ],
            scratch_shapes=[
                pltpu.VMEM((own, d), f32),
                pltpu.VMEM((own, d), bf16),
                pltpu.VMEM((d, own), bf16),
                pltpu.VMEM((d, own), bf16),
                pltpu.VMEM((own, d), f32),
                pltpu.VMEM((own, d), f32),
            ],
        ),
        out_shape=[
            jax.ShapeDtypeStruct((own, d), bf16),
            jax.ShapeDtypeStruct((own, d), f32),
            jax.ShapeDtypeStruct((own, d), bf16),
            jax.ShapeDtypeStruct((d, 2 * half), bf16),
            jax.ShapeDtypeStruct((d, 2 * half), bf16),
            jax.ShapeDtypeStruct((d, d), bf16),
            jax.ShapeDtypeStruct((1, 2 * half), f32),
            jax.ShapeDtypeStruct((8, d), f32),
        ],
        compiler_params=pltpu.CompilerParams(vmem_limit_bytes=VMEM_LIMIT),
        cost_estimate=pl.CostEstimate(
            flops=2 * own * d * (3 * d + 12 * half), bytes_accessed=40_000_000, transcendentals=8_000_000
        ),
        name="middle",
    )(sc, tokens, tokens, tokens, cotangent, cotangent, cotangent, o, w_out, b_out, gain, shift,
      up_own, up_other, b_up, down_own, down_other, b_down)


def project_back_kernel(sc, x_ref, gain, shift, w_ref, dq_ref, dk_ref, dv_ref, dh_ref, g_ref, gb_ref, total, bias):
    i = pl.program_id(0)
    last = pl.num_programs(0) - 1
    d = x_ref.shape[1]
    normed, _ = normalize(x_ref[...].astype(f32))
    hidden_t = (normed * gain[...] + shift[...]).astype(bf16).T

    @pl.when(i == 0)
    def _():
        total[...] = jnp.zeros_like(total)
        bias[...] = jnp.zeros_like(bias)

    def add(s, part):
        cols = slice(s * d, (s + 1) * d)
        total[:, cols] += dot(hidden_t, part)
        bias[:, cols] += jnp.sum(part.astype(f32), 0, keepdims=True)
        return dot(part, w_ref[s], NT)

    dh_ref[...] = add(1, dk_ref[...]) + add(2, dv_ref[...])

    @pl.when(i < last)
    def _():
        dh_ref[...] += add(0, dq_ref[...])

    @pl.when(i == last)
    def _():
        g_ref[...] = total[...].astype(g_ref.dtype)
        gb_ref[...] = bias[...]


def project_back(sc, tokens, gain, shift, w, dq, dk, dv):
    d = tokens.shape[1]
    rows = 4 * BLK
    one = pl.Buffered(buffer_count=1)
    whole = lambda *shape: pl.BlockSpec(shape, lambda i, s: (0,) * len(shape), pipeline_mode=one)
    fixed = lambda *shape: pl.BlockSpec(shape, lambda i, s: (0,) * len(shape))
    block = pl.BlockSpec((BLK, d), lambda i, s: (i, 0))
    return pl.pallas_call(
        project_back_kernel,
        grid_spec=pltpu.PrefetchScalarGridSpec(
            num_scalar_prefetch=1,
            grid=(4,),
            in_specs=[
                pl.BlockSpec((BLK, d), lambda i, s: (s[BLOCK + i], 0)),
                whole(1, d),
                whole(1, d),
                whole(3, d, d),
                pl.BlockSpec((BLK, d), lambda i, s: (jnp.minimum(i, 2), 0)),
                block,
                block,
            ],
            out_specs=[block, fixed(d, 3 * d), fixed(1, 3 * d)],
            scratch_shapes=[pltpu.VMEM((d, 3 * d), f32), pltpu.VMEM((1, 3 * d), f32)],
        ),
        out_shape=[
            jax.ShapeDtypeStruct((rows, d), f32),
            jax.ShapeDtypeStruct((d, 3 * d), bf16),
            jax.ShapeDtypeStruct((1, 3 * d), f32),
        ],
        compiler_params=pltpu.CompilerParams(vmem_limit_bytes=VMEM_LIMIT),
        cost_estimate=pl.CostEstimate(
            flops=4 * rows * d * 3 * d, bytes_accessed=20_000_000, transcendentals=0
        ),
        name="project_back",
    )(sc, tokens, gain, shift, w, dq, dk, dv)


def finish_kernel(sc, x_ref, gain, dh_ref, arrived, mid_ref, out_ref, small):
    i = pl.program_id(0)
    last = pl.num_programs(0) - 1

    @pl.when(i == 0)
    def _():
        small[...] = jnp.zeros_like(small)

    normed, inverse = normalize(x_ref[...].astype(f32))
    dh = dh_ref[...] + jnp.where(i == last, arrived[...].astype(f32), 0.0)
    out_ref[...] = (mid_ref[...] + normalize_back(normed, inverse, dh * gain[...])).astype(bf16)
    small[0:1, :] += jnp.sum(dh * normed, 0, keepdims=True)
    small[1:2, :] += jnp.sum(dh, 0, keepdims=True)


def finish(sc, tokens, gain, dh, arrived, mid):
    d = tokens.shape[1]
    own = 3 * BLK
    block = pl.BlockSpec((BLK, d), lambda i, s: (i, 0))
    return pl.pallas_call(
        finish_kernel,
        grid_spec=pltpu.PrefetchScalarGridSpec(
            num_scalar_prefetch=1,
            grid=(3,),
            in_specs=[
                pl.BlockSpec((BLK, d), lambda i, s: (s[BLOCK + i], 0)),
                pl.BlockSpec((1, d), lambda i, s: (0, 0)),
                block,
                pl.BlockSpec((BLK, d), lambda i, s: (0, 0)),
                block,
            ],
            out_specs=[
                pl.BlockSpec((BLK, d), lambda i, s: (s[PLACE + i], 0)),
                pl.BlockSpec((8, d), lambda i, s: (0, 0)),
            ],
        ),
        out_shape=[jax.ShapeDtypeStruct((own, d), bf16), jax.ShapeDtypeStruct((8, d), f32)],
        compiler_params=pltpu.CompilerParams(vmem_limit_bytes=VMEM_LIMIT),
        cost_estimate=pl.CostEstimate(flops=20_000_000, bytes_accessed=14_000_000, transcendentals=0),
        name="finish",
    )(sc, tokens, gain, dh, arrived, mid)


def on_device(
    tokens, lengths, gain_one, shift_one, w_qkv, b_qkv, w_out, b_out, gain_two, shift_two, w_up, b_up, w_down, b_down,
    cotangent,
):
    d = tokens.shape[1]
    n_dp = lax.axis_size("dp")
    here = lax.axis_index("dp")
    mp = lax.axis_index("mp")
    swap = [(0, 1), (1, 0)]
    half = w_qkv.shape[2]
    hidden = w_up.shape[1]

    long = (lengths[0, 0::2] == LONG).astype(jnp.int32)
    side = jnp.where(mp == 0, long[0], long[2])
    mid = long[1]
    zero = jnp.zeros((), jnp.int32)
    pick = lambda a, b: jnp.where(mp == 0, jnp.array(a, jnp.int32), jnp.array(b, jnp.int32))
    sc = jnp.concatenate(
        [
            jnp.stack([side, side, mid]),
            pick([0, 1, 2, 3], [4, 5, 3, 2]),
            jnp.stack([zero, side, jnp.where(mp == 0, 0, mid), jnp.where(mp == 0, mid, 0)]),
            pick([0, 1, 2], [1, 2, 0]),
        ]
    ).astype(jnp.int32)

    def other(own):
        share = own.shape[0] // n_dp
        piece = lax.dynamic_slice_in_dim(own, here * share, share, 0)
        return lax.all_gather(lax.ppermute(piece, "mp", swap), "dp", tiled=True)

    w_qkv_rows = jnp.transpose(w_qkv, (1, 0, 2)).reshape(d, 3 * half)
    qkv_other = jnp.transpose(other(w_qkv_rows).reshape(d, 3, half), (1, 0, 2))
    w_qkv_all = jnp.concatenate([w_qkv, qkv_other], 2)
    w_out_other = other(w_out.T).T
    w_out_all = jnp.concatenate([w_out, w_out_other], 0)
    up_other = other(w_up)
    down_other = other(w_down)
    b_qkv_all = jnp.concatenate([b_qkv, lax.ppermute(b_qkv, "mp", swap)], 1).astype(f32)
    b_up_all = jnp.concatenate([b_up, lax.ppermute(b_up, "mp", swap)], 0).astype(f32)[None]

    row = lambda v: v.astype(f32)[None]
    cos, sin = (jnp.asarray(t) for t in rope_tables())
    q, k, v = project(sc, tokens, row(gain_one), row(shift_one), w_qkv_all, b_qkv_all, cos, sin)
    o, inverse, expo = attend(sc, q, k, v)
    out_own, grad_mid, do, g_up, g_down, g_out, g_bup, small_two = middle(
        sc, tokens, cotangent, o, w_out_all, row(b_out), row(gain_two), row(shift_two),
        w_up, up_other, b_up_all, w_down, down_other, row(b_down),
    )
    out_tokens = lax.all_gather(out_own, "mp", tiled=True)
    early = lax.psum_scatter(
        jnp.concatenate([g_up, g_down, g_out], 1), "dp", scatter_dimension=0, tiled=True
    )
    dq, dk, dv = attend_back(sc, q, k, v, do, o, inverse, expo, cos, sin)
    dh, g_qkv, g_bqkv = project_back(sc, tokens, row(gain_one), row(shift_one), w_qkv_all, dq, dk, dv)
    arrived = lax.ppermute(dh[3 * BLK :].astype(bf16), "mp", swap)
    grad_own, small_one = finish(sc, tokens, row(gain_one), dh, arrived, grad_mid)
    grad_tokens = lax.all_gather(grad_own, "mp", tiled=True)
    late = lax.psum_scatter(g_qkv, "dp", scatter_dimension=0, tiled=True)

    parts = []
    for block, width in ((early[:, : 2 * hidden], hidden), (early[:, 2 * hidden : 4 * hidden], hidden), (early[:, 4 * hidden :], half)):
        parts.append((block[:, :width], block[:, width:]))
    for s in range(3):
        block = late[:, s * d : (s + 1) * d]
        parts.append((block[:, :half], block[:, half:]))
    mine = jnp.concatenate([a for a, _ in parts], 1)
    theirs = lax.ppermute(jnp.concatenate([b for _, b in parts], 1), "mp", swap)
    total = mine.astype(f32) + theirs.astype(f32)
    grad_w_up = total[:, :hidden]
    grad_w_down = total[:, hidden : 2 * hidden].T
    grad_w_out = total[:, 2 * hidden : 2 * hidden + half].T
    base = 2 * hidden + half
    grad_w_qkv = jnp.stack([total[:, base + s * half : base + (s + 1) * half] for s in range(3)], 0)

    def in_order(v, width):
        v = v.reshape(-1, 2, width)
        return jnp.where(mp == 0, v, v[:, ::-1]).reshape(-1)

    flat = jnp.concatenate(
        [small_one[0], small_one[1], small_two[:4].reshape(-1), in_order(g_bqkv, half), in_order(g_bup, hidden)]
    )
    flat = lax.psum(flat, ("dp", "mp"))
    small = flat[: 6 * d].reshape(6, d)
    g_b = flat[6 * d : 9 * d].reshape(3, 2, half)
    g_u = flat[9 * d :].reshape(2, hidden)
    grad_b_qkv = lax.dynamic_index_in_dim(g_b, mp, 1, keepdims=False)
    grad_b_up = lax.dynamic_index_in_dim(g_u, mp, 0, keepdims=False)
    return (
        out_tokens,
        grad_tokens,
        small[0],
        small[1],
        grad_w_qkv,
        grad_b_qkv,
        grad_w_out,
        small[4],
        small[2],
        small[3],
        grad_w_up,
        grad_b_up,
        grad_w_down,
        small[5],
    )


def solution(mesh):
    in_specs = (
        P("dp", None),
        P("dp", None),
        P(),
        P(),
        P(None, None, "mp"),
        P(None, "mp"),
        P("mp", None),
        P(),
        P(),
        P(),
        P(None, "mp"),
        P("mp"),
        P("mp", None),
        P(),
        P("dp", None),
    )
    out_specs = (
        P("dp", None),
        P("dp", None),
        P(),
        P(),
        P(None, "dp", "mp"),
        P(None, "mp"),
        P("mp", "dp"),
        P(),
        P(),
        P(),
        P("dp", "mp"),
        P("mp"),
        P("mp", "dp"),
        P(),
    )
    return jax.shard_map(on_device, mesh=mesh, in_specs=in_specs, out_specs=out_specs, check_vma=False)
```

```python
import functools

import jax
import jax.numpy as jnp
import numpy as np
from jax import lax
from jax.experimental import pallas as pl
from jax.experimental.pallas import tpu as pltpu
from jax.sharding import PartitionSpec as P

HD = 32
LONG = 1024
BLK = 512
GROUP = 128
epsilon = 1e-05
rotary_base = 10000.0
log2_e = 1.4426950408889634
ln_2 = 0.6931471805599453

f32 = jnp.float32
bf16 = jnp.bfloat16
NT = (((1,), (1,)), ((), ()))
NN = (((1,), (0,)), ((), ()))
TN = (((0,), (0,)), ((), ()))
VMEM_LIMIT = 60 << 20


def dot(a, b, dims=NN):
    return lax.dot_general(a, b, dims, preferred_element_type=f32)


def rope_tables():
    place = np.arange(LONG, dtype=np.float64)[:, None]
    frequency = rotary_base ** (-np.arange(HD // 2, dtype=np.float64) * 2.0 / HD)
    angles = place * frequency[None, :]
    cosines = np.concatenate([np.cos(angles), np.cos(angles)], 1)
    sines = np.concatenate([-np.sin(angles), np.sin(angles)], 1)
    repeat = GROUP // HD
    return (
        np.tile(cosines, (1, repeat)).astype(np.float32),
        np.tile(sines, (1, repeat)).astype(np.float32),
    )


def swap_halves(x):
    lane = lax.broadcasted_iota(jnp.int32, (1, GROUP), 1)
    low = (lane // (HD // 2)) % 2 == 0
    return jnp.where(low, pltpu.roll(x, GROUP - HD // 2, 1), pltpu.roll(x, HD // 2, 1))


def rotate(x, cosines, sines):
    return x * cosines + swap_halves(x) * sines


def rotate_back(x, cosines, sines):
    return x * cosines - swap_halves(x) * sines


def normalize(values):
    centred = values - jnp.mean(values, -1, keepdims=True)
    inverse = lax.rsqrt(jnp.mean(centred * centred, -1, keepdims=True) + epsilon)
    return (centred * inverse, inverse)


def normalize_back(normed, inverse, grad_normed):
    mean_grad = jnp.mean(grad_normed, -1, keepdims=True)
    mean_proj = jnp.mean(grad_normed * normed, -1, keepdims=True)
    return inverse * (grad_normed - mean_grad - normed * mean_proj)


FLAG, BLOCK, TABLE, PLACE = 0, 3, 7, 11


def slot(g, first):
    return g + jnp.where(g >= first, 1, 0)


def project_kernel(with_hidden, count, start, sc, x_ref, gain, shift, b_ref, cos, sin, *rest):
    w_refs, rest = rest[:count], rest[count:]
    if with_hidden:
        q_ref, k_ref, v_ref, h_ref, ht_ref = rest
        normed, _ = normalize(x_ref[...].astype(f32))
        hidden = (normed * gain[...] + shift[...]).astype(bf16)
        h_ref[...] = hidden
        ht_ref[...] = hidden.T
    else:
        q_ref, k_ref, v_ref = rest[-3:]
        hidden = x_ref[...]
    w = jnp.concatenate([w_refs[n][s] for s in range(3) for n in range(count)], 0)
    out = dot(hidden, w, NT)
    for s in range(3):
        for n in range(count):
            at = (s * count + n) * GROUP
            bias = b_ref[s : s + 1, (start + n) * GROUP : (start + n + 1) * GROUP]
            part = out[:, at : at + GROUP] + bias
            if s == 0:
                q_ref[n] = (rotate(part, cos[...], sin[...]) * (HD ** (-0.5) * log2_e)).astype(bf16)
            elif s == 1:
                k_ref[n] = rotate(part, cos[...], sin[...]).astype(bf16)
            else:
                v_ref[n] = part.astype(bf16)


def project(sc, x, gain, shift, w, b, cos, sin, start, count, groups, before=(), after=()):
    d = x.shape[1]
    rows = 4 * BLK
    with_hidden = not before
    table = pl.BlockSpec((BLK, GROUP), lambda i, s: (s[TABLE + i], 0))
    source = (lambda i, s: (s[BLOCK + i], 0)) if with_hidden else (lambda i, s: (i, 0))
    if with_hidden:
        held = groups - count
        out = pl.BlockSpec((held, BLK, GROUP), lambda i, s: (0, i, 0))
    else:
        held = count
        out = pl.BlockSpec((held, BLK, GROUP), lambda i, s: (1, i, 0))
    out_specs = [out, out, out]
    out_shape = [jax.ShapeDtypeStruct((2 * held, rows, GROUP), bf16)] * 3
    if with_hidden:
        out_specs += [pl.BlockSpec((BLK, d), lambda i, s: (i, 0)), pl.BlockSpec((d, BLK), lambda i, s: (0, i))]
        out_shape += [jax.ShapeDtypeStruct((rows, d), bf16), jax.ShapeDtypeStruct((d, rows), bf16)]
    extra = (*before, *after)
    weight = lambda n: pl.BlockSpec((3, GROUP, d), lambda i, s: (0, start + n, 0))
    return pl.pallas_call(
        functools.partial(project_kernel, with_hidden, count, start),
        grid_spec=pltpu.PrefetchScalarGridSpec(
            num_scalar_prefetch=1,
            grid=(4,),
            in_specs=[
                pl.BlockSpec((BLK, d), source),
                pl.BlockSpec((1, d), lambda i, s: (0, 0)),
                pl.BlockSpec((1, d), lambda i, s: (0, 0)),
                pl.BlockSpec(b.shape, lambda i, s: (0, 0)),
                table,
                table,
            ]
            + [weight(n) for n in range(count)]
            + [pl.BlockSpec(memory_space=pl.ANY)] * len(extra),
            out_specs=out_specs,
        ),
        out_shape=out_shape,
        input_output_aliases={7 + count + n: n for n in range(len(before))},
        compiler_params=pltpu.CompilerParams(vmem_limit_bytes=VMEM_LIMIT),
        cost_estimate=pl.CostEstimate(
            flops=2 * rows * d * 3 * GROUP * count, bytes_accessed=6_000_000, transcendentals=0
        ),
        name="project",
    )(sc, x, gain, shift, b, cos, sin, *[w] * count, *extra)


def attend_body(q, k_ref, v_ref, o_ref, l_ref, e_ref, store, start, count):
    lane = lax.broadcasted_iota(jnp.int32, (1, GROUP), 1) // HD
    heads = GROUP // HD
    chunks = count // BLK
    values_t = v_ref[pl.ds(start, count), :].T
    ones = jnp.ones((16, count), bf16)
    outs, inverses = [], []

    def score(h, c):
        keys = k_ref[pl.ds(start + c * BLK, BLK), :]
        scores = dot(jnp.where(lane == h, keys, jnp.zeros_like(keys)), q, NT)
        store[h % 2, c * BLK : (c + 1) * BLK, :] = scores
        return jnp.max(scores.reshape(BLK // 8, 8, BLK), axis=0)

    def score_max(h, c, so_far):
        found = score(h, c)
        return found if so_far is None else jnp.maximum(so_far, found)

    top = None
    for c in range(chunks):
        top = score_max(0, c, top)
    row_max = jnp.max(top, axis=0, keepdims=True)
    for h in range(heads):
        top = None
        total = None
        stacked = jnp.concatenate([values_t[HD * h : HD * (h + 1)], ones], 0)
        for c in range(chunks):
            if h + 1 < heads:
                top = score_max(h + 1, c, top)
            rows = slice(c * BLK, (c + 1) * BLK)
            expo = jnp.exp2(store[h % 2, rows, :] - row_max).astype(bf16)
            e_ref[h, pl.ds(start + c * BLK, BLK), :] = expo
            part = dot(stacked[:, rows], expo)
            total = part if total is None else total + part
        inverse = 1.0 / total[HD : HD + 1]
        outs.append(total[:HD] * inverse)
        inverses.append(jnp.broadcast_to(inverse, (HD, BLK)))
        if h + 1 < heads:
            row_max = jnp.max(top, axis=0, keepdims=True)
    o_ref[...] = jnp.concatenate(outs, 0).T.astype(bf16)
    l_ref[...] = jnp.concatenate(inverses, 0).T


def attend_kernel(sc, q_ref, k_ref, v_ref, *rest):
    o_ref, l_ref, e_ref, store = rest[-4:]
    b = pl.program_id(1)
    refs = (k_ref, v_ref, o_ref, l_ref, e_ref, store)

    @pl.when(sc[FLAG + b] == 1)
    def _():
        attend_body(q_ref[...], *refs, 0, LONG)

    @pl.when(sc[FLAG + b] == 0)
    def _():
        start = pl.multiple_of(jnp.where(b == 1, BLK, 0), BLK)
        attend_body(q_ref[...], *refs, start, BLK)


def attend(sc, q, k, v, start, count, before=()):
    groups = q.shape[0] - 1
    heads = GROUP // HD
    own = 3 * BLK
    place = start + (1 if before else 0)
    qs = pl.BlockSpec((None, BLK, GROUP), lambda g, b, s: (g + place, b, 0))
    ks = pl.BlockSpec((None, LONG, GROUP), lambda g, b, s: (g + place, b // 2, 0))
    os = pl.BlockSpec((None, BLK, GROUP), lambda g, b, s: (g + start, b, 0))
    es = pl.BlockSpec((heads, LONG, BLK), lambda g, b, s: ((g + start) * 3 + b, 0, 0))
    return pl.pallas_call(
        attend_kernel,
        grid_spec=pltpu.PrefetchScalarGridSpec(
            num_scalar_prefetch=1,
            grid=(count, 3),
            in_specs=[qs, ks, ks] + [pl.BlockSpec(memory_space=pl.ANY)] * len(before),
            out_specs=[os, os, es],
            scratch_shapes=[pltpu.VMEM((2, LONG, BLK), f32)],
        ),
        out_shape=[
            jax.ShapeDtypeStruct((groups, own, GROUP), bf16),
            jax.ShapeDtypeStruct((groups, own, GROUP), f32),
            jax.ShapeDtypeStruct((groups * 3 * heads, LONG, BLK), bf16),
        ],
        input_output_aliases={4 + n: n for n in range(len(before))},
        compiler_params=pltpu.CompilerParams(vmem_limit_bytes=VMEM_LIMIT),
        cost_estimate=pl.CostEstimate(
            flops=count * 5_000_000_000, bytes_accessed=count * 16_000_000, transcendentals=count * 6_000_000
        ),
        name="attend",
    )(sc, q, k, v, *before)


def attend_back_body(
    q_ref, k_ref, v_ref, do_ref, o_ref, l_ref, e_ref, cos, sin, dq_ref, prod, dk_sum, dv_sum, start, count
):
    lane = lax.broadcasted_iota(jnp.int32, (1, GROUP), 1) // HD
    heads = GROUP // HD
    q = q_ref[...]
    do = (do_ref[...].astype(f32) * l_ref[...]).astype(bf16)
    both = do.astype(f32) * o_ref[...].astype(f32)
    upper = both.astype(bf16)
    lower = (both - upper.astype(f32)).astype(bf16)
    pick = (
        lax.broadcasted_iota(jnp.int32, (8, GROUP), 0)
        == lax.broadcasted_iota(jnp.int32, (8, GROUP), 1) // HD
    )
    pick = pick.astype(f32).astype(bf16)
    delta = dot(pick, upper, NT) + dot(pick, lower, NT)
    keys_t = k_ref[pl.ds(start, count), :].T
    chunks = count // BLK
    tiles = [(h, c) for h in range(heads) for c in range(chunks)]

    def grad_probs(i):
        h, c = tiles[i]
        values = v_ref[pl.ds(start + c * BLK, BLK), :]
        prod[i % 2] = dot(jnp.where(lane == h, values, jnp.zeros_like(values)), do, NT)

    grad_probs(0)
    dq_t = [None] * heads
    for i, (h, c) in enumerate(tiles):
        if i + 1 < len(tiles):
            grad_probs(i + 1)
        rows = pl.ds(start + c * BLK, BLK)
        expo = e_ref[h, rows, :]
        ds = (expo.astype(f32) * (prod[i % 2] - delta[h : h + 1])).astype(bf16)
        dv_sum[rows, :] += dot(expo, jnp.where(lane == h, do, jnp.zeros_like(do)))
        dk_sum[rows, :] += dot(ds, jnp.where(lane == h, q, jnp.zeros_like(q)))
        part = dot(keys_t[HD * h : HD * (h + 1), c * BLK : (c + 1) * BLK], ds)
        dq_t[h] = part if dq_t[h] is None else dq_t[h] + part
    dq = jnp.concatenate(dq_t, 0).T * (HD ** (-0.5))
    dq_ref[...] = rotate_back(dq, cos[...], sin[...]).astype(bf16)


def window_back(
    sc, last_block, refs, tables, w_ref, ht_ref, dq_cat, dq_ref, dk_sum, dv_sum, dh_sum, start_block
):
    parts = [dq_cat[...]]
    dk = dk_sum[...] * ln_2
    cos0, sin0, cos1, sin1 = tables
    low, high = slice(0, BLK), slice(BLK, LONG)
    parts.append(
        jnp.concatenate(
            [rotate_back(dk[low], cos0[...], sin0[...]), rotate_back(dk[high], cos1[...], sin1[...])], 0
        ).astype(bf16)
    )
    parts.append(dv_sum[...].astype(bf16))
    both = jnp.concatenate(parts, 1)
    w = jnp.concatenate([w_ref[0], w_ref[1], w_ref[2]], 0)
    for rows in (low, high):
        dh_sum[rows, :] += dot(both[rows], w)
    return dot(ht_ref[...], both), jnp.sum(both.astype(f32), 0, keepdims=True)


def back_kernel(
    start_block, blocks, share,
    sc, q_ref, k_ref, v_ref, do_ref, o_ref, l_ref, e_ref, cos, sin, cos0, sin0, cos1, sin1, w_ref, ht_ref,
    *rest,
):
    g = pl.program_id(0)
    last_g = pl.num_programs(0) - 1
    step = pl.program_id(1)
    b = step + start_block
    if blocks == 2:
        x_ref, gain, mid_ref, g_ref, gb_ref, out_ref, small, dq_cat, prod, dk_sum, dv_sum, dh_sum = rest
    else:
        before, before_b, g_ref, gb_ref, own_ref, partner_ref, dq_cat, prod, dk_sum, dv_sum, dh_sum = rest
    dq_ref = dq_cat.at[pl.ds(pl.multiple_of(step * BLK, BLK), BLK), :]
    refs = (q_ref, k_ref, v_ref, do_ref, o_ref, l_ref, e_ref, cos, sin, dq_ref, prod, dk_sum, dv_sum)

    @pl.when(step == 0)
    def _():
        dk_sum[...] = jnp.zeros_like(dk_sum)
        dv_sum[...] = jnp.zeros_like(dv_sum)

    @pl.when((step == 0) & (g == 0))
    def _():
        dh_sum[...] = jnp.zeros_like(dh_sum)
        if blocks == 1:
            dq_cat[BLK:, :] = jnp.zeros((BLK, GROUP), bf16)

    @pl.when(sc[FLAG + b] == 1)
    def _():
        attend_back_body(*refs, 0, LONG)

    @pl.when(sc[FLAG + b] == 0)
    def _():
        start = pl.multiple_of(jnp.where(b == 1, BLK, 0), BLK)
        attend_back_body(*refs, start, BLK)

    @pl.when(step == blocks - 1)
    def _():
        weight, bias = window_back(
            sc, None, refs, (cos0, sin0, cos1, sin1), w_ref, ht_ref, dq_cat, dq_ref, dk_sum, dv_sum, dh_sum, b
        )
        if blocks == 2:
            g_ref[...] = weight
            gb_ref[...] = bias
        else:
            weight = weight + before[...]
            gb_ref[...] = bias + before_b[...]
            if share is None:
                g_ref[...] = weight.astype(bf16)
            else:
                fill = jnp.zeros((g_ref.shape[1] - 3 * share, GROUP), f32)
                for n in range(g_ref.shape[0]):
                    rows = weight[n * share : (n + 1) * share]
                    pieces = [rows[:, s * GROUP : (s + 1) * GROUP] for s in range(3)]
                    g_ref[n] = jnp.concatenate(pieces + [fill], 0).astype(bf16)

    @pl.when((step == blocks - 1) & (g == last_g))
    def _():
        if blocks == 1:
            own_ref[...] = dh_sum[:BLK, :]
            partner_ref[...] = dh_sum[BLK:, :].astype(bf16)
        else:
            sums = [None, None]
            for rows in (slice(0, BLK), slice(BLK, LONG)):
                normed, inverse = normalize(x_ref[rows, :].astype(f32))
                dh = dh_sum[rows, :]
                out_ref[rows, :] = (mid_ref[rows, :] + normalize_back(normed, inverse, dh * gain[...])).astype(bf16)
                for n, term in enumerate((dh * normed, dh)):
                    s = jnp.sum(term, 0, keepdims=True)
                    sums[n] = s if sums[n] is None else sums[n] + s
            small[...] = jnp.concatenate(sums + [jnp.zeros_like(sums[0])] * 6, 0)


def back(sc, q, k, v, do, o, inverse, expo, cos, sin, w, hidden_t, first, start_block, blocks, share, more):
    groups = o.shape[0]
    d = w.shape[2]
    heads = GROUP // HD
    n = start_block
    one = pl.Buffered(buffer_count=1)
    qs = pl.BlockSpec((None, BLK, GROUP), lambda g, b, s: (slot(g, first), b + n, 0))
    ks = pl.BlockSpec((None, LONG, GROUP), lambda g, b, s: (slot(g, first), n // 2, 0))
    os = pl.BlockSpec((None, BLK, GROUP), lambda g, b, s: (g, b + n, 0))
    es = pl.BlockSpec((heads, LONG, BLK), lambda g, b, s: (g * 3 + b + n, 0, 0))
    tq = pl.BlockSpec((BLK, GROUP), lambda g, b, s: (s[TABLE + b + n], 0))
    t0 = pl.BlockSpec((BLK, GROUP), lambda g, b, s: (s[TABLE + n], 0))
    t1 = pl.BlockSpec((BLK, GROUP), lambda g, b, s: (s[TABLE + n + 1], 0))
    weight = pl.BlockSpec((None, d, 3 * GROUP), lambda g, b, s: (g, 0, 0))
    bias = pl.BlockSpec((None, 1, 3 * GROUP), lambda g, b, s: (g, 0, 0))
    whole = lambda *shape: pl.BlockSpec(shape, lambda g, b, s: (0, 0))
    in_specs = [qs, ks, ks, os, os, os, es, tq, tq, t0, t0, t1, t1]
    in_specs += [
        pl.BlockSpec((3, GROUP, d), lambda g, b, s: (0, g, 0)),
        pl.BlockSpec((d, LONG), lambda g, b, s: (0, n // 2), pipeline_mode=one),
    ]
    bias_shape = jax.ShapeDtypeStruct((groups, 1, 3 * GROUP), f32)
    if blocks == 2:
        in_specs += [
            pl.BlockSpec((LONG, d), lambda g, b, s: (s[BLOCK] // 2, 0), pipeline_mode=one),
            whole(1, d),
            pl.BlockSpec((LONG, d), lambda g, b, s: (0, 0), pipeline_mode=one),
        ]
        out_specs = [weight, bias, whole(LONG, d), whole(8, d)]
        out_shape = [
            jax.ShapeDtypeStruct((groups, d, 3 * GROUP), f32),
            bias_shape,
            jax.ShapeDtypeStruct((LONG, d), bf16),
            jax.ShapeDtypeStruct((8, d), f32),
        ]
    else:
        in_specs += [weight, bias]
        if share is None:
            out_specs = [weight]
            out_shape = [jax.ShapeDtypeStruct((groups, d, 3 * GROUP), bf16)]
        else:
            held = -(-3 * share // 16) * 16
            out_specs = [pl.BlockSpec((d // share, None, held, GROUP), lambda g, b, s: (0, g, 0, 0))]
            out_shape = [jax.ShapeDtypeStruct((d // share, groups, held, GROUP), bf16)]
        out_specs += [bias, whole(BLK, d), whole(BLK, d)]
        out_shape += [bias_shape, jax.ShapeDtypeStruct((BLK, d), f32), jax.ShapeDtypeStruct((BLK, d), bf16)]
    return pl.pallas_call(
        functools.partial(back_kernel, start_block, blocks, share),
        grid_spec=pltpu.PrefetchScalarGridSpec(
            num_scalar_prefetch=1,
            grid=(groups, blocks),
            in_specs=in_specs,
            out_specs=out_specs,
            scratch_shapes=[
                pltpu.VMEM((LONG, GROUP), bf16),
                pltpu.VMEM((2, BLK, BLK), f32),
                pltpu.VMEM((LONG, GROUP), f32),
                pltpu.VMEM((LONG, GROUP), f32),
                pltpu.VMEM((LONG, d), f32),
            ],
        ),
        out_shape=out_shape,
        compiler_params=pltpu.CompilerParams(vmem_limit_bytes=VMEM_LIMIT),
        cost_estimate=pl.CostEstimate(
            flops=groups * blocks * 5_000_000_000, bytes_accessed=groups * blocks * 6_000_000, transcendentals=0
        ),
        name="back",
    )(sc, q, k, v, do, o, inverse, expo, cos, sin, cos, sin, cos, sin, w, hidden_t, *more)


def gelu_parts(z):
    density = jnp.exp2(z * z * (-0.5 * log2_e)) * 0.3989422804014327
    t = 1.0 / (1.0 + 0.2316419 * jnp.abs(z))
    poly = t * (
        0.319381530
        + t * (-0.356563782 + t * (1.781477937 + t * (-1.821255978 + t * 1.330274429)))
    )
    tail = density * poly
    cdf = jnp.where(z >= 0, 1.0 - tail, tail)
    return z * cdf, cdf + z * density


def middle_kernel(
    sc, x0, x1, x2, y0, y1, y2, o_ref, w_out, b_out, gain, shift, up_own, up_other, b_up, down_own, down_other, b_down,
    out_ref, mid_ref, do_ref, g_ref, g_bup, g_small,
    r1, h2, h2t, dyt, acc, back, g_out,
):
    i = pl.program_id(0)
    chunks = pl.num_programs(0) - 2
    xs, ys = (x0, x1, x2), (y0, y1, y2)
    blocks = [slice(j * BLK, (j + 1) * BLK) for j in range(3)]
    groups = o_ref.shape[0]
    heads_of = lambda rows: jnp.concatenate([o_ref[g, rows, :] for g in range(groups)], 1)

    @pl.when(i == 0)
    def _():
        for j, rows in enumerate(blocks):
            mixed = dot(heads_of(rows), w_out[...]) + b_out[...] + xs[j][...].astype(f32)
            r1[rows, :] = mixed
            normed, _ = normalize(mixed)
            hidden = (normed * gain[...] + shift[...]).astype(bf16)
            h2[rows, :] = hidden
            h2t[:, rows] = hidden.T
            dyt[:, rows] = ys[j][...].T
            acc[rows, :] = jnp.zeros_like(mixed)
            back[rows, :] = jnp.zeros_like(mixed)

    @pl.when(i < chunks)
    def _():
        first = i < chunks // 2
        w_up = jnp.where(first, up_own[...], up_other[...])
        w_down = jnp.where(first, down_own[...], down_other[...])
        width = w_up.shape[1]
        actives, grads = [], []
        col_sum = None
        for j, rows in enumerate(blocks):
            pre = dot(h2[rows, :], w_up) + b_up[...]
            active, slope = gelu_parts(pre)
            active = active.astype(bf16)
            actives.append(active)
            acc[rows, :] += dot(active, w_down)
            grad = (dot(ys[j][...], w_down, NT) * slope).astype(bf16)
            grads.append(grad)
            back[rows, :] += dot(grad, w_up, NT)
            s = jnp.sum(grad.astype(f32), 0, keepdims=True)
            col_sum = s if col_sum is None else col_sum + s
        g_bup[...] = col_sum
        g_ref[:, :width] = dot(h2t[...], jnp.concatenate(grads, 0)).astype(bf16)
        g_ref[:, width:] = dot(dyt[...], jnp.concatenate(actives, 0)).astype(bf16)

    @pl.when(i == chunks)
    def _():
        sums = [None] * 4
        lows = []
        for j, rows in enumerate(blocks):
            mixed = r1[rows, :]
            place = pl.multiple_of(sc[PLACE + j] * BLK, BLK)
            out_ref[pl.ds(place, BLK), :] = (acc[rows, :] + b_down[...] + mixed).astype(bf16)
            normed, inverse = normalize(mixed)
            top = ys[j][...].astype(f32)
            dh = back[rows, :]
            dr = top + normalize_back(normed, inverse, dh * gain[...])
            mid_ref[rows, :] = dr
            low = dr.astype(bf16)
            lows.append(low)
            do = dot(low, w_out[...], NT).astype(bf16)
            for g in range(groups):
                do_ref[g, rows, :] = do[:, g * GROUP : (g + 1) * GROUP]
            for n, term in enumerate((dh * normed, dh, dr, top)):
                s = jnp.sum(term, 0, keepdims=True)
                sums[n] = s if sums[n] is None else sums[n] + s
        weight = dot(jnp.concatenate(lows, 0).T, heads_of(slice(0, 3 * BLK))).astype(bf16)
        width = g_ref.shape[1]
        g_ref[...] = weight[:, :width]
        g_out[...] = weight[:, width:]
        g_small[...] = jnp.concatenate(sums + [jnp.zeros_like(sums[0])] * 4, 0)

    @pl.when(i == chunks + 1)
    def _():
        rest = g_out.shape[1]
        g_ref[:, :rest] = g_out[...]
        g_ref[:, rest:] = jnp.zeros((g_ref.shape[0], g_ref.shape[1] - rest), bf16)


def middle(sc, tokens, cotangent, o, w_out, b_out, gain, shift, up_own, up_other, b_up, down_own, down_other, b_down):
    d = tokens.shape[1]
    groups = o.shape[0]
    own = 3 * BLK
    half = up_own.shape[1]
    chunk = 256
    per = half // chunk
    steps = 2 * per + 2
    one = pl.Buffered(buffer_count=1)
    whole = lambda *shape: pl.BlockSpec(shape, lambda i, s: (0,) * len(shape), pipeline_mode=one)
    rows_of = lambda j: pl.BlockSpec((BLK, d), lambda i, s: (s[BLOCK + j], 0), pipeline_mode=one)
    fixed = lambda *shape: pl.BlockSpec(shape, lambda i, s: (0,) * len(shape))
    low = lambda i: jnp.minimum(i, per - 1)
    high = lambda i: jnp.clip(i - per, 0, per - 1)
    at = lambda i: jnp.minimum(i, 2 * per - 1)
    return pl.pallas_call(
        middle_kernel,
        grid_spec=pltpu.PrefetchScalarGridSpec(
            num_scalar_prefetch=1,
            grid=(steps,),
            in_specs=[rows_of(0), rows_of(1), rows_of(2)] * 2
            + [
                whole(groups, own, GROUP),
                whole(d, d),
                whole(1, d),
                whole(1, d),
                whole(1, d),
                pl.BlockSpec((d, chunk), lambda i, s: (0, low(i))),
                pl.BlockSpec((d, chunk), lambda i, s: (0, high(i))),
                pl.BlockSpec((1, chunk), lambda i, s: (0, at(i))),
                pl.BlockSpec((chunk, d), lambda i, s: (low(i), 0)),
                pl.BlockSpec((chunk, d), lambda i, s: (high(i), 0)),
                whole(1, d),
            ],
            out_specs=[
                fixed(own, d),
                fixed(own, d),
                fixed(groups, own, GROUP),
                pl.BlockSpec((d, 2 * chunk), lambda i, s: (0, i)),
                pl.BlockSpec((1, chunk), lambda i, s: (0, at(i))),
                fixed(8, d),
            ],
            scratch_shapes=[
                pltpu.VMEM((own, d), f32),
                pltpu.VMEM((own, d), bf16),
                pltpu.VMEM((d, own), bf16),
                pltpu.VMEM((d, own), bf16),
                pltpu.VMEM((own, d), f32),
                pltpu.VMEM((own, d), f32),
                pltpu.VMEM((d, d - 2 * chunk), bf16),
            ],
        ),
        out_shape=[
            jax.ShapeDtypeStruct((own, d), bf16),
            jax.ShapeDtypeStruct((own, d), f32),
            jax.ShapeDtypeStruct((groups, own, GROUP), bf16),
            jax.ShapeDtypeStruct((d, 2 * chunk * steps), bf16),
            jax.ShapeDtypeStruct((1, 2 * half), f32),
            jax.ShapeDtypeStruct((8, d), f32),
        ],
        compiler_params=pltpu.CompilerParams(vmem_limit_bytes=VMEM_LIMIT),
        cost_estimate=pl.CostEstimate(
            flops=2 * own * d * (3 * d + 12 * half), bytes_accessed=40_000_000, transcendentals=8_000_000
        ),
        name="middle",
    )(sc, tokens, tokens, tokens, cotangent, cotangent, cotangent, o, w_out, b_out, gain, shift,
      up_own, up_other, b_up, down_own, down_other, b_down)


def finish_rows(x, gain, mid, dh):
    normed, inverse = normalize(x.astype(f32))
    out = (mid + normalize_back(normed, inverse, dh * gain)).astype(bf16)
    return out, jnp.sum(dh * normed, 0, keepdims=True), jnp.sum(dh, 0, keepdims=True)


def lines(v):
    return jnp.concatenate([v[:, j * GROUP : (j + 1) * GROUP] for j in range(v.shape[1] // GROUP)], 0)


def reduce_kernel(
    cuts, g_ref, part_ref, own_ref, x_ref, gain, mid_ref, small_ref, early_ref,
    sum_ref, theirs_ref, small_sum, small_theirs, rows_ref, rows_theirs, early_theirs,
    part_in, r1, a1, r2, a2, r3, s0, s1, s2, q1, q2, q3, send, recv,
):
    here = lax.axis_index("dp")
    mp = lax.axis_index("mp")
    c = here % 2
    x = (here // 2) % 2
    z = here // 4
    core = (here + 1 - 2 * c, mp)
    side = (here + 2 - 4 * x, mp)
    across = (here, 1 - mp)
    line = [((z + n) % 4, ((z + n) % 4 * 4 + here % 4, mp)) for n in (1, 2, 3)]
    partners = [core, side, across] + [dev for _, dev in line]

    barrier = pltpu.get_barrier_semaphore()
    for dev in partners:
        pl.semaphore_signal(barrier, inc=1, device_id=dev, device_id_type=pl.DeviceIdType.MESH)
    pl.semaphore_wait(barrier, len(partners))

    used = iter(range(send.shape[0]))

    def copy(src, dst, dev):
        n = next(used)
        made = pltpu.make_async_remote_copy(
            src_ref=src,
            dst_ref=dst,
            send_sem=send.at[n],
            recv_sem=recv.at[n],
            device_id=dev,
            device_id_type=pl.DeviceIdType.MESH,
        )
        made.start()
        return made

    rows_in = copy(part_ref, part_in, across)
    pending = [copy(early_ref, early_theirs, across)]
    by_core = [copy(g_ref.at[:, :, 1 - c, lo:hi], r1.at[:, :, lo:hi], core) for lo, hi in cuts]

    by_side = []
    for n, (lo, hi) in enumerate(cuts):
        by_core[n].wait()
        a1[:, :, lo:hi] = (g_ref[:, :, c, lo:hi].astype(f32) + r1[:, :, lo:hi].astype(f32)).astype(bf16)
        by_side.append(copy(a1.at[:, 1 - x, lo:hi], r2.at[:, lo:hi], side))

    rows_in.wait()
    out, first, second = finish_rows(x_ref[...], gain[...], mid_ref[...], own_ref[...] + part_in[...].astype(f32))
    rows_ref[...] = out
    pending.append(copy(rows_ref, rows_theirs, across))
    s0[...] = small_ref[...]
    mine = jnp.concatenate([lines(first), lines(second)], 0)
    s0[: mine.shape[0], :] += mine
    small_copy = copy(s0, q1, core)

    by_line = []
    for n, (lo, hi) in enumerate(cuts):
        by_side[n].wait()
        a2[:, lo:hi] = (a1[:, x, lo:hi].astype(f32) + r2[:, lo:hi].astype(f32)).astype(bf16)
        by_line.append([copy(a2.at[at, lo:hi], r3.at[m, lo:hi], dev) for m, (at, dev) in enumerate(line)])
        if n == 0:
            small_copy.wait()
            s1[...] = s0[...] + q1[...]
            small_copy = copy(s1, q2, side)

    small_copy.wait()
    s2[...] = s1[...] + q2[...]
    small_line = [copy(s2, q3.at[z], dev) for _, dev in line]

    for n, (lo, hi) in enumerate(cuts):
        for made in by_line[n]:
            made.wait()
        total = a2[z, lo:hi].astype(f32)
        for m in range(3):
            total = total + r3[m, lo:hi].astype(f32)
        sum_ref[lo:hi] = total.astype(bf16)
        pending.append(copy(sum_ref.at[lo:hi], theirs_ref.at[lo:hi], across))

    for made in small_line:
        made.wait()
    q3[z] = s2[...]
    small_sum[...] = (q3[0] + q3[1]) + (q3[2] + q3[3])
    pending.append(copy(small_sum, small_theirs, across))
    for made in pending:
        made.wait()


def reduce_all(g, part, own, x, gain, mid, small, early):
    to, groups, held, _ = g.shape
    g = g.reshape(4, 2, 2, groups, held, GROUP)
    cuts = ((0, 3), (3, groups))
    copies = 3 + 6 * len(cuts) + 7
    block = (groups, held, GROUP)
    vmem = pl.BlockSpec(memory_space=pltpu.VMEM)
    return pl.pallas_call(
        functools.partial(reduce_kernel, cuts),
        in_specs=[vmem] * 8,
        out_specs=[vmem] * 7,
        out_shape=[
            jax.ShapeDtypeStruct(block, bf16),
            jax.ShapeDtypeStruct(block, bf16),
            jax.ShapeDtypeStruct(small.shape, f32),
            jax.ShapeDtypeStruct(small.shape, f32),
            jax.ShapeDtypeStruct(x.shape, bf16),
            jax.ShapeDtypeStruct(x.shape, bf16),
            jax.ShapeDtypeStruct(early.shape, bf16),
        ],
        scratch_shapes=[
            pltpu.VMEM(part.shape, bf16),
            pltpu.VMEM((4, 2, *block), bf16),
            pltpu.VMEM((4, 2, *block), bf16),
            pltpu.VMEM((4, *block), bf16),
            pltpu.VMEM((4, *block), bf16),
            pltpu.VMEM((3, *block), bf16),
            pltpu.VMEM(small.shape, f32),
            pltpu.VMEM(small.shape, f32),
            pltpu.VMEM(small.shape, f32),
            pltpu.VMEM(small.shape, f32),
            pltpu.VMEM(small.shape, f32),
            pltpu.VMEM((4, *small.shape), f32),
            pltpu.SemaphoreType.DMA((copies,)),
            pltpu.SemaphoreType.DMA((copies,)),
        ],
        compiler_params=pltpu.CompilerParams(
            vmem_limit_bytes=VMEM_LIMIT, collective_id=0, has_side_effects=True
        ),
        cost_estimate=pl.CostEstimate(flops=10_000_000, bytes_accessed=100_000_000, transcendentals=0),
        name="reduce_all",
    )(g, part, own, x, gain, mid, small, early)


def finish_kernel(x_ref, gain, mid_ref, own_ref, part_ref, out_ref, small):
    out, first, second = finish_rows(
        x_ref[...], gain[...], mid_ref[...], own_ref[...] + part_ref[...].astype(f32)
    )
    out_ref[...] = out
    small[...] = jnp.concatenate([lines(first), lines(second)], 0)


def finish(x, gain, mid, own, part):
    d = x.shape[1]
    return pl.pallas_call(
        finish_kernel,
        out_shape=[jax.ShapeDtypeStruct(x.shape, bf16), jax.ShapeDtypeStruct((2 * d // GROUP, GROUP), f32)],
        compiler_params=pltpu.CompilerParams(vmem_limit_bytes=VMEM_LIMIT),
        name="finish",
    )(x, gain, mid, own, part)


def place_pieces(sc, first, pieces, out_ref, sem):
    copies = []
    for n, piece in enumerate(pieces):
        start = pl.multiple_of(sc[first + n] * BLK, BLK)
        copies.append(pltpu.make_async_copy(piece, out_ref.at[pl.ds(start, piece.shape[0]), :], sem.at[n]))
        copies[-1].start()
    return copies


def assemble_kernel(count, sc, *rest):
    for made in place_pieces(sc, 0, rest[:count], rest[count], rest[-1]):
        made.wait()


def assemble(places, pieces, rows):
    count = len(pieces)
    return pl.pallas_call(
        functools.partial(assemble_kernel, count),
        grid_spec=pltpu.PrefetchScalarGridSpec(
            num_scalar_prefetch=1,
            grid=(1,),
            in_specs=[pl.BlockSpec(p.shape, lambda i, s: (0, 0)) for p in pieces],
            out_specs=pl.BlockSpec(memory_space=pl.ANY),
            scratch_shapes=[pltpu.SemaphoreType.DMA((count,))],
        ),
        out_shape=jax.ShapeDtypeStruct((rows, pieces[0].shape[1]), pieces[0].dtype),
        compiler_params=pltpu.CompilerParams(vmem_limit_bytes=VMEM_LIMIT),
        cost_estimate=pl.CostEstimate(flops=0, bytes_accessed=8_000_000, transcendentals=0),
        name="assemble",
    )(places, *pieces)


def one_line(v):
    return jnp.concatenate([v[j : j + 1] for j in range(v.shape[0])], 1)


def conclude_kernel(
    share, half, hidden, sc, late, late_theirs, early, early_theirs, small, small_theirs, p0, p1, p2, p3,
    g_qkv, g_up, g_down, g_out, g_bqkv, g_bup, grad, *rest,
):
    vectors, sem = rest[:-1], rest[-1]
    copies = place_pieces(sc, 0, (p0, p1, p2, p3), grad, sem)
    groups = late.shape[0]
    d = groups * GROUP
    whole = half // GROUP
    for s in range(3):
        rows = slice(s * share, (s + 1) * share)
        mine = [late[g].astype(f32)[rows] for g in range(whole + 1)]
        other = [late_theirs[g].astype(f32)[rows] for g in range(whole, groups)]
        g_qkv[s] = jnp.concatenate(mine, 1)[:, :half] + jnp.concatenate(other, 1)[:, half - whole * GROUP :]
    width = 256
    for c in range(hidden // width):
        mine = early[:, 2 * c * width : 2 * (c + 1) * width].astype(f32)
        other = early_theirs[:share, 2 * c * width : 2 * (c + 1) * width].astype(f32)
        both = mine + other
        cols = slice(c * width, (c + 1) * width)
        g_up[:, cols] = both[:, :width]
        g_down[:, cols] = both[:, width:]
    mine = early[:, 4 * hidden : 4 * hidden + d].astype(f32)
    other = early_theirs[:share, 2 * hidden : 2 * hidden + d].astype(f32)
    g_out[...] = mine[:, :half] + other[:, half:]
    per = d // GROUP
    for n, ref in enumerate(vectors):
        ref[...] = one_line(small[n * per : (n + 1) * per] + small_theirs[n * per : (n + 1) * per])[0]
    base = 6 * per
    for s in range(3):
        rows = slice(base + s * per, base + (s + 1) * per)
        g_bqkv[s : s + 1, :] = one_line(small[rows])[:, :half] + one_line(small_theirs[rows])[:, half:]
    base += 3 * per
    count = hidden // GROUP
    g_bup[...] = one_line(small[base : base + count] + small_theirs[base + count : base + 2 * count])[0]
    for made in copies:
        made.wait()


def conclude(share, half, hidden, places, args, pieces, rows):
    d = 2 * half
    vmem = pl.BlockSpec(memory_space=pltpu.VMEM)
    return pl.pallas_call(
        functools.partial(conclude_kernel, share, half, hidden),
        in_specs=[pl.BlockSpec(memory_space=pltpu.SMEM)] + [vmem] * (len(args) + len(pieces)),
        out_specs=[vmem] * 6 + [pl.BlockSpec(memory_space=pl.ANY)] + [vmem] * 6,
        out_shape=[
            jax.ShapeDtypeStruct((3, share, half), f32),
            jax.ShapeDtypeStruct((share, hidden), f32),
            jax.ShapeDtypeStruct((share, hidden), f32),
            jax.ShapeDtypeStruct((share, half), f32),
            jax.ShapeDtypeStruct((3, half), f32),
            jax.ShapeDtypeStruct((hidden,), f32),
            jax.ShapeDtypeStruct((rows, d), bf16),
        ]
        + [jax.ShapeDtypeStruct((d,), f32)] * 6,
        scratch_shapes=[pltpu.SemaphoreType.DMA((len(pieces),))],
        compiler_params=pltpu.CompilerParams(vmem_limit_bytes=VMEM_LIMIT),
        cost_estimate=pl.CostEstimate(flops=1_000_000, bytes_accessed=12_000_000, transcendentals=0),
        name="conclude",
    )(places, *args, *pieces)


def on_device(
    tokens, lengths, gain_one, shift_one, w_qkv, b_qkv, w_out, b_out, gain_two, shift_two, w_up, b_up, w_down, b_down,
    cotangent,
):
    d = tokens.shape[1]
    n_dp = lax.axis_size("dp")
    here = lax.axis_index("dp")
    mp = lax.axis_index("mp")
    swap = [(0, 1), (1, 0)]
    half = w_qkv.shape[2]
    hidden = w_up.shape[1]

    long = (lengths[0] == LONG).astype(jnp.int32)
    side = jnp.where(mp == 0, long[0], long[4])
    mid = long[2]
    pick = lambda a, b: jnp.where(mp == 0, jnp.array(a, jnp.int32), jnp.array(b, jnp.int32))
    sc = pick([0, 0, 0, 0, 1, 2, 3, 0, 0, 0, 0, 0, 1, 2], [0, 0, 0, 4, 5, 3, 2, 0, 0, 0, 0, 1, 2, 0])
    sc = sc + side * jnp.array([1, 1, 0, 0, 0, 0, 0, 0, 1, 0, 0, 0, 0, 0], jnp.int32)
    sc = sc + mid * pick(
        [0, 0, 1, 0, 0, 0, 0, 0, 0, 0, 1, 0, 0, 0], [0, 0, 1, 0, 0, 0, 0, 0, 0, 1, 0, 0, 0, 0]
    )

    def other(own):
        share = own.shape[0] // n_dp
        piece = lax.dynamic_slice_in_dim(own, here * share, share, 0)
        return lax.all_gather(lax.ppermute(piece, "mp", swap), "dp", tiled=True)

    groups = d // GROUP
    first = half // GROUP
    share = d // n_dp
    by_hand = n_dp == 16
    row = lambda v: v.astype(f32)[None]
    cos, sin = (jnp.asarray(t) for t in rope_tables())
    up_other = other(w_up)
    down_other = other(w_down)
    w_out_all = jnp.concatenate([w_out, lax.ppermute(w_out, "mp", swap)], 0)
    w_own = jnp.transpose(w_qkv, (0, 2, 1))
    w_all = jnp.concatenate([w_own, lax.ppermute(w_own, "mp", swap)], 1)
    biases = lax.ppermute(jnp.concatenate([b_qkv.reshape(-1), b_up]), "mp", swap)
    b_qkv_all = jnp.concatenate([b_qkv, biases[: 3 * half].reshape(3, half)], 1).astype(f32)
    b_up_all = jnp.concatenate([b_up, biases[3 * half :]]).astype(f32)[None]

    gain, shift = row(gain_one), row(shift_one)
    tables = (cos, sin)
    *qkv, hidden_one, hidden_t = project(
        sc, tokens, gain, shift, w_own, b_qkv.astype(f32), *tables, 0, first, groups
    )
    attended = attend(sc, *qkv, 0, first)
    qkv = project(
        sc, hidden_one, gain, shift, w_all, b_qkv_all, *tables, first, groups - first, groups, qkv, attended[:1]
    )
    attended = attend(sc, *qkv, first, groups - first, attended)
    out_own, grad_mid, do, g_early, g_bup, small_two = middle(
        sc, tokens, cotangent, attended[0], w_out_all, row(b_out), row(gain_two), row(shift_two),
        w_up, up_other, b_up_all, w_down, down_other, row(b_down),
    )
    early = lax.psum_scatter(g_early, "dp", scatter_dimension=0, tiled=True)

    theirs = lax.ppermute(out_own, "mp", swap)
    out_tokens = assemble(jnp.stack([3 * mp, 3 - 3 * mp]), [out_own, theirs], 6 * BLK)
    args = (sc, *qkv, do, *attended, *tables, w_all, hidden_t, first)
    g_whole, gb_whole, grad_whole, small_w = back(*args, 0, 2, None, (tokens, gain, grad_mid))
    whole_theirs = lax.ppermute(grad_whole, "mp", swap)
    g_whole, out_tokens = lax.optimization_barrier((g_whole, out_tokens))
    g_qkv, g_bqkv, own, part = back(*args, 2, 1, share if by_hand else None, (g_whole, gb_whole))
    part, whole_theirs = lax.optimization_barrier((part, whole_theirs))

    x_shared = lax.dynamic_slice_in_dim(tokens, sc[BLOCK + 2] * BLK, BLK, 0)
    mid_shared = grad_mid[2 * BLK :]
    g_bqkv = g_bqkv.reshape(groups, 3, GROUP).transpose(1, 0, 2)
    small = jnp.concatenate(
        [small_w[:2].reshape(-1, GROUP), small_two[:4].reshape(-1, GROUP), g_bqkv.reshape(-1, GROUP), g_bup.reshape(-1, GROUP)]
    )
    n_small = small.shape[0]
    used = 4 * hidden
    if by_hand:
        small = jnp.pad(small, ((0, -n_small % 8), (0, 0)))
        early_part = jnp.pad(early[:, 2 * hidden :], ((0, -share % 16), (0, 0)))
        late, late_theirs, small, small_theirs, shared, shared_theirs, early_theirs = reduce_all(
            g_qkv, part, own, x_shared, gain, mid_shared, small, early_part
        )
    else:
        shared, last_sums = finish(x_shared, gain, mid_shared, own, lax.ppermute(part, "mp", swap))
        small = small.at[: last_sums.shape[0]].add(last_sums)
        shared_theirs = lax.ppermute(shared, "mp", swap)
        g_qkv = g_qkv.reshape(groups, d, 3, GROUP).transpose(2, 1, 0, 3).reshape(3, d, d)
        late = lax.psum_scatter(g_qkv, "dp", scatter_dimension=1, tiled=True)
        late_theirs = lax.ppermute(late, "mp", swap)
        small = lax.psum(small, "dp")
        small_theirs = lax.ppermute(small, "mp", swap)
        early_theirs = lax.ppermute(early[:, 2 * hidden :], "mp", swap)
    places = pick([0, 2, 3, 4], [4, 3, 2, 0])
    pieces = [grad_whole, shared, shared_theirs, whole_theirs]

    if by_hand:
        g_w, g_up, g_down, g_out, g_bq, g_bu, grad_tokens, *vectors = conclude(
            share, half, hidden, places,
            (late, late_theirs, early, early_theirs, small, small_theirs), pieces, 6 * BLK,
        )
        g_down, g_out = g_down.T, g_out.T
    else:
        grad_tokens = assemble(places, pieces, 6 * BLK)
        mlp = early[:, : 2 * hidden].astype(f32) + early_theirs[:, : 2 * hidden].astype(f32)
        mlp = mlp.reshape(share, hidden // 256, 2, 256)
        g_up = mlp[:, :, 0].reshape(share, hidden)
        g_down = mlp[:, :, 1].reshape(share, hidden).T
        g_out = early[:, used : used + half].astype(f32)
        g_out = (g_out + early_theirs[:, 2 * hidden + half : 2 * hidden + d].astype(f32)).T
        g_w = late[:, :, :half].astype(f32) + late_theirs[:, :, half:].astype(f32)
        mine, others = small[:n_small].reshape(-1), small_theirs[:n_small].reshape(-1)
        vectors = list((mine[: 6 * d] + others[: 6 * d]).reshape(6, d))
        pair = lambda v, lo, n, w: v[lo : lo + 2 * n * w].reshape(n, 2, w)
        g_bq = pair(mine, 6 * d, 3, half)[:, 0] + pair(others, 6 * d, 3, half)[:, 1]
        g_bu = pair(mine, 9 * d, 1, hidden)[0, 0] + pair(others, 9 * d, 1, hidden)[0, 1]
    return (
        out_tokens,
        grad_tokens,
        vectors[0],
        vectors[1],
        g_w,
        g_bq,
        g_out,
        vectors[4],
        vectors[2],
        vectors[3],
        g_up,
        g_bu,
        g_down,
        vectors[5],
    )


def solution(mesh):
    in_specs = (
        P("dp", None),
        P("dp", None),
        P(),
        P(),
        P(None, None, "mp"),
        P(None, "mp"),
        P("mp", None),
        P(),
        P(),
        P(),
        P(None, "mp"),
        P("mp"),
        P("mp", None),
        P(),
        P("dp", None),
    )
    out_specs = (
        P("dp", None),
        P("dp", None),
        P(),
        P(),
        P(None, "dp", "mp"),
        P(None, "mp"),
        P("mp", "dp"),
        P(),
        P(),
        P(),
        P("dp", "mp"),
        P("mp"),
        P("mp", "dp"),
        P(),
    )
    return jax.shard_map(on_device, mesh=mesh, in_specs=in_specs, out_specs=out_specs, check_vma=False)
```

```python
import functools

import jax
import jax.numpy as jnp
import numpy as np
from jax import lax
from jax.experimental import pallas as pl
from jax.experimental.pallas import tpu as pltpu
from jax.sharding import PartitionSpec as P

HD = 32
LONG = 1024
BLK = 512
GROUP = 128
epsilon = 1e-05
rotary_base = 10000.0
log2_e = 1.4426950408889634
ln_2 = 0.6931471805599453

f32 = jnp.float32
bf16 = jnp.bfloat16
NT = (((1,), (1,)), ((), ()))
NN = (((1,), (0,)), ((), ()))
TN = (((0,), (0,)), ((), ()))
VMEM_LIMIT = 60 << 20


def dot(a, b, dims=NN):
    return lax.dot_general(a, b, dims, preferred_element_type=f32)


def rope_tables():
    place = np.arange(LONG, dtype=np.float64)[:, None]
    frequency = rotary_base ** (-np.arange(HD // 2, dtype=np.float64) * 2.0 / HD)
    angles = place * frequency[None, :]
    cosines = np.concatenate([np.cos(angles), np.cos(angles)], 1)
    sines = np.concatenate([-np.sin(angles), np.sin(angles)], 1)
    repeat = GROUP // HD
    return (
        np.tile(cosines, (1, repeat)).astype(np.float32),
        np.tile(sines, (1, repeat)).astype(np.float32),
    )


def swap_halves(x):
    lane = lax.broadcasted_iota(jnp.int32, (1, GROUP), 1)
    low = (lane // (HD // 2)) % 2 == 0
    return jnp.where(low, pltpu.roll(x, GROUP - HD // 2, 1), pltpu.roll(x, HD // 2, 1))


def rotate(x, cosines, sines):
    return x * cosines + swap_halves(x) * sines


def rotate_back(x, cosines, sines):
    return x * cosines - swap_halves(x) * sines


def normalize(values):
    centred = values - jnp.mean(values, -1, keepdims=True)
    inverse = lax.rsqrt(jnp.mean(centred * centred, -1, keepdims=True) + epsilon)
    return (centred * inverse, inverse)


def normalize_back(normed, inverse, grad_normed):
    mean_grad = jnp.mean(grad_normed, -1, keepdims=True)
    mean_proj = jnp.mean(grad_normed * normed, -1, keepdims=True)
    return inverse * (grad_normed - mean_grad - normed * mean_proj)


FLAG, BLOCK, TABLE, PLACE = 0, 3, 7, 11


def slot(g, first):
    return g + jnp.where(g >= first, 1, 0)


def wide(ref):
    return ref[...].astype(f32)[None]


def project_kernel(with_hidden, count, start, sc, x_ref, gain, shift, b_ref, cos, sin, *rest):
    w_refs, rest = rest[:count], rest[count:]
    if with_hidden:
        q_ref, k_ref, v_ref, h_ref, ht_ref = rest
        normed, _ = normalize(x_ref[...].astype(f32))
        hidden = (normed * wide(gain) + wide(shift)).astype(bf16)
        h_ref[...] = hidden
        ht_ref[...] = hidden.T
    else:
        q_ref, k_ref, v_ref = rest[-3:]
        hidden = x_ref[...]
    w = jnp.concatenate([w_refs[n][s] for s in range(3) for n in range(count)], 0)
    out = dot(hidden, w, NT)
    for s in range(3):
        for n in range(count):
            at = (s * count + n) * GROUP
            bias = b_ref[s : s + 1, (start + n) * GROUP : (start + n + 1) * GROUP]
            part = out[:, at : at + GROUP] + bias
            if s == 0:
                q_ref[n] = (rotate(part, cos[...], sin[...]) * (HD ** (-0.5) * log2_e)).astype(bf16)
            elif s == 1:
                k_ref[n] = rotate(part, cos[...], sin[...]).astype(bf16)
            else:
                v_ref[n] = part.astype(bf16)


def project(sc, x, gain, shift, w, b, cos, sin, start, count, groups, before=(), after=()):
    d = x.shape[1]
    rows = 4 * BLK
    with_hidden = not before
    table = pl.BlockSpec((BLK, GROUP), lambda i, s: (s[TABLE + i], 0))
    source = (lambda i, s: (s[BLOCK + i], 0)) if with_hidden else (lambda i, s: (i, 0))
    if with_hidden:
        held = groups - count
        out = pl.BlockSpec((held, BLK, GROUP), lambda i, s: (0, i, 0))
    else:
        held = count
        out = pl.BlockSpec((held, BLK, GROUP), lambda i, s: (1, i, 0))
    out_specs = [out, out, out]
    out_shape = [jax.ShapeDtypeStruct((2 * held, rows, GROUP), bf16)] * 3
    if with_hidden:
        out_specs += [pl.BlockSpec((BLK, d), lambda i, s: (i, 0)), pl.BlockSpec((d, BLK), lambda i, s: (0, i))]
        out_shape += [jax.ShapeDtypeStruct((rows, d), bf16), jax.ShapeDtypeStruct((d, rows), bf16)]
    extra = (*before, *after)
    weight = lambda n: pl.BlockSpec((3, GROUP, d), lambda i, s: (0, start + n, 0))
    return pl.pallas_call(
        functools.partial(project_kernel, with_hidden, count, start),
        grid_spec=pltpu.PrefetchScalarGridSpec(
            num_scalar_prefetch=1,
            grid=(4,),
            in_specs=[
                pl.BlockSpec((BLK, d), source),
                pl.BlockSpec((d,), lambda i, s: (0,)),
                pl.BlockSpec((d,), lambda i, s: (0,)),
                pl.BlockSpec(b.shape, lambda i, s: (0, 0)),
                table,
                table,
            ]
            + [weight(n) for n in range(count)]
            + [pl.BlockSpec(memory_space=pl.ANY)] * len(extra),
            out_specs=out_specs,
        ),
        out_shape=out_shape,
        input_output_aliases={7 + count + n: n for n in range(len(before))},
        compiler_params=pltpu.CompilerParams(vmem_limit_bytes=VMEM_LIMIT),
        cost_estimate=pl.CostEstimate(
            flops=2 * rows * d * 3 * GROUP * count, bytes_accessed=6_000_000, transcendentals=0
        ),
        name="project",
    )(sc, x, gain, shift, b, cos, sin, *[w] * count, *extra)


def attend_body(q, k_ref, v_ref, o_ref, l_ref, e_ref, store, start, count):
    lane = lax.broadcasted_iota(jnp.int32, (1, GROUP), 1) // HD
    heads = GROUP // HD
    chunks = count // BLK
    values_t = v_ref[pl.ds(start, count), :].T
    ones = jnp.ones((16, count), bf16)
    outs, inverses = [], []

    def score(h, c):
        keys = k_ref[pl.ds(start + c * BLK, BLK), :]
        scores = dot(jnp.where(lane == h, keys, jnp.zeros_like(keys)), q, NT)
        store[h % 2, c * BLK : (c + 1) * BLK, :] = scores
        return jnp.max(scores.reshape(BLK // 8, 8, BLK), axis=0)

    def score_max(h, c, so_far):
        found = score(h, c)
        return found if so_far is None else jnp.maximum(so_far, found)

    top = None
    for c in range(chunks):
        top = score_max(0, c, top)
    row_max = jnp.max(top, axis=0, keepdims=True)
    for h in range(heads):
        top = None
        total = None
        stacked = jnp.concatenate([values_t[HD * h : HD * (h + 1)], ones], 0)
        for c in range(chunks):
            if h + 1 < heads:
                top = score_max(h + 1, c, top)
            rows = slice(c * BLK, (c + 1) * BLK)
            expo = jnp.exp2(store[h % 2, rows, :] - row_max).astype(bf16)
            e_ref[h, pl.ds(start + c * BLK, BLK), :] = expo
            part = dot(stacked[:, rows], expo)
            total = part if total is None else total + part
        inverse = 1.0 / total[HD : HD + 1]
        outs.append(total[:HD] * inverse)
        inverses.append(jnp.broadcast_to(inverse, (HD, BLK)))
        if h + 1 < heads:
            row_max = jnp.max(top, axis=0, keepdims=True)
    o_ref[...] = jnp.concatenate(outs, 0).T.astype(bf16)
    l_ref[...] = jnp.concatenate(inverses, 0).T


def attend_kernel(sc, q_ref, k_ref, v_ref, *rest):
    o_ref, l_ref, e_ref, store = rest[-4:]
    b = pl.program_id(1)
    refs = (k_ref, v_ref, o_ref, l_ref, e_ref, store)

    @pl.when(sc[FLAG + b] == 1)
    def _():
        attend_body(q_ref[...], *refs, 0, LONG)

    @pl.when(sc[FLAG + b] == 0)
    def _():
        start = pl.multiple_of(jnp.where(b == 1, BLK, 0), BLK)
        attend_body(q_ref[...], *refs, start, BLK)


def attend(sc, q, k, v, start, count, before=()):
    groups = q.shape[0] - 1
    heads = GROUP // HD
    own = 3 * BLK
    place = start + (1 if before else 0)
    qs = pl.BlockSpec((None, BLK, GROUP), lambda g, b, s: (g + place, b, 0))
    ks = pl.BlockSpec((None, LONG, GROUP), lambda g, b, s: (g + place, b // 2, 0))
    os = pl.BlockSpec((None, BLK, GROUP), lambda g, b, s: (g + start, b, 0))
    es = pl.BlockSpec((heads, LONG, BLK), lambda g, b, s: ((g + start) * 3 + b, 0, 0))
    return pl.pallas_call(
        attend_kernel,
        grid_spec=pltpu.PrefetchScalarGridSpec(
            num_scalar_prefetch=1,
            grid=(count, 3),
            in_specs=[qs, ks, ks] + [pl.BlockSpec(memory_space=pl.ANY)] * len(before),
            out_specs=[os, os, es],
            scratch_shapes=[pltpu.VMEM((2, LONG, BLK), f32)],
        ),
        out_shape=[
            jax.ShapeDtypeStruct((groups, own, GROUP), bf16),
            jax.ShapeDtypeStruct((groups, own, GROUP), f32),
            jax.ShapeDtypeStruct((groups * 3 * heads, LONG, BLK), bf16),
        ],
        input_output_aliases={4 + n: n for n in range(len(before))},
        compiler_params=pltpu.CompilerParams(vmem_limit_bytes=VMEM_LIMIT),
        cost_estimate=pl.CostEstimate(
            flops=count * 5_000_000_000, bytes_accessed=count * 16_000_000, transcendentals=count * 6_000_000
        ),
        name="attend",
    )(sc, q, k, v, *before)


def attend_back_body(
    q_ref, k_ref, v_ref, do_ref, o_ref, l_ref, e_ref, prod, dk_sum, dv_sum, start, count
):
    lane = lax.broadcasted_iota(jnp.int32, (1, GROUP), 1) // HD
    heads = GROUP // HD
    q = q_ref[...]
    do = (do_ref[...].astype(f32) * l_ref[...]).astype(bf16)
    both = do.astype(f32) * o_ref[...].astype(f32)
    upper = both.astype(bf16)
    lower = (both - upper.astype(f32)).astype(bf16)
    pick = (
        lax.broadcasted_iota(jnp.int32, (8, GROUP), 0)
        == lax.broadcasted_iota(jnp.int32, (8, GROUP), 1) // HD
    )
    pick = pick.astype(f32).astype(bf16)
    delta = dot(pick, upper, NT) + dot(pick, lower, NT)
    keys_t = k_ref[pl.ds(start, count), :].T
    chunks = count // BLK
    tiles = [(h, c) for h in range(heads) for c in range(chunks)]

    def grad_probs(i):
        h, c = tiles[i]
        values = v_ref[pl.ds(start + c * BLK, BLK), :]
        prod[i % 2] = dot(jnp.where(lane == h, values, jnp.zeros_like(values)), do, NT)

    grad_probs(0)
    dq_t = [None] * heads
    for i, (h, c) in enumerate(tiles):
        if i + 1 < len(tiles):
            grad_probs(i + 1)
        rows = pl.ds(start + c * BLK, BLK)
        expo = e_ref[h, rows, :]
        ds = (expo.astype(f32) * (prod[i % 2] - delta[h : h + 1])).astype(bf16)
        dv_sum[rows, :] += dot(expo, jnp.where(lane == h, do, jnp.zeros_like(do)))
        dk_sum[rows, :] += dot(ds, jnp.where(lane == h, q, jnp.zeros_like(q)))
        part = dot(keys_t[HD * h : HD * (h + 1), c * BLK : (c + 1) * BLK], ds)
        dq_t[h] = part if dq_t[h] is None else dq_t[h] + part
    return jnp.concatenate(dq_t, 0).T


def window_back(dq, dk_sum, dv_sum, tables, w_ref, ht_ref, dh_sum):
    parts = [] if dq is None else [dq]
    dk = dk_sum[...] * ln_2
    rotated = []
    for n, (cos, sin) in enumerate(tables):
        rotated.append(rotate_back(dk[n * BLK : (n + 1) * BLK], cos[...], sin[...]))
    parts.append(jnp.concatenate(rotated, 0).astype(bf16))
    parts.append(dv_sum[...].astype(bf16))
    both = jnp.concatenate(parts, 1)
    w = jnp.concatenate([w_ref[s] for s in range(3 - len(parts), 3)], 0)
    for n in range(len(tables)):
        rows = slice(n * BLK, (n + 1) * BLK)
        dh_sum[rows, :] += dot(both[rows], w)
    return dot(ht_ref[...], both), jnp.sum(both.astype(f32), 0, keepdims=True)


def back_kernel(
    mode, sc, q_ref, k_ref, v_ref, do_ref, o_ref, l_ref, e_ref, cos, sin, cos0, sin0, cos1, sin1, w_ref, ht_ref,
    *rest,
):
    g = pl.program_id(0)
    last_g = pl.num_programs(0) - 1
    step = pl.program_id(1)
    if mode == "whole":
        x_ref, gain, mid_ref, g_ref, gb_ref, out_ref, small, dq_cat, prod, dk_sum, dv_sum, dh_sum = rest
    elif mode == "far":
        before, before_b, g_ref, gb_ref, dq_out, part_ref, prod, dk_sum, dv_sum, dh_sum = rest
    else:
        before, before_b, dq_in, g_ref, gb_ref, own_ref, prod, dk_sum, dv_sum, dh_sum = rest
    refs = (q_ref, k_ref, v_ref, do_ref, o_ref, l_ref, e_ref, prod, dk_sum, dv_sum)
    own_tables = (cos0, sin0), (cos1, sin1)
    finish_q = lambda dq: rotate_back(dq * (HD ** (-0.5)), cos[...], sin[...]).astype(bf16)

    @pl.when(step == 0)
    def _():
        dk_sum[...] = jnp.zeros_like(dk_sum)
        dv_sum[...] = jnp.zeros_like(dv_sum)

    @pl.when((step == 0) & (g == 0))
    def _():
        dh_sum[...] = jnp.zeros_like(dh_sum)

    if mode == "whole":
        place = pl.ds(pl.multiple_of(step * BLK, BLK), BLK)

        @pl.when(sc[FLAG] == 1)
        def _():
            dq_cat[place, :] = finish_q(attend_back_body(*refs, 0, LONG))

        @pl.when(sc[FLAG] == 0)
        def _():
            dq_cat[place, :] = finish_q(attend_back_body(*refs, pl.multiple_of(step * BLK, BLK), BLK))

        @pl.when(step == 1)
        def _():
            g_ref[...], gb_ref[...] = window_back(
                dq_cat[...], dk_sum, dv_sum, own_tables, w_ref, ht_ref, dh_sum
            )

        @pl.when((step == 1) & (g == last_g))
        def _():
            sums = [None, None]
            for rows in (slice(0, BLK), slice(BLK, LONG)):
                out, *terms = finish_rows(x_ref[rows, :], wide(gain), mid_ref[rows, :], dh_sum[rows, :])
                out_ref[rows, :] = out
                for n, term in enumerate(terms):
                    sums[n] = term if sums[n] is None else sums[n] + term
            small[...] = jnp.concatenate(sums + [jnp.zeros_like(sums[0])] * 6, 0)

    elif mode == "far":

        @pl.when(sc[FLAG + 2] == 1)
        def _():
            dq_out[...] = attend_back_body(*refs, 0, BLK)

        @pl.when(sc[FLAG + 2] == 0)
        def _():
            dq_out[...] = jnp.zeros_like(dq_out)

        weight, bias = window_back(None, dk_sum, dv_sum, own_tables[:1], w_ref, ht_ref, dh_sum)
        g_ref[:, :GROUP] = before[:, :GROUP]
        g_ref[:, GROUP:] = before[:, GROUP:] + weight
        gb_ref[:, :GROUP] = before_b[:, :GROUP]
        gb_ref[:, GROUP:] = before_b[:, GROUP:] + bias

        @pl.when(g == last_g)
        def _():
            part_ref[...] = dh_sum[...].astype(bf16)

    else:
        dq = finish_q(attend_back_body(*refs, 0, BLK) + dq_in[...])
        weight, bias = window_back(dq, dk_sum, dv_sum, own_tables[:1], w_ref, ht_ref, dh_sum)
        weight = weight + before[...]
        gb_ref[...] = bias + before_b[...]
        g_ref[...] = weight.astype(bf16)

        @pl.when(g == last_g)
        def _():
            own_ref[...] = dh_sum[...]


def back(mode, sc, q, k, v, do, o, inverse, expo, cos, sin, w, hidden_t, first, more):
    groups = o.shape[0]
    d = w.shape[2]
    heads = GROUP // HD
    blocks = 2 if mode == "whole" else 1
    query = 0 if mode == "whole" else 2
    key = {"whole": 0, "far": 3, "near": 2}[mode]
    keys = LONG if mode == "whole" else BLK
    one = pl.Buffered(buffer_count=1)
    qs = pl.BlockSpec((None, BLK, GROUP), lambda g, b, s: (slot(g, first), b + query, 0))
    ks = pl.BlockSpec((None, keys, GROUP), lambda g, b, s: (slot(g, first), key, 0))
    os = pl.BlockSpec((None, BLK, GROUP), lambda g, b, s: (g, b + query, 0))
    es = pl.BlockSpec((heads, keys, BLK), lambda g, b, s: (g * 3 + b + query, 1 if mode == "far" else 0, 0))
    tq = pl.BlockSpec((BLK, GROUP), lambda g, b, s: (s[TABLE + b + query], 0))
    t0 = pl.BlockSpec((BLK, GROUP), lambda g, b, s: (s[TABLE + key], 0))
    t1 = pl.BlockSpec((BLK, GROUP), lambda g, b, s: (s[TABLE + key + (blocks - 1)], 0))
    weight = pl.BlockSpec((None, d, 3 * GROUP), lambda g, b, s: (g, 0, 0))
    bias = pl.BlockSpec((None, 1, 3 * GROUP), lambda g, b, s: (g, 0, 0))
    dq_part = pl.BlockSpec((None, BLK, GROUP), lambda g, b, s: (g, 0, 0))
    whole = lambda *shape: pl.BlockSpec(shape, lambda g, b, s: (0, 0))
    in_specs = [qs, ks, ks, os, os, os, es, tq, tq, t0, t0, t1, t1]
    in_specs += [
        pl.BlockSpec((3, GROUP, d), lambda g, b, s: (0, g, 0)),
        pl.BlockSpec((d, keys), lambda g, b, s: (0, key), pipeline_mode=one),
    ]
    bias_shape = jax.ShapeDtypeStruct((groups, 1, 3 * GROUP), f32)
    scratch = [
        pltpu.VMEM((2, BLK, BLK), f32),
        pltpu.VMEM((keys, GROUP), f32),
        pltpu.VMEM((keys, GROUP), f32),
        pltpu.VMEM((keys, d), f32),
    ]
    if mode == "whole":
        in_specs += [
            pl.BlockSpec((LONG, d), lambda g, b, s: (s[BLOCK] // 2, 0), pipeline_mode=one),
            pl.BlockSpec((d,), lambda g, b, s: (0,)),
            pl.BlockSpec((LONG, d), lambda g, b, s: (0, 0), pipeline_mode=one),
        ]
        out_specs = [weight, bias, whole(LONG, d), whole(8, d)]
        out_shape = [
            jax.ShapeDtypeStruct((groups, d, 3 * GROUP), f32),
            bias_shape,
            jax.ShapeDtypeStruct((LONG, d), bf16),
            jax.ShapeDtypeStruct((8, d), f32),
        ]
        scratch = [pltpu.VMEM((LONG, GROUP), bf16)] + scratch
    elif mode == "far":
        in_specs += [weight, bias]
        out_specs = [weight, bias, dq_part, whole(BLK, d)]
        out_shape = [
            jax.ShapeDtypeStruct((groups, d, 3 * GROUP), f32),
            bias_shape,
            jax.ShapeDtypeStruct((groups, BLK, GROUP), f32),
            jax.ShapeDtypeStruct((BLK, d), bf16),
        ]
    else:
        in_specs += [weight, bias, dq_part]
        out_specs = [weight, bias, whole(BLK, d)]
        out_shape = [
            jax.ShapeDtypeStruct((groups, d, 3 * GROUP), bf16),
            bias_shape,
            jax.ShapeDtypeStruct((BLK, d), f32),
        ]
    return pl.pallas_call(
        functools.partial(back_kernel, mode),
        grid_spec=pltpu.PrefetchScalarGridSpec(
            num_scalar_prefetch=1,
            grid=(groups, blocks),
            in_specs=in_specs,
            out_specs=out_specs,
            scratch_shapes=scratch,
        ),
        out_shape=out_shape,
        compiler_params=pltpu.CompilerParams(vmem_limit_bytes=VMEM_LIMIT),
        cost_estimate=pl.CostEstimate(
            flops=groups * blocks * keys * 5_000_000, bytes_accessed=groups * blocks * 6_000_000, transcendentals=0
        ),
        name="back_" + mode,
    )(sc, q, k, v, do, o, inverse, expo, cos, sin, cos, sin, cos, sin, w, hidden_t, *more)


def gelu_parts(z):
    density = jnp.exp2(z * z * (-0.5 * log2_e)) * 0.3989422804014327
    t = 1.0 / (1.0 + 0.2316419 * jnp.abs(z))
    poly = t * (
        0.319381530
        + t * (-0.356563782 + t * (1.781477937 + t * (-1.821255978 + t * 1.330274429)))
    )
    tail = density * poly
    cdf = jnp.where(z >= 0, 1.0 - tail, tail)
    return z * cdf, cdf + z * density


def middle_kernel(
    sc, x0, x1, x2, y0, y1, y2, o_ref, w_out_own, w_out_other, b_out, gain, shift,
    up_a, up_b, up_c, up_d, b_up, down_a, down_b, down_c, down_d, b_down,
    out_ref, mid_ref, do_ref, g_ref, g_bup, g_small,
    w_out, r1, h2, h2t, dy, dyt, acc, back,
):
    i = pl.program_id(0)
    last = pl.num_programs(0) - 1
    xs, ys = (x0, x1, x2), (y0, y1, y2)
    blocks = [slice(j * BLK, (j + 1) * BLK) for j in range(3)]
    groups = o_ref.shape[0]
    heads_of = lambda rows: jnp.concatenate([o_ref[g, rows, :] for g in range(groups)], 1)

    @pl.when(i == 0)
    def _():
        w_out[: w_out_own.shape[0], :] = w_out_own[...]
        w_out[w_out_own.shape[0] :, :] = w_out_other[...]
        for j, rows in enumerate(blocks):
            mixed = dot(heads_of(rows), w_out[...]) + wide(b_out) + xs[j][...].astype(f32)
            r1[rows, :] = mixed
            normed, _ = normalize(mixed)
            hidden = (normed * wide(gain) + wide(shift)).astype(bf16)
            h2[rows, :] = hidden
            h2t[:, rows] = hidden.T
            dy[rows, :] = ys[j][...]
            dyt[:, rows] = ys[j][...].T
            acc[rows, :] = jnp.zeros_like(mixed)
            back[rows, :] = jnp.zeros_like(mixed)

    @pl.when(i < last)
    def _():
        first, second = 2 * i < last, 2 * i + 1 < last
        w_up = jnp.concatenate(
            [jnp.where(first, up_a[...], up_c[...]), jnp.where(second, up_b[...], up_d[...])], 1
        )
        w_down = jnp.concatenate(
            [jnp.where(first, down_a[...], down_c[...]), jnp.where(second, down_b[...], down_d[...])], 0
        )
        bias = b_up[...]
        width = up_a.shape[1]
        total = dy.shape[0]
        parts = [slice(j, j + 256) for j in range(0, total, BLK // 2)]
        count = len(parts)
        actives, grads = [None] * count, [None] * count
        ups, downs = [None] * count, [None] * count
        col_sum = None

        def ahead(j):
            ups[j] = dot(h2[parts[j], :], w_up) + bias
            downs[j] = dot(dy[parts[j], :], w_down, NT)

        ahead(0)
        for j, rows in enumerate(parts):
            if j + 1 < count:
                ahead(j + 1)
            active, slope = gelu_parts(ups[j])
            actives[j] = active.astype(bf16)
            grads[j] = (downs[j] * slope).astype(bf16)
            s = jnp.sum(grads[j].astype(f32), 0, keepdims=True)
            col_sum = s if col_sum is None else col_sum + s
            acc[rows, :] += dot(actives[j], w_down)
            back[rows, :] += dot(grads[j], w_up, NT)
        g_bup[...] = col_sum
        g_up = dot(h2t[...], jnp.concatenate(grads, 0)).astype(bf16)
        g_down = dot(dyt[...], jnp.concatenate(actives, 0)).astype(bf16)
        for n in range(2):
            cols = slice(n * width, (n + 1) * width)
            g_ref[:, 2 * n * width : (2 * n + 1) * width] = g_up[:, cols]
            g_ref[:, (2 * n + 1) * width : (2 * n + 2) * width] = g_down[:, cols]

    @pl.when(i == last)
    def _():
        sums = [None] * 4
        lows = []
        for j, rows in enumerate(blocks):
            mixed = r1[rows, :]
            place = pl.multiple_of(sc[PLACE + j] * BLK, BLK)
            out_ref[pl.ds(place, BLK), :] = (acc[rows, :] + wide(b_down) + mixed).astype(bf16)
            normed, inverse = normalize(mixed)
            top = dy[rows, :].astype(f32)
            dh = back[rows, :]
            dr = top + normalize_back(normed, inverse, dh * wide(gain))
            mid_ref[rows, :] = dr
            low = dr.astype(bf16)
            lows.append(low)
            do = dot(low, w_out[...], NT).astype(bf16)
            for g in range(groups):
                do_ref[g, rows, :] = do[:, g * GROUP : (g + 1) * GROUP]
            for n, term in enumerate((dh * normed, dh, dr, top)):
                s = jnp.sum(term, 0, keepdims=True)
                sums[n] = s if sums[n] is None else sums[n] + s
        weight = dot(jnp.concatenate(lows, 0).T, heads_of(slice(0, 3 * BLK))).astype(bf16)
        width = weight.shape[1]
        g_ref[:, :width] = weight
        g_ref[:, width:] = jnp.zeros((g_ref.shape[0], g_ref.shape[1] - width), bf16)
        g_small[...] = jnp.concatenate(sums + [jnp.zeros_like(sums[0])] * 4, 0)


def middle(sc, tokens, cotangent, o, w_out_own, w_out_other, b_out, gain, shift, up_own, up_other, b_up, down_own, down_other, b_down):
    d = tokens.shape[1]
    groups = o.shape[0]
    own = 3 * BLK
    half = up_own.shape[1]
    piece = 256
    per = half // piece
    steps = per + 1
    one = pl.Buffered(buffer_count=1)
    whole = lambda *shape: pl.BlockSpec(shape, lambda i, s: (0,) * len(shape), pipeline_mode=one)
    rows_of = lambda j: pl.BlockSpec((BLK, d), lambda i, s: (s[BLOCK + j], 0), pipeline_mode=one)
    fixed = lambda *shape: pl.BlockSpec(shape, lambda i, s: (0,) * len(shape))
    at = lambda i: jnp.minimum(i, per - 1)
    places = [
        lambda i: jnp.minimum(2 * i, per - 1),
        lambda i: jnp.minimum(2 * i + 1, per - 1),
        lambda i: jnp.clip(2 * i - per, 0, per - 1),
        lambda i: jnp.clip(2 * i + 1 - per, 0, per - 1),
    ]
    ups = [pl.BlockSpec((d, piece), functools.partial(lambda p, i, s: (0, p(i)), p)) for p in places]
    downs = [pl.BlockSpec((piece, d), functools.partial(lambda p, i, s: (p(i), 0), p)) for p in places]
    return pl.pallas_call(
        middle_kernel,
        grid_spec=pltpu.PrefetchScalarGridSpec(
            num_scalar_prefetch=1,
            grid=(steps,),
            in_specs=[rows_of(0), rows_of(1), rows_of(2)] * 2
            + [
                whole(groups, own, GROUP),
                whole(*w_out_own.shape),
                whole(*w_out_other.shape),
                whole(d),
                whole(d),
                whole(d),
                *ups,
                pl.BlockSpec((1, 2 * piece), lambda i, s: (0, at(i))),
                *downs,
                whole(d),
            ],
            out_specs=[
                fixed(own, d),
                fixed(own, d),
                fixed(groups, own, GROUP),
                pl.BlockSpec((d, 4 * piece), lambda i, s: (0, i)),
                pl.BlockSpec((1, 2 * piece), lambda i, s: (0, at(i))),
                fixed(8, d),
            ],
            scratch_shapes=[
                pltpu.VMEM((d, d), bf16),
                pltpu.VMEM((own, d), f32),
                pltpu.VMEM((own, d), bf16),
                pltpu.VMEM((d, own), bf16),
                pltpu.VMEM((own, d), bf16),
                pltpu.VMEM((d, own), bf16),
                pltpu.VMEM((own, d), f32),
                pltpu.VMEM((own, d), f32),
            ],
        ),
        out_shape=[
            jax.ShapeDtypeStruct((own, d), bf16),
            jax.ShapeDtypeStruct((own, d), f32),
            jax.ShapeDtypeStruct((groups, own, GROUP), bf16),
            jax.ShapeDtypeStruct((d, 4 * piece * steps), bf16),
            jax.ShapeDtypeStruct((1, 2 * half), f32),
            jax.ShapeDtypeStruct((8, d), f32),
        ],
        compiler_params=pltpu.CompilerParams(vmem_limit_bytes=VMEM_LIMIT),
        cost_estimate=pl.CostEstimate(
            flops=2 * own * d * (3 * d + 12 * half), bytes_accessed=40_000_000, transcendentals=8_000_000
        ),
        name="middle",
    )(sc, tokens, tokens, tokens, cotangent, cotangent, cotangent, o, w_out_own, w_out_other, b_out, gain, shift,
      *[up_own] * 2, *[up_other] * 2, b_up, *[down_own] * 2, *[down_other] * 2, b_down)


def finish_rows(x, gain, mid, dh):
    normed, inverse = normalize(x.astype(f32))
    out = (mid + normalize_back(normed, inverse, dh * gain)).astype(bf16)
    return out, jnp.sum(dh * normed, 0, keepdims=True), jnp.sum(dh, 0, keepdims=True)


def lines(v):
    return jnp.concatenate([v[:, j * GROUP : (j + 1) * GROUP] for j in range(v.shape[1] // GROUP)], 0)


def last_kernel(
    q_ref, k_ref, v_ref, do_ref, o_ref, l_ref, e_ref, cos, sin, w_ref, ht_ref, before, before_b, dq_in,
    part_ref, tokens, gain, mid, small_w, small_two, gup_ref, early_ref,
    sum_out, theirs_out, small_out, small_theirs_out, rows_out, rows_theirs_out, early_out,
    prod, dk_sum, dv_sum, dh_sum, gb_sum, g_all, part_in, x_ref, mid_ref, early_part, early_in,
    r1, a1, r2, a2, r3, sums, theirs, rows_ref, rows_in, s0, s1, s2, s3, q1, q2, q3, q4, send, recv, local,
):
    g = pl.program_id(0)
    groups = g_all.shape[3]
    here = lax.axis_index("dp")
    mp = lax.axis_index("mp")
    c = here % 2
    x = (here // 2) % 2
    z = here // 4
    core = (here + 1 - 2 * c, mp)
    side = (here + 2 - 4 * x, mp)
    across = (here, 1 - mp)
    line = [((z + n) % 4, ((z + n) % 4 * 4 + here % 4, mp)) for n in (1, 2, 3)]

    numbers = {}

    def copy(name, src, dst, dev):
        n = numbers.setdefault(name, len(numbers))
        return pltpu.make_async_remote_copy(
            src_ref=src,
            dst_ref=dst,
            send_sem=send.at[n],
            recv_sem=recv.at[n],
            device_id=dev,
            device_id_type=pl.DeviceIdType.MESH,
        )

    part_copy = copy("part", part_ref, part_in, across)
    early_copy = copy("early", early_part, early_in, across)
    rows_copy = copy("rows", rows_ref, rows_in, across)
    by_core = [copy(("c", n), g_all.at[:, :, 1 - c, n], r1.at[:, :, n], core) for n in range(groups)]
    by_side = [copy(("x", n), a1.at[:, 1 - x, n], r2.at[:, n], side) for n in range(groups)]
    by_line = [
        [copy(("z", n, m), a2.at[at, n], r3.at[m, n], dev) for m, (at, dev) in enumerate(line)]
        for n in range(groups)
    ]
    by_across = [copy(("y", n), sums.at[n], theirs.at[n], across) for n in range(groups)]
    small_core = copy("sc", s0, q1, core)
    small_side = copy("sx", s1, q2, side)
    small_line = [copy(("sz", m), s2, q3.at[z], dev) for m, (_, dev) in enumerate(line)]
    small_across = copy("sy", s3, q4, across)
    rows = pl.ds(pl.multiple_of((2 + mp) * BLK, BLK), BLK)
    x_copy = pltpu.make_async_copy(tokens.at[rows, :], x_ref, local.at[0])
    mid_copy = pltpu.make_async_copy(mid.at[2 * BLK : 3 * BLK, :], mid_ref, local.at[1])

    @pl.when(g == 0)
    def _():
        barrier = pltpu.get_barrier_semaphore()
        partners = [core, side, across] + [dev for _, dev in line]
        for dev in partners:
            pl.semaphore_signal(barrier, inc=1, device_id=dev, device_id_type=pl.DeviceIdType.MESH)
        pl.semaphore_wait(barrier, len(partners))
        part_copy.start()
        x_copy.start()
        mid_copy.start()
        dh_sum[...] = jnp.zeros_like(dh_sum)
        share, width = early_ref.shape[0], early_part.shape[1]
        start = 2 * gup_ref.shape[1] // 2
        early_part[share:, :] = jnp.zeros((early_part.shape[0] - share, width), bf16)
        early_part[:share, :] = early_ref[:, start : start + width]
        early_copy.start()

    dk_sum[...] = jnp.zeros_like(dk_sum)
    dv_sum[...] = jnp.zeros_like(dv_sum)
    refs = (q_ref, k_ref, v_ref, do_ref, o_ref, l_ref, e_ref, prod, dk_sum, dv_sum)
    dq = (attend_back_body(*refs, 0, BLK) + dq_in[...]) * (HD ** (-0.5))
    dq = rotate_back(dq, cos[...], sin[...]).astype(bf16)
    weight, bias = window_back(dq, dk_sum, dv_sum, ((cos, sin),), w_ref, ht_ref, dh_sum)
    weight = weight + before[...]
    gb_sum[g] = bias + before_b[...]
    share = early_ref.shape[0]
    fill = jnp.zeros((g_all.shape[4] - 3 * share, GROUP), f32)
    for n in range(16):
        part = weight[n * share : (n + 1) * share]
        pieces = [part[:, s * GROUP : (s + 1) * GROUP] for s in range(3)]
        g_all[n // 4, n // 2 % 2, n % 2, g] = jnp.concatenate(pieces + [fill], 0).astype(bf16)

    def second(n):
        by_core[n].wait()
        a1[:, :, n] = (g_all[:, :, c, n].astype(f32) + r1[:, :, n].astype(f32)).astype(bf16)
        by_side[n].start()

    def third(n):
        by_side[n].wait()
        a2[:, n] = (a1[:, x, n].astype(f32) + r2[:, n].astype(f32)).astype(bf16)
        for made in by_line[n]:
            made.start()

    def fourth(n):
        for made in by_line[n]:
            made.wait()
        total = a2[z, n].astype(f32)
        for m in range(3):
            total = total + r3[m, n].astype(f32)
        sums[n] = total.astype(bf16)
        by_across[n].start()

    for n in range(groups):

        @pl.when(g == n)
        def _(n=n):
            by_core[n].start()
            if n == groups - 1:
                return
            for late, stage in ((1, second), (2, third), (3, fourth)):
                if n >= late:
                    stage(n - late)

    @pl.when(g == groups - 1)
    def _():
        x_copy.wait()
        mid_copy.wait()
        part_copy.wait()
        out, one, two = finish_rows(x_ref[...], wide(gain), mid_ref[...], dh_sum[...] + part_in[...].astype(f32))
        rows_ref[...] = out
        rows_copy.start()
        n = groups - 1
        second(n - 1)
        third(n - 2)
        held = [lines(small_w[0:1, :] + one), lines(small_w[1:2, :] + two)]
        held += [lines(small_two[m : m + 1, :]) for m in range(4)]
        held += [gb_sum[m, :, s * GROUP : (s + 1) * GROUP] for s in range(3) for m in range(groups)]
        held.append(lines(gup_ref[...]))
        held = jnp.concatenate(held, 0)
        s0[...] = jnp.concatenate([held, jnp.zeros((s0.shape[0] - held.shape[0], GROUP), f32)], 0)
        small_core.start()
        second(n)
        fourth(n - 3)
        third(n - 1)
        small_core.wait()
        s1[...] = s0[...] + q1[...]
        small_side.start()
        fourth(n - 2)
        third(n)
        small_side.wait()
        s2[...] = s1[...] + q2[...]
        for made in small_line:
            made.start()
        fourth(n - 1)
        for made in small_line:
            made.wait()
        q3[z] = s2[...]
        s3[...] = (q3[0] + q3[1]) + (q3[2] + q3[3])
        small_across.start()
        fourth(n)
        early_copy.wait()
        early_out[...] = early_in[...]
        small_out[...] = s3[...]
        sum_out[...] = sums[...]
        rows_out[...] = rows_ref[...]
        rows_copy.wait()
        rows_theirs_out[...] = rows_in[...]
        small_across.wait()
        small_theirs_out[...] = q4[...]
        for made in by_across:
            made.wait()
        theirs_out[...] = theirs[...]


def last(q, k, v, do, o, inverse, expo, cos, sin, w, hidden_t, first, g_sum, gb_sum, dq_far, part, tokens, gain, mid,
         small_w, small_two, g_bup, early):
    groups = o.shape[0]
    d = w.shape[2]
    heads = GROUP // HD
    share = early.shape[0]
    held = -(-3 * share // 16) * 16
    block = (groups, held, GROUP)
    count = 6 * d // GROUP + groups * 3 + g_bup.shape[1] // GROUP
    small = (-(-count // 8) * 8, GROUP)
    early_part = (-(-share // 16) * 16, g_bup.shape[1] + d)
    copies = 3 + 6 * groups + 6
    one = pl.Buffered(buffer_count=1)
    hbm = pl.BlockSpec(memory_space=pl.ANY)
    whole = lambda a: pl.BlockSpec(a.shape, lambda g: (0,) * a.ndim, pipeline_mode=one)
    fixed = lambda shape: pl.BlockSpec(shape, lambda g: (0,) * len(shape))
    qs = pl.BlockSpec((None, BLK, GROUP), lambda g: (slot(g, first), 2, 0))
    os = pl.BlockSpec((None, BLK, GROUP), lambda g: (g, 2, 0))
    outs = [(block, bf16), (block, bf16), (small, f32), (small, f32), ((BLK, d), bf16), ((BLK, d), bf16)]
    outs.append((early_part, bf16))
    return pl.pallas_call(
        last_kernel,
        grid=(groups,),
        in_specs=[qs, qs, qs, os, os, os]
        + [
            pl.BlockSpec((heads, BLK, BLK), lambda g: (g * 3 + 2, 0, 0)),
            whole(cos),
            whole(sin),
            pl.BlockSpec((3, GROUP, d), lambda g: (0, g, 0)),
            pl.BlockSpec((d, BLK), lambda g: (0, 2), pipeline_mode=one),
            pl.BlockSpec((None, d, 3 * GROUP), lambda g: (g, 0, 0)),
            pl.BlockSpec((None, 1, 3 * GROUP), lambda g: (g, 0, 0)),
            pl.BlockSpec((None, BLK, GROUP), lambda g: (g, 0, 0)),
            whole(part),
            hbm,
            whole(gain),
            hbm,
            whole(small_w),
            whole(small_two),
            whole(g_bup),
            whole(early),
        ],
        out_specs=[fixed(shape) for shape, _ in outs],
        out_shape=[jax.ShapeDtypeStruct(*spec) for spec in outs],
        scratch_shapes=[
            pltpu.VMEM((2, BLK, BLK), f32),
            pltpu.VMEM((BLK, GROUP), f32),
            pltpu.VMEM((BLK, GROUP), f32),
            pltpu.VMEM((BLK, d), f32),
            pltpu.VMEM((groups, 1, 3 * GROUP), f32),
            pltpu.VMEM((4, 2, 2, *block), bf16),
            pltpu.VMEM((BLK, d), bf16),
            pltpu.VMEM((BLK, d), bf16),
            pltpu.VMEM((BLK, d), f32),
            pltpu.VMEM(early_part, bf16),
            pltpu.VMEM(early_part, bf16),
            pltpu.VMEM((4, 2, *block), bf16),
            pltpu.VMEM((4, 2, *block), bf16),
            pltpu.VMEM((4, *block), bf16),
            pltpu.VMEM((4, *block), bf16),
            pltpu.VMEM((3, *block), bf16),
            pltpu.VMEM(block, bf16),
            pltpu.VMEM(block, bf16),
            pltpu.VMEM((BLK, d), bf16),
            pltpu.VMEM((BLK, d), bf16),
            pltpu.VMEM(small, f32),
            pltpu.VMEM(small, f32),
            pltpu.VMEM(small, f32),
            pltpu.VMEM(small, f32),
            pltpu.VMEM(small, f32),
            pltpu.VMEM(small, f32),
            pltpu.VMEM((4, *small), f32),
            pltpu.VMEM(small, f32),
            pltpu.SemaphoreType.DMA((copies,)),
            pltpu.SemaphoreType.DMA((copies,)),
            pltpu.SemaphoreType.DMA((2,)),
        ],
        compiler_params=pltpu.CompilerParams(
            vmem_limit_bytes=VMEM_LIMIT, collective_id=0, has_side_effects=True
        ),
        cost_estimate=pl.CostEstimate(flops=30_000_000_000, bytes_accessed=100_000_000, transcendentals=0),
        name="last",
    )(q, k, v, do, o, inverse, expo, cos, sin, w, hidden_t, g_sum, gb_sum, dq_far, part, tokens, gain, mid,
      small_w, small_two, g_bup, early)


def finish_kernel(x_ref, gain, mid_ref, own_ref, part_ref, out_ref, small):
    out, first, second = finish_rows(
        x_ref[...], wide(gain), mid_ref[...], own_ref[...] + part_ref[...].astype(f32)
    )
    out_ref[...] = out
    small[...] = jnp.concatenate([lines(first), lines(second)], 0)


def finish(x, gain, mid, own, part):
    d = x.shape[1]
    return pl.pallas_call(
        finish_kernel,
        out_shape=[jax.ShapeDtypeStruct(x.shape, bf16), jax.ShapeDtypeStruct((2 * d // GROUP, GROUP), f32)],
        compiler_params=pltpu.CompilerParams(vmem_limit_bytes=VMEM_LIMIT),
        name="finish",
    )(x, gain, mid, own, part)


def place_pieces(sc, first, pieces, out_ref, sem):
    copies = []
    for n, piece in enumerate(pieces):
        start = pl.multiple_of(sc[first + n] * BLK, BLK)
        copies.append(pltpu.make_async_copy(piece, out_ref.at[pl.ds(start, piece.shape[0]), :], sem.at[n]))
        copies[-1].start()
    return copies


def assemble_kernel(count, sc, *rest):
    for made in place_pieces(sc, 0, rest[:count], rest[count], rest[-1]):
        made.wait()


def assemble(places, pieces, rows):
    count = len(pieces)
    return pl.pallas_call(
        functools.partial(assemble_kernel, count),
        grid_spec=pltpu.PrefetchScalarGridSpec(
            num_scalar_prefetch=1,
            grid=(1,),
            in_specs=[pl.BlockSpec(p.shape, lambda i, s: (0, 0)) for p in pieces],
            out_specs=pl.BlockSpec(memory_space=pl.ANY),
            scratch_shapes=[pltpu.SemaphoreType.DMA((count,))],
        ),
        out_shape=jax.ShapeDtypeStruct((rows, pieces[0].shape[1]), pieces[0].dtype),
        compiler_params=pltpu.CompilerParams(vmem_limit_bytes=VMEM_LIMIT),
        cost_estimate=pl.CostEstimate(flops=0, bytes_accessed=8_000_000, transcendentals=0),
        name="assemble",
    )(places, *pieces)


def one_line(v):
    return jnp.concatenate([v[j : j + 1] for j in range(v.shape[0])], 1)


def conclude_kernel(
    share, half, hidden, sc, late, late_theirs, early, early_theirs, small, small_theirs, p0, p1, p2, p3,
    g_qkv, g_up, g_down, g_out, g_bqkv, g_bup, grad, *rest,
):
    vectors, sem = rest[:-1], rest[-1]
    copies = place_pieces(sc, 0, (p0, p1, p2, p3), grad, sem)
    groups = late.shape[0]
    d = groups * GROUP
    whole = half // GROUP
    for s in range(3):
        rows = slice(s * share, (s + 1) * share)
        mine = [late[g].astype(f32)[rows] for g in range(whole + 1)]
        other = [late_theirs[g].astype(f32)[rows] for g in range(whole, groups)]
        g_qkv[s] = jnp.concatenate(mine, 1)[:, :half] + jnp.concatenate(other, 1)[:, half - whole * GROUP :]
    width = 256
    for c in range(hidden // width):
        mine = early[:, 2 * c * width : 2 * (c + 1) * width].astype(f32)
        other = early_theirs[:share, 2 * c * width : 2 * (c + 1) * width].astype(f32)
        both = mine + other
        cols = slice(c * width, (c + 1) * width)
        g_up[:, cols] = both[:, :width]
        g_down[:, cols] = both[:, width:]
    mine = early[:, 4 * hidden : 4 * hidden + d].astype(f32)
    other = early_theirs[:share, 2 * hidden : 2 * hidden + d].astype(f32)
    g_out[...] = mine[:, :half] + other[:, half:]
    per = d // GROUP
    for n, ref in enumerate(vectors):
        ref[...] = one_line(small[n * per : (n + 1) * per] + small_theirs[n * per : (n + 1) * per])[0]
    base = 6 * per
    for s in range(3):
        rows = slice(base + s * per, base + (s + 1) * per)
        g_bqkv[s : s + 1, :] = one_line(small[rows])[:, :half] + one_line(small_theirs[rows])[:, half:]
    base += 3 * per
    count = hidden // GROUP
    g_bup[...] = one_line(small[base : base + count] + small_theirs[base + count : base + 2 * count])[0]
    for made in copies:
        made.wait()


def conclude(share, half, hidden, places, args, pieces, rows):
    d = 2 * half
    vmem = pl.BlockSpec(memory_space=pltpu.VMEM)
    return pl.pallas_call(
        functools.partial(conclude_kernel, share, half, hidden),
        in_specs=[pl.BlockSpec(memory_space=pltpu.SMEM)] + [vmem] * (len(args) + len(pieces)),
        out_specs=[vmem] * 6 + [pl.BlockSpec(memory_space=pl.ANY)] + [vmem] * 6,
        out_shape=[
            jax.ShapeDtypeStruct((3, share, half), f32),
            jax.ShapeDtypeStruct((share, hidden), f32),
            jax.ShapeDtypeStruct((share, hidden), f32),
            jax.ShapeDtypeStruct((share, half), f32),
            jax.ShapeDtypeStruct((3, half), f32),
            jax.ShapeDtypeStruct((hidden,), f32),
            jax.ShapeDtypeStruct((rows, d), bf16),
        ]
        + [jax.ShapeDtypeStruct((d,), f32)] * 6,
        scratch_shapes=[pltpu.SemaphoreType.DMA((len(pieces),))],
        compiler_params=pltpu.CompilerParams(vmem_limit_bytes=VMEM_LIMIT),
        cost_estimate=pl.CostEstimate(flops=1_000_000, bytes_accessed=12_000_000, transcendentals=0),
        name="conclude",
    )(places, *args, *pieces)


def on_device(
    tokens, lengths, gain_one, shift_one, w_qkv, b_qkv, w_out, b_out, gain_two, shift_two, w_up, b_up, w_down, b_down,
    cotangent,
):
    d = tokens.shape[1]
    n_dp = lax.axis_size("dp")
    here = lax.axis_index("dp")
    mp = lax.axis_index("mp")
    swap = [(0, 1), (1, 0)]
    half = w_qkv.shape[2]
    hidden = w_up.shape[1]

    long = (lengths[0] == LONG).astype(jnp.int32)
    plain, weights = np.zeros((2, 14), np.int32), np.zeros((2, 14, 6), np.int32)
    plain[0, BLOCK : BLOCK + 4], plain[1, BLOCK : BLOCK + 4] = [0, 1, 2, 3], [4, 5, 3, 2]
    plain[0, PLACE : PLACE + 3], plain[1, PLACE : PLACE + 3] = [0, 1, 2], [1, 2, 0]
    for n, (side, late) in enumerate(((0, 3), (4, 2))):
        weights[n, [FLAG, FLAG + 1, TABLE + 1], side] = 1
        weights[n, [FLAG + 2, TABLE + late], 2] = 1
    pick = lambda a, b: jnp.where(mp == 0, jnp.asarray(a, jnp.int32), jnp.asarray(b, jnp.int32))
    sc = pick(*plain) + jnp.sum(pick(*weights) * long[None], 1)

    def other(own):
        share = own.shape[0] // n_dp
        piece = lax.dynamic_slice_in_dim(own, here * share, share, 0)
        return lax.all_gather(lax.ppermute(piece, "mp", swap), "dp", tiled=True)

    groups = d // GROUP
    first = half // GROUP
    share = d // n_dp
    by_hand = n_dp == 16
    tables = tuple(jnp.asarray(t) for t in rope_tables())
    w_own = jnp.transpose(w_qkv, (0, 2, 1))
    down_other = other(w_down)
    biases = lax.ppermute(jnp.concatenate([b_qkv.reshape(-1), b_up]), "mp", swap)
    w_partner = lax.ppermute(w_own, "mp", swap)
    *qkv, hidden_one, hidden_t = project(
        sc, tokens, gain_one, shift_one, w_own, b_qkv.astype(f32), *tables, 0, first, groups
    )
    hidden_one, w_up_sent, w_out_sent = lax.optimization_barrier((hidden_one, w_up, w_out))
    w_out_other = lax.ppermute(w_out_sent, "mp", swap)
    up_other = lax.ppermute(w_up_sent, "mp", swap)
    b_qkv_all = jnp.concatenate([b_qkv, biases[: 3 * half].reshape(3, half)], 1).astype(f32)
    b_up_all = jnp.concatenate([b_up, biases[3 * half :]]).astype(f32)[None]
    w_all = jnp.concatenate([w_own, w_partner], 1)
    attended = attend(sc, *qkv, 0, first)
    qkv = project(
        sc, hidden_one, gain_one, shift_one, w_all, b_qkv_all, *tables, first, groups - first, groups, qkv, attended[:1]
    )
    attended = attend(sc, *qkv, first, groups - first, attended)
    out_own, grad_mid, do, g_early, g_bup, small_two = middle(
        sc, tokens, cotangent, attended[0], w_out, w_out_other, b_out, gain_two, shift_two,
        w_up, up_other, b_up_all, w_down, down_other, b_down,
    )
    early = lax.psum_scatter(g_early, "dp", scatter_dimension=0, tiled=True)

    theirs = lax.ppermute(out_own, "mp", swap)
    out_tokens = assemble(jnp.stack([3 * mp, 3 - 3 * mp]), [out_own, theirs], 6 * BLK)
    args = (sc, *qkv, do, *attended, *tables, w_all, hidden_t, first)
    g_sum, gb_sum, grad_whole, small_w = back("whole", *args, (tokens, gain_one, grad_mid))
    whole_theirs = lax.ppermute(grad_whole, "mp", swap)
    g_sum, gb_sum, dq_far, part = back("far", *args, (g_sum, gb_sum))
    used = 4 * hidden
    if by_hand:
        part, out_tokens, whole_theirs, early = lax.optimization_barrier((part, out_tokens, whole_theirs, early))
        near_tables = [lax.dynamic_slice_in_dim(t, sc[TABLE + 2] * BLK, BLK, 0) for t in tables]
        late, late_theirs, small, small_theirs, shared, shared_theirs, early_theirs = last(
            *args[1:8], *near_tables, *args[10:], g_sum, gb_sum, dq_far, part, tokens, gain_one, grad_mid,
            small_w, small_two, g_bup, early,
        )
    else:
        arrived = lax.ppermute(part, "mp", swap)
        g_qkv, g_bqkv, own = back("near", *args, (g_sum, gb_sum, dq_far))
        x_shared = lax.dynamic_slice_in_dim(tokens, sc[BLOCK + 2] * BLK, BLK, 0)
        shared, last_sums = finish(x_shared, gain_one, grad_mid[2 * BLK :], own, arrived)
        g_bqkv = g_bqkv.reshape(groups, 3, GROUP).transpose(1, 0, 2)
        small = jnp.concatenate(
            [
                small_w[:2].reshape(-1, GROUP) + last_sums,
                small_two[:4].reshape(-1, GROUP),
                g_bqkv.reshape(-1, GROUP),
                g_bup.reshape(-1, GROUP),
            ]
        )
        n_small = small.shape[0]
        shared_theirs = lax.ppermute(shared, "mp", swap)
        g_qkv = g_qkv.reshape(groups, d, 3, GROUP).transpose(2, 1, 0, 3).reshape(3, d, d)
        late = lax.psum_scatter(g_qkv, "dp", scatter_dimension=1, tiled=True)
        late_theirs = lax.ppermute(late, "mp", swap)
        small = lax.psum(small, "dp")
        small_theirs = lax.ppermute(small, "mp", swap)
        early_theirs = lax.ppermute(early[:, 2 * hidden :], "mp", swap)
    places = pick([0, 2, 3, 4], [4, 3, 2, 0])
    pieces = [grad_whole, shared, shared_theirs, whole_theirs]

    if by_hand:
        g_w, g_up, g_down, g_out, g_bq, g_bu, grad_tokens, *vectors = conclude(
            share, half, hidden, places,
            (late, late_theirs, early, early_theirs, small, small_theirs), pieces, 6 * BLK,
        )
        g_down, g_out = g_down.T, g_out.T
    else:
        grad_tokens = assemble(places, pieces, 6 * BLK)
        mlp = early[:, : 2 * hidden].astype(f32) + early_theirs[:, : 2 * hidden].astype(f32)
        mlp = mlp.reshape(share, hidden // 256, 2, 256)
        g_up = mlp[:, :, 0].reshape(share, hidden)
        g_down = mlp[:, :, 1].reshape(share, hidden).T
        g_out = early[:, used : used + half].astype(f32)
        g_out = (g_out + early_theirs[:, 2 * hidden + half : 2 * hidden + d].astype(f32)).T
        g_w = late[:, :, :half].astype(f32) + late_theirs[:, :, half:].astype(f32)
        mine, others = small[:n_small].reshape(-1), small_theirs[:n_small].reshape(-1)
        vectors = list((mine[: 6 * d] + others[: 6 * d]).reshape(6, d))
        pair = lambda v, lo, n, w: v[lo : lo + 2 * n * w].reshape(n, 2, w)
        g_bq = pair(mine, 6 * d, 3, half)[:, 0] + pair(others, 6 * d, 3, half)[:, 1]
        g_bu = pair(mine, 9 * d, 1, hidden)[0, 0] + pair(others, 9 * d, 1, hidden)[0, 1]
    return (
        out_tokens,
        grad_tokens,
        vectors[0],
        vectors[1],
        g_w,
        g_bq,
        g_out,
        vectors[4],
        vectors[2],
        vectors[3],
        g_up,
        g_bu,
        g_down,
        vectors[5],
    )


def solution(mesh):
    in_specs = (
        P("dp", None),
        P("dp", None),
        P(),
        P(),
        P(None, None, "mp"),
        P(None, "mp"),
        P("mp", None),
        P(),
        P(),
        P(),
        P(None, "mp"),
        P("mp"),
        P("mp", None),
        P(),
        P("dp", None),
    )
    out_specs = (
        P("dp", None),
        P("dp", None),
        P(),
        P(),
        P(None, "dp", "mp"),
        P(None, "mp"),
        P("mp", "dp"),
        P(),
        P(),
        P(),
        P("dp", "mp"),
        P("mp"),
        P("mp", "dp"),
        P(),
    )
    return jax.shard_map(on_device, mesh=mesh, in_specs=in_specs, out_specs=out_specs, check_vma=False)
```

```python
import functools

import jax
import jax.numpy as jnp
import numpy as np
from jax import lax
from jax.experimental import pallas as pl
from jax.experimental.pallas import tpu as pltpu
from jax.sharding import PartitionSpec as P

HD = 32
LONG = 1024
BLK = 512
GROUP = 128
epsilon = 1e-05
rotary_base = 10000.0
log2_e = 1.4426950408889634
ln_2 = 0.6931471805599453

f32 = jnp.float32
bf16 = jnp.bfloat16
NT = (((1,), (1,)), ((), ()))
NN = (((1,), (0,)), ((), ()))
TN = (((0,), (0,)), ((), ()))
VMEM_LIMIT = 60 << 20


def dot(a, b, dims=NN):
    return lax.dot_general(a, b, dims, preferred_element_type=f32)


def rope_tables():
    place = np.arange(LONG, dtype=np.float64)[:, None]
    frequency = rotary_base ** (-np.arange(HD // 2, dtype=np.float64) * 2.0 / HD)
    angles = place * frequency[None, :]
    cosines = np.concatenate([np.cos(angles), np.cos(angles)], 1)
    sines = np.concatenate([-np.sin(angles), np.sin(angles)], 1)
    repeat = GROUP // HD
    return (
        np.tile(cosines, (1, repeat)).astype(np.float32),
        np.tile(sines, (1, repeat)).astype(np.float32),
    )


def swap_halves(x):
    lane = lax.broadcasted_iota(jnp.int32, (1, GROUP), 1)
    low = (lane // (HD // 2)) % 2 == 0
    return jnp.where(low, pltpu.roll(x, GROUP - HD // 2, 1), pltpu.roll(x, HD // 2, 1))


def rotate(x, cosines, sines):
    return x * cosines + swap_halves(x) * sines


def rotate_back(x, cosines, sines):
    return x * cosines - swap_halves(x) * sines


def normalize(values):
    centred = values - jnp.mean(values, -1, keepdims=True)
    inverse = lax.rsqrt(jnp.mean(centred * centred, -1, keepdims=True) + epsilon)
    return (centred * inverse, inverse)


def normalize_back(normed, inverse, grad_normed):
    mean_grad = jnp.mean(grad_normed, -1, keepdims=True)
    mean_proj = jnp.mean(grad_normed * normed, -1, keepdims=True)
    return inverse * (grad_normed - mean_grad - normed * mean_proj)


FLAG, BLOCK, TABLE, PLACE = 0, 3, 7, 11


def wide(ref):
    return ref[...].astype(f32)[None]


def attend_body(q, k_ref, v_ref, o_ref, l_ref, e_ref, store, bias):
    lane = lax.broadcasted_iota(jnp.int32, (1, GROUP), 1) // HD
    heads = GROUP // HD
    count = k_ref.shape[0]
    chunks = count // BLK
    values_t = v_ref[...].T
    ones = jnp.ones((16, count), bf16)
    outs, inverses = [], []

    def score(h, c):
        keys = k_ref[c * BLK : (c + 1) * BLK, :]
        scores = dot(jnp.where(lane == h, keys, jnp.zeros_like(keys)), q, NT)
        store[h % 2, c * BLK : (c + 1) * BLK, :] = scores
        return jnp.max(scores.reshape(BLK // 8, 8, BLK), axis=0) + bias[c]

    def score_max(h, c, so_far):
        found = score(h, c)
        return found if so_far is None else jnp.maximum(so_far, found)

    top = None
    for c in range(chunks):
        top = score_max(0, c, top)
    row_max = jnp.max(top, axis=0, keepdims=True)
    for h in range(heads):
        top = None
        total = None
        stacked = jnp.concatenate([values_t[HD * h : HD * (h + 1)], ones], 0)
        for c in range(chunks):
            if h + 1 < heads:
                top = score_max(h + 1, c, top)
            rows = slice(c * BLK, (c + 1) * BLK)
            expo = jnp.exp2(store[h % 2, rows, :] - (row_max - bias[c])).astype(bf16)
            e_ref[h, rows, :] = expo
            part = dot(stacked[:, rows], expo)
            total = part if total is None else total + part
        inverse = 1.0 / total[HD : HD + 1]
        outs.append(total[:HD] * inverse)
        inverses.append(jnp.broadcast_to(inverse, (HD, BLK)))
        if h + 1 < heads:
            row_max = jnp.max(top, axis=0, keepdims=True)
    o_ref[...] = jnp.concatenate(outs, 0).T.astype(bf16)
    l_ref[...] = jnp.concatenate(inverses, 0).T


CHUNK_BIAS, CHOICE = 0, 6


def front_kernel(
    first, ctl, gain, shift, b_own, b_up, cos, sin, w_own, tokens, w_out, w_up, w_down,
    o_ref, l_ref, e_ref, q_out, k_out, v_out, ht_out, w_all, out_other, up_other, down_other, b_all,
    store, x_all, hidden, q_all, k_all, v_all, ht, w_in, b_mine, b_in, local, send, recv,
):
    g, b = pl.program_id(0), pl.program_id(1)
    step = 3 * g + b
    here = lax.axis_index("dp")
    mp = lax.axis_index("mp")
    c = here % 2
    x = (here // 2) % 2
    core = (here + 1 - 2 * c, mp)
    side = (here + 2 - 4 * x, mp)
    across = (here, 1 - mp)
    groups = q_all.shape[0]
    half = w_own.shape[1]
    numbers = {}

    def copy(name, src, dst, dev):
        n = numbers.setdefault(name, len(numbers))
        return pltpu.make_async_remote_copy(
            src_ref=src,
            dst_ref=dst,
            send_sem=send.at[n],
            recv_sem=recv.at[n],
            device_id=dev,
            device_id_type=pl.DeviceIdType.MESH,
        )

    def quarter(ref, n):
        size = ref.shape[0] // 4
        return ref.at[pl.ds(pl.multiple_of(n * size, size), size), :]

    share = half // 2
    mine = pl.ds(pl.multiple_of(c * share, share), share)
    w_across = copy("w", w_own.at[:, mine, :], w_in.at[:, mine, :], across)
    w_core = copy("wc", w_in.at[:, mine, :], w_in.at[:, mine, :], core)
    b_across = copy("b", b_mine, b_in, across)
    out_across = copy("o", w_out, out_other, across)
    n_mine, n_side = 2 * x + c, 2 * (1 - x) + c
    pairs = ((w_up, up_other), (w_down, down_other))
    by_across = [copy(("y", n), quarter(a, n_mine), quarter(to, n_mine), across) for n, (a, to) in enumerate(pairs)]
    by_side = [copy(("x", n), quarter(to, n_mine), quarter(to, n_mine), side) for n, (_, to) in enumerate(pairs)]
    by_core = [
        copy(("c", n, m), quarter(to, at), quarter(to, at), core)
        for n, (_, to) in enumerate(pairs)
        for m, at in enumerate((n_mine, n_side))
    ]
    block = lambda at, count: pl.ds(pl.multiple_of(at * BLK, BLK), count * BLK)
    x_copies = [
        pltpu.make_async_copy(tokens.at[block(at, count), :], x_all.at[to * BLK : (to + count) * BLK, :], local.at[n])
        for n, (at, to, count) in enumerate(((4 * mp, 0, 2), (2 + mp, 2, 1), (3 - mp, 3, 1)))
    ]
    w_copies = [
        pltpu.make_async_copy(w_own, w_all.at[:, :half, :], local.at[3]),
        pltpu.make_async_copy(w_in, w_all.at[:, half:, :], local.at[4]),
    ]
    ht_copy = pltpu.make_async_copy(ht, ht_out, local.at[5])

    def qkv_copies(lo, hi, n):
        return [
            pltpu.make_async_copy(a.at[lo:hi], out.at[lo:hi], local.at[n + m])
            for m, (a, out) in enumerate(((q_all, q_out), (k_all, k_out), (v_all, v_out)))
        ]

    early, late = qkv_copies(0, first, 6), qkv_copies(first, groups, 9)

    def project(w, bias, lo, hi):
        count = hi - lo
        for i in range(4):
            rows = slice(i * BLK, (i + 1) * BLK)
            out = dot(hidden[rows, :], w, NT)
            chosen = ctl[CHOICE + i : CHOICE + i + 1, :GROUP] > 0.5
            cosines = jnp.where(chosen, cos[BLK:, :], cos[:BLK, :])
            sines = jnp.where(chosen, sin[BLK:, :], sin[:BLK, :])
            for s in range(3):
                for n in range(count):
                    at = (s * count + n) * GROUP
                    part = out[:, at : at + GROUP] + bias[s : s + 1, n * GROUP : (n + 1) * GROUP]
                    if s == 0:
                        part = rotate(part, cosines, sines) * (HD ** (-0.5) * log2_e)
                        q_all[lo + n, rows, :] = part.astype(bf16)
                    elif s == 1:
                        k_all[lo + n, rows, :] = rotate(part, cosines, sines).astype(bf16)
                    else:
                        v_all[lo + n, rows, :] = part.astype(bf16)

    @pl.when(step == 0)
    def _():
        for made in x_copies:
            made.start()
        b_mine[...] = jnp.zeros_like(b_mine)
        b_mine[:3, :half] = b_own[...].astype(f32)
        b_mine[3:4, :] = wide(b_up)
        barrier = pltpu.get_barrier_semaphore()
        for dev in (across, core, side):
            pl.semaphore_signal(barrier, inc=1, device_id=dev, device_id_type=pl.DeviceIdType.MESH)
        pl.semaphore_wait(barrier, 3)
        w_across.start()
        b_across.start()
        for made in x_copies:
            made.wait()
        for i in range(4):
            rows = slice(i * BLK, (i + 1) * BLK)
            normed, _ = normalize(x_all[rows, :].astype(f32))
            fresh = (normed * wide(gain) + wide(shift)).astype(bf16)
            hidden[rows, :] = fresh
            ht[:, rows] = fresh.T
        ht_copy.start()
        w_copies[0].start()
        w = jnp.concatenate([w_own[s, : first * GROUP, :] for s in range(3)], 0)
        project(w, b_mine[:3, : first * GROUP], 0, first)
        for made in early:
            made.start()

    @pl.when(step == 2)
    def _():
        by_across[0].start()

    @pl.when(step == 3)
    def _():
        w_across.wait()
        w_core.start()
        b_across.wait()
        by_across[1].start()

    @pl.when(step == 3 * first)
    def _():
        w_core.wait()
        w_copies[1].start()
        tail = first * GROUP
        w = jnp.concatenate([part for s in range(3) for part in (w_own[s, tail:, :], w_in[s])], 0)
        bias = jnp.concatenate([b_mine[:3, tail:half], b_in[:3, :half]], 1)
        project(w, bias, first, groups)
        for made in late:
            made.start()
        by_across[0].wait()
        by_side[0].start()

    @pl.when(step == 3 * first + 1)
    def _():
        by_across[1].wait()
        by_side[1].start()

    @pl.when(step == 3 * first + 2)
    def _():
        out_across.start()

    @pl.when(step == 3 * first + 6)
    def _():
        by_side[0].wait()
        for made in by_core[:2]:
            made.start()

    @pl.when(step == 3 * groups - 1)
    def _():
        by_side[1].wait()
        for made in by_core[2:]:
            made.start()

    keys = pl.ds(pl.multiple_of(b // 2 * LONG, LONG), LONG)
    q = q_all[g, pl.ds(pl.multiple_of(b * BLK, BLK), BLK), :]
    bias = [ctl[pl.ds(CHUNK_BIAS + 2 * b + n, 1), :] for n in range(2)]
    @pl.when(b != 2)
    def _():
        attend_body(q, k_all.at[g, keys, :], v_all.at[g, keys, :], o_ref, l_ref, e_ref, store, bias)

    @pl.when(b == 2)
    def _():
        attend_body(q, k_all.at[g, keys, :], v_all.at[g, keys, :], o_ref, l_ref, e_ref, store, bias)

    @pl.when(step == 3 * groups - 1)
    def _():
        b_all[:, : b_mine.shape[1]] = b_mine[3:4, :]
        b_all[:, b_mine.shape[1] :] = b_in[3:4, :]
        out_across.wait()
        for made in by_core:
            made.wait()
        for made in (*early, *late, *w_copies, ht_copy):
            made.wait()


def front(ctl, gain, shift, b_own, b_up, cos, sin, w_own, tokens, w_out, w_up, w_down):
    d = tokens.shape[1]
    groups = d // GROUP
    heads = GROUP // HD
    half = w_own.shape[1]
    own, rows = 3 * BLK, 4 * BLK
    one = pl.Buffered(buffer_count=1)
    whole = lambda a: pl.BlockSpec(a.shape, lambda g, b: (0,) * a.ndim, pipeline_mode=one)
    os = pl.BlockSpec((None, BLK, GROUP), lambda g, b: (g, b, 0))
    es = pl.BlockSpec((heads, LONG, BLK), lambda g, b: (g * 3 + b, 0, 0))
    hbm = pl.BlockSpec(memory_space=pl.ANY)
    held = jax.ShapeDtypeStruct((groups, rows, GROUP), bf16)
    copies = 2 + 2 + 2 + 2 + 4
    return pl.pallas_call(
        functools.partial(front_kernel, half // GROUP),
        grid=(groups, 3),
        in_specs=[whole(a) for a in (ctl, gain, shift, b_own, b_up, cos, sin, w_own)] + [hbm] * 4,
        out_specs=[os, os, es] + [hbm] * 8 + [pl.BlockSpec((1, 2 * b_up.shape[0]), lambda g, b: (0, 0))],
        out_shape=[
            jax.ShapeDtypeStruct((groups, own, GROUP), bf16),
            jax.ShapeDtypeStruct((groups, own, GROUP), f32),
            jax.ShapeDtypeStruct((groups * 3 * heads, LONG, BLK), bf16),
            held,
            held,
            held,
            jax.ShapeDtypeStruct((d, rows), bf16),
            jax.ShapeDtypeStruct((3, 2 * half, d), bf16),
            jax.ShapeDtypeStruct(w_out.shape, bf16),
            jax.ShapeDtypeStruct(w_up.shape, bf16),
            jax.ShapeDtypeStruct(w_down.shape, bf16),
            jax.ShapeDtypeStruct((1, 2 * b_up.shape[0]), f32),
        ],
        scratch_shapes=[
            pltpu.VMEM((2, LONG, BLK), f32),
            pltpu.VMEM((rows, d), bf16),
            pltpu.VMEM((rows, d), bf16),
            pltpu.VMEM((groups, rows, GROUP), bf16),
            pltpu.VMEM((groups, rows, GROUP), bf16),
            pltpu.VMEM((groups, rows, GROUP), bf16),
            pltpu.VMEM((d, rows), bf16),
            pltpu.VMEM(w_own.shape, bf16),
            pltpu.VMEM((8, b_up.shape[0]), f32),
            pltpu.VMEM((8, b_up.shape[0]), f32),
            pltpu.SemaphoreType.DMA((12,)),
            pltpu.SemaphoreType.DMA((copies,)),
            pltpu.SemaphoreType.DMA((copies,)),
        ],
        compiler_params=pltpu.CompilerParams(
            vmem_limit_bytes=VMEM_LIMIT, collective_id=1, has_side_effects=True
        ),
        cost_estimate=pl.CostEstimate(
            flops=50_000_000_000, bytes_accessed=100_000_000, transcendentals=31_000_000
        ),
        name="front",
    )(ctl, gain, shift, b_own, b_up, cos, sin, w_own, tokens, w_out, w_up, w_down)


def attend_back_body(
    q_ref, k_ref, v_ref, do_ref, o_ref, l_ref, e_ref, prod, dk_sum, dv_sum, start, count
):
    lane = lax.broadcasted_iota(jnp.int32, (1, GROUP), 1) // HD
    heads = GROUP // HD
    q = q_ref[...]
    do = (do_ref[...].astype(f32) * l_ref[...]).astype(bf16)
    both = do.astype(f32) * o_ref[...].astype(f32)
    upper = both.astype(bf16)
    lower = (both - upper.astype(f32)).astype(bf16)
    pick = (
        lax.broadcasted_iota(jnp.int32, (8, GROUP), 0)
        == lax.broadcasted_iota(jnp.int32, (8, GROUP), 1) // HD
    )
    pick = pick.astype(f32).astype(bf16)
    delta = dot(pick, upper, NT) + dot(pick, lower, NT)
    keys_t = k_ref[pl.ds(start, count), :].T
    chunks = count // BLK
    tiles = [(h, c) for h in range(heads) for c in range(chunks)]

    def grad_probs(i):
        h, c = tiles[i]
        values = v_ref[pl.ds(start + c * BLK, BLK), :]
        prod[i % 2] = dot(jnp.where(lane == h, values, jnp.zeros_like(values)), do, NT)

    grad_probs(0)
    dq_t = [None] * heads
    for i, (h, c) in enumerate(tiles):
        if i + 1 < len(tiles):
            grad_probs(i + 1)
        rows = pl.ds(start + c * BLK, BLK)
        expo = e_ref[h, rows, :]
        ds = (expo.astype(f32) * (prod[i % 2] - delta[h : h + 1])).astype(bf16)
        dv_sum[rows, :] += dot(expo, jnp.where(lane == h, do, jnp.zeros_like(do)))
        dk_sum[rows, :] += dot(ds, jnp.where(lane == h, q, jnp.zeros_like(q)))
        part = dot(keys_t[HD * h : HD * (h + 1), c * BLK : (c + 1) * BLK], ds)
        dq_t[h] = part if dq_t[h] is None else dq_t[h] + part
    return jnp.concatenate(dq_t, 0).T


def window_back(dq, dk_sum, dv_sum, tables, w_ref, ht_ref, dh_sum):
    parts = [] if dq is None else [dq]
    dk = dk_sum[...] * ln_2
    rotated = []
    for n, (cos, sin) in enumerate(tables):
        rotated.append(rotate_back(dk[n * BLK : (n + 1) * BLK], cos[...], sin[...]))
    parts.append(jnp.concatenate(rotated, 0).astype(bf16))
    parts.append(dv_sum[...].astype(bf16))
    both = jnp.concatenate(parts, 1)
    w = jnp.concatenate([w_ref[s] for s in range(3 - len(parts), 3)], 0)
    for n in range(len(tables)):
        rows = slice(n * BLK, (n + 1) * BLK)
        dh_sum[rows, :] += dot(both[rows], w)
    return dot(ht_ref[...], both), jnp.sum(both.astype(f32), 0, keepdims=True)


def back_kernel(
    mode, sc, q_ref, k_ref, v_ref, do_ref, o_ref, l_ref, e_ref, cos, sin, cos0, sin0, cos1, sin1, w_ref, ht_ref,
    *rest,
):
    g = pl.program_id(0)
    last_g = pl.num_programs(0) - 1
    step = pl.program_id(1)
    if mode == "whole":
        x_ref, gain, mid_ref, g_ref, gb_ref, out_ref, small, dq_cat, prod, dk_sum, dv_sum, dh_sum = rest
    elif mode == "far":
        before, before_b, g_ref, gb_ref, dq_out, part_ref, prod, dk_sum, dv_sum, dh_sum = rest
    else:
        before, before_b, dq_in, g_ref, gb_ref, own_ref, prod, dk_sum, dv_sum, dh_sum = rest
    refs = (q_ref, k_ref, v_ref, do_ref, o_ref, l_ref, e_ref, prod, dk_sum, dv_sum)
    own_tables = (cos0, sin0), (cos1, sin1)
    finish_q = lambda dq: rotate_back(dq * (HD ** (-0.5)), cos[...], sin[...]).astype(bf16)

    @pl.when(step == 0)
    def _():
        dk_sum[...] = jnp.zeros_like(dk_sum)
        dv_sum[...] = jnp.zeros_like(dv_sum)

    @pl.when((step == 0) & (g == 0))
    def _():
        dh_sum[...] = jnp.zeros_like(dh_sum)

    if mode == "whole":
        place = pl.ds(pl.multiple_of(step * BLK, BLK), BLK)

        @pl.when(sc[FLAG] == 1)
        def _():
            dq_cat[place, :] = finish_q(attend_back_body(*refs, 0, LONG))

        @pl.when(sc[FLAG] == 0)
        def _():
            dq_cat[place, :] = finish_q(attend_back_body(*refs, pl.multiple_of(step * BLK, BLK), BLK))

        @pl.when(step == 1)
        def _():
            g_ref[...], gb_ref[...] = window_back(
                dq_cat[...], dk_sum, dv_sum, own_tables, w_ref, ht_ref, dh_sum
            )

        @pl.when((step == 1) & (g == last_g))
        def _():
            sums = [None, None]
            for rows in (slice(0, BLK), slice(BLK, LONG)):
                out, *terms = finish_rows(x_ref[rows, :], wide(gain), mid_ref[rows, :], dh_sum[rows, :])
                out_ref[rows, :] = out
                for n, term in enumerate(terms):
                    sums[n] = term if sums[n] is None else sums[n] + term
            small[...] = jnp.concatenate(sums + [jnp.zeros_like(sums[0])] * 6, 0)

    elif mode == "far":

        @pl.when(sc[FLAG + 2] == 1)
        def _():
            dq_out[...] = attend_back_body(*refs, 0, BLK)

        @pl.when(sc[FLAG + 2] == 0)
        def _():
            dq_out[...] = jnp.zeros_like(dq_out)

        weight, bias = window_back(None, dk_sum, dv_sum, own_tables[:1], w_ref, ht_ref, dh_sum)
        g_ref[:, :GROUP] = before[:, :GROUP]
        g_ref[:, GROUP:] = before[:, GROUP:] + weight
        gb_ref[:, :GROUP] = before_b[:, :GROUP]
        gb_ref[:, GROUP:] = before_b[:, GROUP:] + bias

        @pl.when(g == last_g)
        def _():
            part_ref[...] = dh_sum[...].astype(bf16)

    else:
        dq = finish_q(attend_back_body(*refs, 0, BLK) + dq_in[...])
        weight, bias = window_back(dq, dk_sum, dv_sum, own_tables[:1], w_ref, ht_ref, dh_sum)
        weight = weight + before[...]
        gb_ref[...] = bias + before_b[...]
        g_ref[...] = weight.astype(bf16)

        @pl.when(g == last_g)
        def _():
            own_ref[...] = dh_sum[...]


def back(mode, sc, q, k, v, do, o, inverse, expo, cos, sin, w, hidden_t, more):
    groups = o.shape[0]
    d = w.shape[2]
    heads = GROUP // HD
    blocks = 2 if mode == "whole" else 1
    query = 0 if mode == "whole" else 2
    key = {"whole": 0, "far": 3, "near": 2}[mode]
    keys = LONG if mode == "whole" else BLK
    one = pl.Buffered(buffer_count=1)
    qs = pl.BlockSpec((None, BLK, GROUP), lambda g, b, s: (g, b + query, 0))
    ks = pl.BlockSpec((None, keys, GROUP), lambda g, b, s: (g, key, 0))
    os = pl.BlockSpec((None, BLK, GROUP), lambda g, b, s: (g, b + query, 0))
    es = pl.BlockSpec((heads, keys, BLK), lambda g, b, s: (g * 3 + b + query, 1 if mode == "far" else 0, 0))
    tq = pl.BlockSpec((BLK, GROUP), lambda g, b, s: (s[TABLE + b + query], 0))
    t0 = pl.BlockSpec((BLK, GROUP), lambda g, b, s: (s[TABLE + key], 0))
    t1 = pl.BlockSpec((BLK, GROUP), lambda g, b, s: (s[TABLE + key + (blocks - 1)], 0))
    weight = pl.BlockSpec((None, d, 3 * GROUP), lambda g, b, s: (g, 0, 0))
    bias = pl.BlockSpec((None, 1, 3 * GROUP), lambda g, b, s: (g, 0, 0))
    dq_part = pl.BlockSpec((None, BLK, GROUP), lambda g, b, s: (g, 0, 0))
    whole = lambda *shape: pl.BlockSpec(shape, lambda g, b, s: (0, 0))
    in_specs = [qs, ks, ks, os, os, os, es, tq, tq, t0, t0, t1, t1]
    in_specs += [
        pl.BlockSpec((3, GROUP, d), lambda g, b, s: (0, g, 0)),
        pl.BlockSpec((d, keys), lambda g, b, s: (0, key), pipeline_mode=one),
    ]
    bias_shape = jax.ShapeDtypeStruct((groups, 1, 3 * GROUP), f32)
    scratch = [
        pltpu.VMEM((2, BLK, BLK), f32),
        pltpu.VMEM((keys, GROUP), f32),
        pltpu.VMEM((keys, GROUP), f32),
        pltpu.VMEM((keys, d), f32),
    ]
    if mode == "whole":
        in_specs += [
            pl.BlockSpec((LONG, d), lambda g, b, s: (s[BLOCK] // 2, 0), pipeline_mode=one),
            pl.BlockSpec((d,), lambda g, b, s: (0,)),
            pl.BlockSpec((LONG, d), lambda g, b, s: (0, 0), pipeline_mode=one),
        ]
        out_specs = [weight, bias, whole(LONG, d), whole(8, d)]
        out_shape = [
            jax.ShapeDtypeStruct((groups, d, 3 * GROUP), f32),
            bias_shape,
            jax.ShapeDtypeStruct((LONG, d), bf16),
            jax.ShapeDtypeStruct((8, d), f32),
        ]
        scratch = [pltpu.VMEM((LONG, GROUP), bf16)] + scratch
    elif mode == "far":
        in_specs += [weight, bias]
        out_specs = [weight, bias, dq_part, whole(BLK, d)]
        out_shape = [
            jax.ShapeDtypeStruct((groups, d, 3 * GROUP), f32),
            bias_shape,
            jax.ShapeDtypeStruct((groups, BLK, GROUP), f32),
            jax.ShapeDtypeStruct((BLK, d), bf16),
        ]
    else:
        in_specs += [weight, bias, dq_part]
        out_specs = [weight, bias, whole(BLK, d)]
        out_shape = [
            jax.ShapeDtypeStruct((groups, d, 3 * GROUP), bf16),
            bias_shape,
            jax.ShapeDtypeStruct((BLK, d), f32),
        ]
    return pl.pallas_call(
        functools.partial(back_kernel, mode),
        grid_spec=pltpu.PrefetchScalarGridSpec(
            num_scalar_prefetch=1,
            grid=(groups, blocks),
            in_specs=in_specs,
            out_specs=out_specs,
            scratch_shapes=scratch,
        ),
        out_shape=out_shape,
        compiler_params=pltpu.CompilerParams(vmem_limit_bytes=VMEM_LIMIT),
        cost_estimate=pl.CostEstimate(
            flops=groups * blocks * keys * 5_000_000, bytes_accessed=groups * blocks * 6_000_000, transcendentals=0
        ),
        name="back_" + mode,
    )(sc, q, k, v, do, o, inverse, expo, cos, sin, cos, sin, cos, sin, w, hidden_t, *more)


def gelu_parts(z):
    density = jnp.exp2(z * z * (-0.5 * log2_e)) * 0.3989422804014327
    t = 1.0 / (1.0 + 0.2316419 * jnp.abs(z))
    poly = t * (
        0.319381530
        + t * (-0.356563782 + t * (1.781477937 + t * (-1.821255978 + t * 1.330274429)))
    )
    tail = density * poly
    cdf = jnp.where(z >= 0, 1.0 - tail, tail)
    return z * cdf, cdf + z * density


def middle_kernel(
    sc, x0, x1, x2, y0, y1, y2, o_ref, w_out_own, w_out_other, b_out, gain, shift,
    up_a, up_b, up_c, up_d, b_up, down_a, down_b, down_c, down_d, b_down,
    out_ref, mid_ref, do_ref, g_ref, g_out, g_bup, g_small,
    w_out, r1, h2, h2t, dy, dyt, acc, back,
):
    i = pl.program_id(0)
    last = pl.num_programs(0) - 1
    xs, ys = (x0, x1, x2), (y0, y1, y2)
    blocks = [slice(j * BLK, (j + 1) * BLK) for j in range(3)]
    groups = o_ref.shape[0]
    heads_of = lambda rows: jnp.concatenate([o_ref[g, rows, :] for g in range(groups)], 1)

    @pl.when(i == 0)
    def _():
        w_out[: w_out_own.shape[0], :] = w_out_own[...]
        w_out[w_out_own.shape[0] :, :] = w_out_other[...]
        for j, rows in enumerate(blocks):
            mixed = dot(heads_of(rows), w_out[...]) + wide(b_out) + xs[j][...].astype(f32)
            r1[rows, :] = mixed
            normed, _ = normalize(mixed)
            hidden = (normed * wide(gain) + wide(shift)).astype(bf16)
            h2[rows, :] = hidden
            h2t[:, rows] = hidden.T
            dy[rows, :] = ys[j][...]
            dyt[:, rows] = ys[j][...].T
            acc[rows, :] = jnp.zeros_like(mixed)
            back[rows, :] = jnp.zeros_like(mixed)

    @pl.when(i < last)
    def _():
        first, second = 2 * i < last, 2 * i + 1 < last
        w_up = jnp.concatenate(
            [jnp.where(first, up_a[...], up_c[...]), jnp.where(second, up_b[...], up_d[...])], 1
        )
        w_down = jnp.concatenate(
            [jnp.where(first, down_a[...], down_c[...]), jnp.where(second, down_b[...], down_d[...])], 0
        )
        bias = b_up[...]
        width = up_a.shape[1]
        total = dy.shape[0]
        parts = [slice(j, j + 256) for j in range(0, total, BLK // 2)]
        count = len(parts)
        actives, grads = [None] * count, [None] * count
        ups, downs = [None] * count, [None] * count
        col_sum = None

        def ahead(j):
            ups[j] = dot(h2[parts[j], :], w_up) + bias
            downs[j] = dot(dy[parts[j], :], w_down, NT)

        ahead(0)
        for j, rows in enumerate(parts):
            if j + 1 < count:
                ahead(j + 1)
            active, slope = gelu_parts(ups[j])
            actives[j] = active.astype(bf16)
            grads[j] = (downs[j] * slope).astype(bf16)
            s = jnp.sum(grads[j].astype(f32), 0, keepdims=True)
            col_sum = s if col_sum is None else col_sum + s
            acc[rows, :] += dot(actives[j], w_down)
            back[rows, :] += dot(grads[j], w_up, NT)
        g_bup[...] = col_sum
        g_up = dot(h2t[...], jnp.concatenate(grads, 0)).astype(bf16)
        g_down = dot(dyt[...], jnp.concatenate(actives, 0)).astype(bf16)
        for n in range(2):
            cols = slice(n * width, (n + 1) * width)
            g_ref[:, 2 * n * width : (2 * n + 1) * width] = g_up[:, cols]
            g_ref[:, (2 * n + 1) * width : (2 * n + 2) * width] = g_down[:, cols]

    @pl.when(i == last)
    def _():
        sums = [None] * 4
        lows = []
        for j, rows in enumerate(blocks):
            mixed = r1[rows, :]
            place = pl.multiple_of(sc[PLACE + j] * BLK, BLK)
            out_ref[pl.ds(place, BLK), :] = (acc[rows, :] + wide(b_down) + mixed).astype(bf16)
            normed, inverse = normalize(mixed)
            top = dy[rows, :].astype(f32)
            dh = back[rows, :]
            dr = top + normalize_back(normed, inverse, dh * wide(gain))
            mid_ref[rows, :] = dr
            low = dr.astype(bf16)
            lows.append(low)
            do = dot(low, w_out[...], NT).astype(bf16)
            for g in range(groups):
                do_ref[g, rows, :] = do[:, g * GROUP : (g + 1) * GROUP]
            for n, term in enumerate((dh * normed, dh, dr, top)):
                s = jnp.sum(term, 0, keepdims=True)
                sums[n] = s if sums[n] is None else sums[n] + s
        g_out[...] = dot(jnp.concatenate(lows, 0).T, heads_of(slice(0, 3 * BLK))).astype(bf16)
        g_small[...] = jnp.concatenate(sums + [jnp.zeros_like(sums[0])] * 4, 0)


def middle(sc, tokens, cotangent, o, w_out_own, w_out_other, b_out, gain, shift, up_own, down_own, up_other, down_other, b_up, b_down):
    d = tokens.shape[1]
    groups = o.shape[0]
    own = 3 * BLK
    half = up_own.shape[1]
    piece = 256
    per = half // piece
    steps = per + 1
    one = pl.Buffered(buffer_count=1)
    whole = lambda *shape: pl.BlockSpec(shape, lambda i, s: (0,) * len(shape), pipeline_mode=one)
    rows_of = lambda j: pl.BlockSpec((BLK, d), lambda i, s: (s[BLOCK + j], 0), pipeline_mode=one)
    fixed = lambda *shape: pl.BlockSpec(shape, lambda i, s: (0,) * len(shape))
    at = lambda i: jnp.minimum(i, per - 1)
    places = [
        lambda i: jnp.minimum(2 * i, per - 1),
        lambda i: jnp.minimum(2 * i + 1, per - 1),
        lambda i: jnp.clip(2 * i - per, 0, per - 1),
        lambda i: jnp.clip(2 * i + 1 - per, 0, per - 1),
    ]
    ups = [pl.BlockSpec((d, piece), functools.partial(lambda p, i, s: (0, p(i)), p)) for p in places]
    downs = [pl.BlockSpec((piece, d), functools.partial(lambda p, i, s: (p(i), 0), p)) for p in places]
    return pl.pallas_call(
        middle_kernel,
        grid_spec=pltpu.PrefetchScalarGridSpec(
            num_scalar_prefetch=1,
            grid=(steps,),
            in_specs=[rows_of(0), rows_of(1), rows_of(2)] * 2
            + [
                whole(groups, own, GROUP),
                whole(*w_out_own.shape),
                whole(*w_out_other.shape),
                whole(d),
                whole(d),
                whole(d),
                *ups,
                pl.BlockSpec((1, 2 * piece), lambda i, s: (0, at(i))),
                *downs,
                whole(d),
            ],
            out_specs=[
                fixed(own, d),
                fixed(own, d),
                fixed(groups, own, GROUP),
                pl.BlockSpec((d, 4 * piece), lambda i, s: (0, at(i))),
                fixed(d, d),
                pl.BlockSpec((1, 2 * piece), lambda i, s: (0, at(i))),
                fixed(8, d),
            ],
            scratch_shapes=[
                pltpu.VMEM((d, d), bf16),
                pltpu.VMEM((own, d), f32),
                pltpu.VMEM((own, d), bf16),
                pltpu.VMEM((d, own), bf16),
                pltpu.VMEM((own, d), bf16),
                pltpu.VMEM((d, own), bf16),
                pltpu.VMEM((own, d), f32),
                pltpu.VMEM((own, d), f32),
            ],
        ),
        out_shape=[
            jax.ShapeDtypeStruct((own, d), bf16),
            jax.ShapeDtypeStruct((own, d), f32),
            jax.ShapeDtypeStruct((groups, own, GROUP), bf16),
            jax.ShapeDtypeStruct((d, 4 * half), bf16),
            jax.ShapeDtypeStruct((d, d), bf16),
            jax.ShapeDtypeStruct((1, 2 * half), f32),
            jax.ShapeDtypeStruct((8, d), f32),
        ],
        compiler_params=pltpu.CompilerParams(vmem_limit_bytes=VMEM_LIMIT),
        cost_estimate=pl.CostEstimate(
            flops=2 * own * d * (3 * d + 12 * half), bytes_accessed=40_000_000, transcendentals=8_000_000
        ),
        name="middle",
    )(sc, tokens, tokens, tokens, cotangent, cotangent, cotangent, o, w_out_own, w_out_other, b_out, gain, shift,
      *[up_own] * 2, *[up_other] * 2, b_up, *[down_own] * 2, *[down_other] * 2, b_down)


def finish_rows(x, gain, mid, dh):
    normed, inverse = normalize(x.astype(f32))
    out = (mid + normalize_back(normed, inverse, dh * gain)).astype(bf16)
    return out, jnp.sum(dh * normed, 0, keepdims=True), jnp.sum(dh, 0, keepdims=True)


def lines(v):
    return jnp.concatenate([v[:, j * GROUP : (j + 1) * GROUP] for j in range(v.shape[1] // GROUP)], 0)


def last_kernel(
    q_ref, k_ref, v_ref, do_ref, o_ref, l_ref, e_ref, cos, sin, w_ref, ht_ref, before, before_b, dq_in, gout_ref,
    part_ref, tokens, gain, mid, small_w, small_two, gup_ref, early_ref,
    sum_out, theirs_out, small_out, small_theirs_out, rows_out, rows_theirs_out, early_out,
    prod, dk_sum, dv_sum, dh_sum, gb_sum, g_all, part_in, x_ref, mid_ref, early_part, early_in,
    r1, a1, r2, a2, r3, sums, theirs, rows_ref, rows_in, s0, s1, s2, s3, q1, q2, q3, q4, send, recv, local,
):
    g = pl.program_id(0)
    groups = g_all.shape[3]
    here = lax.axis_index("dp")
    mp = lax.axis_index("mp")
    c = here % 2
    x = (here // 2) % 2
    z = here // 4
    core = (here + 1 - 2 * c, mp)
    side = (here + 2 - 4 * x, mp)
    across = (here, 1 - mp)
    line = [((z + n) % 4, ((z + n) % 4 * 4 + here % 4, mp)) for n in (1, 2, 3)]

    numbers = {}

    def copy(name, src, dst, dev):
        n = numbers.setdefault(name, len(numbers))
        return pltpu.make_async_remote_copy(
            src_ref=src,
            dst_ref=dst,
            send_sem=send.at[n],
            recv_sem=recv.at[n],
            device_id=dev,
            device_id_type=pl.DeviceIdType.MESH,
        )

    part_copy = copy("part", part_ref, part_in, across)
    early_copy = copy("early", early_part, early_in, across)
    rows_copy = copy("rows", rows_ref, rows_in, across)
    by_core = [copy(("c", n), g_all.at[:, :, 1 - c, n], r1.at[:, :, n], core) for n in range(groups)]
    by_side = [copy(("x", n), a1.at[:, 1 - x, n], r2.at[:, n], side) for n in range(groups)]
    by_line = [
        [copy(("z", n, m), a2.at[at, n], r3.at[m, n], dev) for m, (at, dev) in enumerate(line)]
        for n in range(groups)
    ]
    by_across = [copy(("y", n), sums.at[n], theirs.at[n], across) for n in range(groups)]
    small_core = copy("sc", s0, q1, core)
    small_side = copy("sx", s1, q2, side)
    small_line = [copy(("sz", m), s2, q3.at[z], dev) for m, (_, dev) in enumerate(line)]
    small_across = copy("sy", s3, q4, across)
    rows = pl.ds(pl.multiple_of((2 + mp) * BLK, BLK), BLK)
    x_copy = pltpu.make_async_copy(tokens.at[rows, :], x_ref, local.at[0])
    mid_copy = pltpu.make_async_copy(mid.at[2 * BLK : 3 * BLK, :], mid_ref, local.at[1])

    @pl.when(g == 0)
    def _():
        barrier = pltpu.get_barrier_semaphore()
        partners = [core, side, across] + [dev for _, dev in line]
        for dev in partners:
            pl.semaphore_signal(barrier, inc=1, device_id=dev, device_id_type=pl.DeviceIdType.MESH)
        pl.semaphore_wait(barrier, len(partners))
        part_copy.start()
        x_copy.start()
        mid_copy.start()
        dh_sum[...] = jnp.zeros_like(dh_sum)
        share, width = early_ref.shape[0], early_part.shape[1]
        start = gup_ref.shape[1]
        early_part[share:, :] = jnp.zeros((early_part.shape[0] - share, width), bf16)
        early_part[:share, :] = early_ref[:, start : start + width]
        early_copy.start()

    dk_sum[...] = jnp.zeros_like(dk_sum)
    dv_sum[...] = jnp.zeros_like(dv_sum)
    refs = (q_ref, k_ref, v_ref, do_ref, o_ref, l_ref, e_ref, prod, dk_sum, dv_sum)
    dq = (attend_back_body(*refs, 0, BLK) + dq_in[...]) * (HD ** (-0.5))
    dq = rotate_back(dq, cos[...], sin[...]).astype(bf16)
    weight, bias = window_back(dq, dk_sum, dv_sum, ((cos, sin),), w_ref, ht_ref, dh_sum)
    weight = weight + before[...]
    gb_sum[g] = bias + before_b[...]
    share = early_ref.shape[0]
    held_rows = 4 * share
    fill = jnp.zeros((g_all.shape[4] - held_rows, GROUP), f32)
    weight = jnp.concatenate([weight, gout_ref[...].astype(f32)], 1)
    for n in range(16):
        part = weight[n * share : (n + 1) * share]
        pieces = [part[:, s * GROUP : (s + 1) * GROUP] for s in range(4)]
        pieces = pieces + [fill] if fill.shape[0] else pieces
        g_all[n // 4, n // 2 % 2, n % 2, g] = jnp.concatenate(pieces, 0).astype(bf16)

    def second(n):
        by_core[n].wait()
        a1[:, :, n] = (g_all[:, :, c, n].astype(f32) + r1[:, :, n].astype(f32)).astype(bf16)
        by_side[n].start()

    def third(n):
        by_side[n].wait()
        a2[:, n] = (a1[:, x, n].astype(f32) + r2[:, n].astype(f32)).astype(bf16)
        for made in by_line[n]:
            made.start()

    def fourth(n):
        for made in by_line[n]:
            made.wait()
        total = a2[z, n].astype(f32)
        for m in range(3):
            total = total + r3[m, n].astype(f32)
        sums[n] = total.astype(bf16)
        by_across[n].start()

    for n in range(groups):

        @pl.when(g == n)
        def _(n=n):
            by_core[n].start()
            if n == groups - 1:
                return
            for late, stage in ((1, second), (2, third), (3, fourth)):
                if n >= late:
                    stage(n - late)

    @pl.when(g == groups - 1)
    def _():
        x_copy.wait()
        mid_copy.wait()
        part_copy.wait()
        out, one, two = finish_rows(x_ref[...], wide(gain), mid_ref[...], dh_sum[...] + part_in[...].astype(f32))
        rows_ref[...] = out
        rows_copy.start()
        n = groups - 1
        second(n - 1)
        third(n - 2)
        held = [lines(small_w[0:1, :] + one), lines(small_w[1:2, :] + two)]
        held += [lines(small_two[m : m + 1, :]) for m in range(4)]
        held += [gb_sum[m, :, s * GROUP : (s + 1) * GROUP] for s in range(3) for m in range(groups)]
        held.append(lines(gup_ref[...]))
        held = jnp.concatenate(held, 0)
        s0[...] = jnp.concatenate([held, jnp.zeros((s0.shape[0] - held.shape[0], GROUP), f32)], 0)
        small_core.start()
        second(n)
        fourth(n - 3)
        third(n - 1)
        small_core.wait()
        s1[...] = s0[...] + q1[...]
        small_side.start()
        fourth(n - 2)
        third(n)
        small_side.wait()
        s2[...] = s1[...] + q2[...]
        for made in small_line:
            made.start()
        fourth(n - 1)
        for made in small_line:
            made.wait()
        q3[z] = s2[...]
        s3[...] = (q3[0] + q3[1]) + (q3[2] + q3[3])
        small_across.start()
        fourth(n)
        early_copy.wait()
        early_out[...] = early_in[...]
        small_out[...] = s3[...]
        sum_out[...] = sums[...]
        rows_out[...] = rows_ref[...]
        rows_copy.wait()
        rows_theirs_out[...] = rows_in[...]
        small_across.wait()
        small_theirs_out[...] = q4[...]
        for made in by_across:
            made.wait()
        theirs_out[...] = theirs[...]


def last(q, k, v, do, o, inverse, expo, cos, sin, w, hidden_t, g_sum, gb_sum, dq_far, g_out, part, tokens, gain, mid,
         small_w, small_two, g_bup, early):
    groups = o.shape[0]
    d = w.shape[2]
    heads = GROUP // HD
    share = early.shape[0]
    held = -(-4 * share // 16) * 16
    block = (groups, held, GROUP)
    count = 6 * d // GROUP + groups * 3 + g_bup.shape[1] // GROUP
    small = (-(-count // 8) * 8, GROUP)
    early_part = (-(-share // 16) * 16, g_bup.shape[1])
    copies = 3 + 6 * groups + 6
    one = pl.Buffered(buffer_count=1)
    hbm = pl.BlockSpec(memory_space=pl.ANY)
    whole = lambda a: pl.BlockSpec(a.shape, lambda g: (0,) * a.ndim, pipeline_mode=one)
    fixed = lambda shape: pl.BlockSpec(shape, lambda g: (0,) * len(shape))
    qs = pl.BlockSpec((None, BLK, GROUP), lambda g: (g, 2, 0))
    os = pl.BlockSpec((None, BLK, GROUP), lambda g: (g, 2, 0))
    outs = [(block, bf16), (block, bf16), (small, f32), (small, f32), ((BLK, d), bf16), ((BLK, d), bf16)]
    outs.append((early_part, bf16))
    return pl.pallas_call(
        last_kernel,
        grid=(groups,),
        in_specs=[qs, qs, qs, os, os, os]
        + [
            pl.BlockSpec((heads, BLK, BLK), lambda g: (g * 3 + 2, 0, 0)),
            whole(cos),
            whole(sin),
            pl.BlockSpec((3, GROUP, d), lambda g: (0, g, 0)),
            pl.BlockSpec((d, BLK), lambda g: (0, 2), pipeline_mode=one),
            pl.BlockSpec((None, d, 3 * GROUP), lambda g: (g, 0, 0)),
            pl.BlockSpec((None, 1, 3 * GROUP), lambda g: (g, 0, 0)),
            pl.BlockSpec((None, BLK, GROUP), lambda g: (g, 0, 0)),
            pl.BlockSpec((d, GROUP), lambda g: (0, g)),
            whole(part),
            hbm,
            whole(gain),
            hbm,
            whole(small_w),
            whole(small_two),
            whole(g_bup),
            whole(early),
        ],
        out_specs=[fixed(shape) for shape, _ in outs],
        out_shape=[jax.ShapeDtypeStruct(*spec) for spec in outs],
        scratch_shapes=[
            pltpu.VMEM((2, BLK, BLK), f32),
            pltpu.VMEM((BLK, GROUP), f32),
            pltpu.VMEM((BLK, GROUP), f32),
            pltpu.VMEM((BLK, d), f32),
            pltpu.VMEM((groups, 1, 3 * GROUP), f32),
            pltpu.VMEM((4, 2, 2, *block), bf16),
            pltpu.VMEM((BLK, d), bf16),
            pltpu.VMEM((BLK, d), bf16),
            pltpu.VMEM((BLK, d), f32),
            pltpu.VMEM(early_part, bf16),
            pltpu.VMEM(early_part, bf16),
            pltpu.VMEM((4, 2, *block), bf16),
            pltpu.VMEM((4, 2, *block), bf16),
            pltpu.VMEM((4, *block), bf16),
            pltpu.VMEM((4, *block), bf16),
            pltpu.VMEM((3, *block), bf16),
            pltpu.VMEM(block, bf16),
            pltpu.VMEM(block, bf16),
            pltpu.VMEM((BLK, d), bf16),
            pltpu.VMEM((BLK, d), bf16),
            pltpu.VMEM(small, f32),
            pltpu.VMEM(small, f32),
            pltpu.VMEM(small, f32),
            pltpu.VMEM(small, f32),
            pltpu.VMEM(small, f32),
            pltpu.VMEM(small, f32),
            pltpu.VMEM((4, *small), f32),
            pltpu.VMEM(small, f32),
            pltpu.SemaphoreType.DMA((copies,)),
            pltpu.SemaphoreType.DMA((copies,)),
            pltpu.SemaphoreType.DMA((2,)),
        ],
        compiler_params=pltpu.CompilerParams(
            vmem_limit_bytes=VMEM_LIMIT, collective_id=0, has_side_effects=True
        ),
        cost_estimate=pl.CostEstimate(flops=30_000_000_000, bytes_accessed=100_000_000, transcendentals=0),
        name="last",
    )(q, k, v, do, o, inverse, expo, cos, sin, w, hidden_t, g_sum, gb_sum, dq_far, g_out, part, tokens, gain, mid,
      small_w, small_two, g_bup, early)


def finish_kernel(x_ref, gain, mid_ref, own_ref, part_ref, out_ref, small):
    out, first, second = finish_rows(
        x_ref[...], wide(gain), mid_ref[...], own_ref[...] + part_ref[...].astype(f32)
    )
    out_ref[...] = out
    small[...] = jnp.concatenate([lines(first), lines(second)], 0)


def finish(x, gain, mid, own, part):
    d = x.shape[1]
    return pl.pallas_call(
        finish_kernel,
        out_shape=[jax.ShapeDtypeStruct(x.shape, bf16), jax.ShapeDtypeStruct((2 * d // GROUP, GROUP), f32)],
        compiler_params=pltpu.CompilerParams(vmem_limit_bytes=VMEM_LIMIT),
        name="finish",
    )(x, gain, mid, own, part)


def place_pieces(sc, first, pieces, out_ref, sem):
    copies = []
    for n, piece in enumerate(pieces):
        start = pl.multiple_of(sc[first + n] * BLK, BLK)
        copies.append(pltpu.make_async_copy(piece, out_ref.at[pl.ds(start, piece.shape[0]), :], sem.at[n]))
        copies[-1].start()
    return copies


def assemble_kernel(count, sc, *rest):
    for made in place_pieces(sc, 0, rest[:count], rest[count], rest[-1]):
        made.wait()


def assemble(places, pieces, rows):
    count = len(pieces)
    return pl.pallas_call(
        functools.partial(assemble_kernel, count),
        grid_spec=pltpu.PrefetchScalarGridSpec(
            num_scalar_prefetch=1,
            grid=(1,),
            in_specs=[pl.BlockSpec(p.shape, lambda i, s: (0, 0)) for p in pieces],
            out_specs=pl.BlockSpec(memory_space=pl.ANY),
            scratch_shapes=[pltpu.SemaphoreType.DMA((count,))],
        ),
        out_shape=jax.ShapeDtypeStruct((rows, pieces[0].shape[1]), pieces[0].dtype),
        compiler_params=pltpu.CompilerParams(vmem_limit_bytes=VMEM_LIMIT),
        cost_estimate=pl.CostEstimate(flops=0, bytes_accessed=8_000_000, transcendentals=0),
        name="assemble",
    )(places, *pieces)


def one_line(v):
    return jnp.concatenate([v[j : j + 1] for j in range(v.shape[0])], 1)


def conclude_kernel(
    share, half, hidden, sc, late, late_theirs, early, early_theirs, small, small_theirs, p0, p1, p2, p3,
    g_qkv, g_up, g_down, g_out, g_bqkv, g_bup, grad, *rest,
):
    vectors, sem = rest[:-1], rest[-1]
    copies = place_pieces(sc, 0, (p0, p1, p2, p3), grad, sem)
    groups = late.shape[0]
    d = groups * GROUP
    whole = half // GROUP
    for s in range(4):
        rows = slice(s * share, (s + 1) * share)
        mine = [late[g].astype(f32)[rows] for g in range(whole + 1)]
        other = [late_theirs[g].astype(f32)[rows] for g in range(whole, groups)]
        both = jnp.concatenate(mine, 1)[:, :half] + jnp.concatenate(other, 1)[:, half - whole * GROUP :]
        if s < 3:
            g_qkv[s] = both
        else:
            g_out[...] = both
    width = 256
    for c in range(hidden // width):
        mine = early[:, 2 * c * width : 2 * (c + 1) * width].astype(f32)
        other = early_theirs[:share, 2 * c * width : 2 * (c + 1) * width].astype(f32)
        both = mine + other
        cols = slice(c * width, (c + 1) * width)
        g_up[:, cols] = both[:, :width]
        g_down[:, cols] = both[:, width:]
    per = d // GROUP
    for n, ref in enumerate(vectors):
        ref[...] = one_line(small[n * per : (n + 1) * per] + small_theirs[n * per : (n + 1) * per])[0]
    base = 6 * per
    for s in range(3):
        rows = slice(base + s * per, base + (s + 1) * per)
        g_bqkv[s : s + 1, :] = one_line(small[rows])[:, :half] + one_line(small_theirs[rows])[:, half:]
    base += 3 * per
    count = hidden // GROUP
    g_bup[...] = one_line(small[base : base + count] + small_theirs[base + count : base + 2 * count])[0]
    for made in copies:
        made.wait()


def conclude(share, half, hidden, places, args, pieces, rows):
    d = 2 * half
    vmem = pl.BlockSpec(memory_space=pltpu.VMEM)
    return pl.pallas_call(
        functools.partial(conclude_kernel, share, half, hidden),
        in_specs=[pl.BlockSpec(memory_space=pltpu.SMEM)] + [vmem] * (len(args) + len(pieces)),
        out_specs=[vmem] * 6 + [pl.BlockSpec(memory_space=pl.ANY)] + [vmem] * 6,
        out_shape=[
            jax.ShapeDtypeStruct((3, share, half), f32),
            jax.ShapeDtypeStruct((share, hidden), f32),
            jax.ShapeDtypeStruct((share, hidden), f32),
            jax.ShapeDtypeStruct((share, half), f32),
            jax.ShapeDtypeStruct((3, half), f32),
            jax.ShapeDtypeStruct((hidden,), f32),
            jax.ShapeDtypeStruct((rows, d), bf16),
        ]
        + [jax.ShapeDtypeStruct((d,), f32)] * 6,
        scratch_shapes=[pltpu.SemaphoreType.DMA((len(pieces),))],
        compiler_params=pltpu.CompilerParams(vmem_limit_bytes=VMEM_LIMIT),
        cost_estimate=pl.CostEstimate(flops=1_000_000, bytes_accessed=12_000_000, transcendentals=0),
        name="conclude",
    )(places, *args, *pieces)


def on_device(
    tokens, lengths, gain_one, shift_one, w_qkv, b_qkv, w_out, b_out, gain_two, shift_two, w_up, b_up, w_down, b_down,
    cotangent,
):
    d = tokens.shape[1]
    n_dp = lax.axis_size("dp")
    here = lax.axis_index("dp")
    mp = lax.axis_index("mp")
    swap = [(0, 1), (1, 0)]
    half = w_qkv.shape[2]
    hidden = w_up.shape[1]

    long = (lengths[0] == LONG).astype(jnp.int32)
    plain, weights = np.zeros((2, 14), np.int32), np.zeros((2, 14, 6), np.int32)
    plain[0, BLOCK : BLOCK + 4], plain[1, BLOCK : BLOCK + 4] = [0, 1, 2, 3], [4, 5, 3, 2]
    plain[0, PLACE : PLACE + 3], plain[1, PLACE : PLACE + 3] = [0, 1, 2], [1, 2, 0]
    for n, (side, late) in enumerate(((0, 3), (4, 2))):
        weights[n, [FLAG, FLAG + 1, TABLE + 1], side] = 1
        weights[n, [FLAG + 2, TABLE + late], 2] = 1
    pick = lambda a, b: jnp.where(mp == 0, jnp.asarray(a, jnp.int32), jnp.asarray(b, jnp.int32))
    sc = pick(*plain) + jnp.sum(pick(*weights) * long[None], 1)

    groups = d // GROUP
    share = d // n_dp
    by_hand = n_dp == 16
    tables = tuple(jnp.asarray(t) for t in rope_tables())
    plain, weights = np.zeros((2, 16), np.float32), np.zeros((2, 16, 6), np.float32)
    for n, (side, late) in enumerate(((0, 3), (4, 2))):
        for row, window in ((1, side), (2, side), (5, 2)):
            plain[n, CHUNK_BIAS + row], weights[n, CHUNK_BIAS + row, window] = -1e30, 1e30
        weights[n, CHOICE + 1, side] = 1
        weights[n, CHOICE + late, 2] = 1
    choose = lambda a: jnp.where(mp == 0, jnp.asarray(a[0]), jnp.asarray(a[1]))
    ctl = choose(plain) + jnp.sum(choose(weights) * long[None].astype(f32), 1)
    ctl = jnp.broadcast_to(ctl[:, None], (16, BLK))

    *attended, q, k, v, hidden_t, w_all, w_out_other, up_other, down_other, b_up_all = front(
        ctl, gain_one, shift_one, b_qkv, b_up, *tables, jnp.transpose(w_qkv, (0, 2, 1)), tokens, w_out, w_up, w_down
    )
    qkv = (q, k, v)
    out_own, grad_mid, do, g_early, g_out, g_bup, small_two = middle(
        sc, tokens, cotangent, attended[0], w_out, w_out_other, b_out, gain_two, shift_two,
        w_up, w_down, up_other, down_other, b_up_all, b_down,
    )
    early = lax.psum_scatter(g_early, "dp", scatter_dimension=0, tiled=True)

    theirs = lax.ppermute(out_own, "mp", swap)
    out_tokens = assemble(jnp.stack([3 * mp, 3 - 3 * mp]), [out_own, theirs], 6 * BLK)
    args = (sc, *qkv, do, *attended, *tables, w_all, hidden_t)
    g_sum, gb_sum, grad_whole, small_w = back("whole", *args, (tokens, gain_one, grad_mid))
    whole_theirs = lax.ppermute(grad_whole, "mp", swap)
    g_sum, gb_sum, dq_far, part = back("far", *args, (g_sum, gb_sum))
    if by_hand:
        part, out_tokens, whole_theirs, early = lax.optimization_barrier((part, out_tokens, whole_theirs, early))
        near_tables = [lax.dynamic_slice_in_dim(t, sc[TABLE + 2] * BLK, BLK, 0) for t in tables]
        late, late_theirs, small, small_theirs, shared, shared_theirs, early_theirs = last(
            *args[1:8], *near_tables, *args[10:], g_sum, gb_sum, dq_far, g_out, part, tokens, gain_one, grad_mid,
            small_w, small_two, g_bup, early,
        )
    else:
        arrived = lax.ppermute(part, "mp", swap)
        g_qkv, g_bqkv, own = back("near", *args, (g_sum, gb_sum, dq_far))
        x_shared = lax.dynamic_slice_in_dim(tokens, sc[BLOCK + 2] * BLK, BLK, 0)
        shared, last_sums = finish(x_shared, gain_one, grad_mid[2 * BLK :], own, arrived)
        g_bqkv = g_bqkv.reshape(groups, 3, GROUP).transpose(1, 0, 2)
        small = jnp.concatenate(
            [
                small_w[:2].reshape(-1, GROUP) + last_sums,
                small_two[:4].reshape(-1, GROUP),
                g_bqkv.reshape(-1, GROUP),
                g_bup.reshape(-1, GROUP),
            ]
        )
        n_small = small.shape[0]
        shared_theirs = lax.ppermute(shared, "mp", swap)
        g_qkv = g_qkv.reshape(groups, d, 3, GROUP).transpose(2, 1, 0, 3).reshape(3, d, d)
        late = lax.psum_scatter(g_qkv, "dp", scatter_dimension=1, tiled=True)
        late_theirs = lax.ppermute(late, "mp", swap)
        small = lax.psum(small, "dp")
        small_theirs = lax.ppermute(small, "mp", swap)
        early_theirs = lax.ppermute(early[:, 2 * hidden :], "mp", swap)
    places = pick([0, 2, 3, 4], [4, 3, 2, 0])
    pieces = [grad_whole, shared, shared_theirs, whole_theirs]

    if by_hand:
        g_w, g_up, g_down, g_out, g_bq, g_bu, grad_tokens, *vectors = conclude(
            share, half, hidden, places,
            (late, late_theirs, early, early_theirs, small, small_theirs), pieces, 6 * BLK,
        )
        g_down, g_out = g_down.T, g_out.T
    else:
        grad_tokens = assemble(places, pieces, 6 * BLK)
        mlp = early[:, : 2 * hidden].astype(f32) + early_theirs[:, : 2 * hidden].astype(f32)
        mlp = mlp.reshape(share, hidden // 256, 2, 256)
        g_up = mlp[:, :, 0].reshape(share, hidden)
        g_down = mlp[:, :, 1].reshape(share, hidden).T
        g_out = lax.psum_scatter(g_out, "dp", scatter_dimension=0, tiled=True)
        out_theirs = lax.ppermute(g_out[:, half:], "mp", swap)
        g_out = (g_out[:, :half].astype(f32) + out_theirs.astype(f32)).T
        g_w = late[:, :, :half].astype(f32) + late_theirs[:, :, half:].astype(f32)
        mine, others = small[:n_small].reshape(-1), small_theirs[:n_small].reshape(-1)
        vectors = list((mine[: 6 * d] + others[: 6 * d]).reshape(6, d))
        pair = lambda v, lo, n, w: v[lo : lo + 2 * n * w].reshape(n, 2, w)
        g_bq = pair(mine, 6 * d, 3, half)[:, 0] + pair(others, 6 * d, 3, half)[:, 1]
        g_bu = pair(mine, 9 * d, 1, hidden)[0, 0] + pair(others, 9 * d, 1, hidden)[0, 1]
    return (
        out_tokens,
        grad_tokens,
        vectors[0],
        vectors[1],
        g_w,
        g_bq,
        g_out,
        vectors[4],
        vectors[2],
        vectors[3],
        g_up,
        g_bu,
        g_down,
        vectors[5],
    )


def solution(mesh):
    in_specs = (
        P("dp", None),
        P("dp", None),
        P(),
        P(),
        P(None, None, "mp"),
        P(None, "mp"),
        P("mp", None),
        P(),
        P(),
        P(),
        P(None, "mp"),
        P("mp"),
        P("mp", None),
        P(),
        P("dp", None),
    )
    out_specs = (
        P("dp", None),
        P("dp", None),
        P(),
        P(),
        P(None, "dp", "mp"),
        P(None, "mp"),
        P("mp", "dp"),
        P(),
        P(),
        P(),
        P("dp", "mp"),
        P("mp"),
        P("mp", "dp"),
        P(),
    )
    return jax.shard_map(on_device, mesh=mesh, in_specs=in_specs, out_specs=out_specs, check_vma=False)
```

```python
import functools

import jax
import jax.numpy as jnp
import numpy as np
from jax import lax
from jax.experimental import pallas as pl
from jax.experimental.pallas import tpu as pltpu
from jax.sharding import PartitionSpec as P

HD = 32
LONG = 1024
BLK = 512
GROUP = 128
epsilon = 1e-05
rotary_base = 10000.0
log2_e = 1.4426950408889634
ln_2 = 0.6931471805599453

f32 = jnp.float32
bf16 = jnp.bfloat16
NT = (((1,), (1,)), ((), ()))
NN = (((1,), (0,)), ((), ()))
TN = (((0,), (0,)), ((), ()))
VMEM_LIMIT = 60 << 20


def dot(a, b, dims=NN):
    return lax.dot_general(a, b, dims, preferred_element_type=f32)


def rope_tables():
    place = np.arange(LONG, dtype=np.float64)[:, None]
    frequency = rotary_base ** (-np.arange(HD // 2, dtype=np.float64) * 2.0 / HD)
    angles = place * frequency[None, :]
    cosines = np.concatenate([np.cos(angles), np.cos(angles)], 1)
    sines = np.concatenate([-np.sin(angles), np.sin(angles)], 1)
    repeat = GROUP // HD
    return (
        np.tile(cosines, (1, repeat)).astype(np.float32),
        np.tile(sines, (1, repeat)).astype(np.float32),
    )


def swap_halves(x):
    lane = lax.broadcasted_iota(jnp.int32, (1, GROUP), 1)
    low = (lane // (HD // 2)) % 2 == 0
    return jnp.where(low, pltpu.roll(x, GROUP - HD // 2, 1), pltpu.roll(x, HD // 2, 1))


def rotate(x, cosines, sines):
    return x * cosines + swap_halves(x) * sines


def rotate_back(x, cosines, sines):
    return x * cosines - swap_halves(x) * sines


def normalize(values):
    centred = values - jnp.mean(values, -1, keepdims=True)
    inverse = lax.rsqrt(jnp.mean(centred * centred, -1, keepdims=True) + epsilon)
    return (centred * inverse, inverse)


def normalize_back(normed, inverse, grad_normed):
    mean_grad = jnp.mean(grad_normed, -1, keepdims=True)
    mean_proj = jnp.mean(grad_normed * normed, -1, keepdims=True)
    return inverse * (grad_normed - mean_grad - normed * mean_proj)


FLAG, BLOCK, TABLE, PLACE = 0, 3, 7, 11


def wide(ref):
    return ref[...].astype(f32)[None]


def attend_body(q, k_ref, v_ref, o_ref, l_ref, e_ref, store, bias):
    lane = lax.broadcasted_iota(jnp.int32, (1, GROUP), 1) // HD
    heads = GROUP // HD
    count = k_ref.shape[0]
    chunks = count // BLK
    values_t = v_ref[...].T
    ones = jnp.ones((16, count), bf16)
    outs, inverses = [], []

    def score(h, c):
        keys = k_ref[c * BLK : (c + 1) * BLK, :]
        scores = dot(jnp.where(lane == h, keys, jnp.zeros_like(keys)), q, NT)
        store[h % 2, c * BLK : (c + 1) * BLK, :] = scores
        return jnp.max(scores.reshape(BLK // 8, 8, BLK), axis=0) + bias[c]

    def score_max(h, c, so_far):
        found = score(h, c)
        return found if so_far is None else jnp.maximum(so_far, found)

    top = None
    for c in range(chunks):
        top = score_max(0, c, top)
    row_max = jnp.max(top, axis=0, keepdims=True)
    for h in range(heads):
        top = None
        total = None
        stacked = jnp.concatenate([values_t[HD * h : HD * (h + 1)], ones], 0)
        for c in range(chunks):
            if h + 1 < heads:
                top = score_max(h + 1, c, top)
            rows = slice(c * BLK, (c + 1) * BLK)
            expo = jnp.exp2(store[h % 2, rows, :] - (row_max - bias[c])).astype(bf16)
            e_ref[h, rows, :] = expo
            part = dot(stacked[:, rows], expo)
            total = part if total is None else total + part
        inverse = 1.0 / total[HD : HD + 1]
        outs.append(total[:HD] * inverse)
        inverses.append(jnp.broadcast_to(inverse, (HD, BLK)))
        if h + 1 < heads:
            row_max = jnp.max(top, axis=0, keepdims=True)
    o_ref[...] = jnp.concatenate(outs, 0).T.astype(bf16)
    l_ref[...] = jnp.concatenate(inverses, 0).T


def front_kernel(
    first, lengths, gain, shift, b_own, b_up, cos, sin, w_own, tokens, w_out, w_up, w_down,
    o_ref, l_ref, e_ref, q_out, k_out, v_out, ht_out, w_all, out_other, up_other, down_other, b_all, sc, near_cos, near_sin,
    store, x_all, hidden, q_all, k_all, v_all, ht, w_in, b_mine, b_in, local, send, recv,
):
    g, b = pl.program_id(0), pl.program_id(1)
    step = 3 * g + b
    here = lax.axis_index("dp")
    mp = lax.axis_index("mp")
    c = here % 2
    x = (here // 2) % 2
    core = (here + 1 - 2 * c, mp)
    side = (here + 2 - 4 * x, mp)
    across = (here, 1 - mp)
    groups = q_all.shape[0]
    half = w_own.shape[1]
    side_long = (lengths[0, 4 * mp] == LONG).astype(jnp.int32)
    mid_long = (lengths[0, 2] == LONG).astype(jnp.int32)
    table = [0, side_long, mp * mid_long, (1 - mp) * mid_long]
    numbers = {}

    def copy(name, src, dst, dev):
        n = numbers.setdefault(name, len(numbers))
        return pltpu.make_async_remote_copy(
            src_ref=src,
            dst_ref=dst,
            send_sem=send.at[n],
            recv_sem=recv.at[n],
            device_id=dev,
            device_id_type=pl.DeviceIdType.MESH,
        )

    def quarter(ref, n):
        size = ref.shape[0] // 4
        return ref.at[pl.ds(pl.multiple_of(n * size, size), size), :]

    share = half // 2
    mine = pl.ds(pl.multiple_of(c * share, share), share)
    w_across = copy("w", w_own.at[:, mine, :], w_in.at[:, mine, :], across)
    w_core = copy("wc", w_in.at[:, mine, :], w_in.at[:, mine, :], core)
    b_across = copy("b", b_mine, b_in, across)
    out_across = copy("o", w_out, out_other, across)
    n_mine, n_side = 2 * x + c, 2 * (1 - x) + c
    pairs = ((w_up, up_other), (w_down, down_other))
    by_across = [copy(("y", n), quarter(a, n_mine), quarter(to, n_mine), across) for n, (a, to) in enumerate(pairs)]
    by_side = [copy(("x", n), quarter(to, n_mine), quarter(to, n_mine), side) for n, (_, to) in enumerate(pairs)]
    by_core = [
        copy(("c", n, m), quarter(to, at), quarter(to, at), core)
        for n, (_, to) in enumerate(pairs)
        for m, at in enumerate((n_mine, n_side))
    ]
    block = lambda at, count: pl.ds(pl.multiple_of(at * BLK, BLK), count * BLK)
    x_copies = [
        pltpu.make_async_copy(tokens.at[block(at, count), :], x_all.at[to * BLK : (to + count) * BLK, :], local.at[n])
        for n, (at, to, count) in enumerate(((4 * mp, 0, 2), (2 + mp, 2, 1), (3 - mp, 3, 1)))
    ]
    w_copies = [
        pltpu.make_async_copy(w_own, w_all.at[:, :half, :], local.at[3]),
        pltpu.make_async_copy(w_in, w_all.at[:, half:, :], local.at[4]),
    ]
    ht_copy = pltpu.make_async_copy(ht, ht_out, local.at[5])

    def qkv_copies(lo, hi, n):
        return [
            pltpu.make_async_copy(a.at[lo:hi], out.at[lo:hi], local.at[n + m])
            for m, (a, out) in enumerate(((q_all, q_out), (k_all, k_out), (v_all, v_out)))
        ]

    early, late = qkv_copies(0, first, 6), qkv_copies(first, groups, 9)

    def table_rows(i):
        chosen = jnp.full((1, GROUP), table[i], jnp.int32) > 0
        return jnp.where(chosen, cos[BLK:, :], cos[:BLK, :]), jnp.where(chosen, sin[BLK:, :], sin[:BLK, :])

    def project(w, bias, lo, hi):
        count = hi - lo
        for i in range(4):
            rows = slice(i * BLK, (i + 1) * BLK)
            out = dot(hidden[rows, :], w, NT)
            cosines, sines = table_rows(i)
            for s in range(3):
                for n in range(count):
                    at = (s * count + n) * GROUP
                    part = out[:, at : at + GROUP] + bias[s : s + 1, n * GROUP : (n + 1) * GROUP]
                    if s == 0:
                        part = rotate(part, cosines, sines) * (HD ** (-0.5) * log2_e)
                        q_all[lo + n, rows, :] = part.astype(bf16)
                    elif s == 1:
                        k_all[lo + n, rows, :] = rotate(part, cosines, sines).astype(bf16)
                    else:
                        v_all[lo + n, rows, :] = part.astype(bf16)

    @pl.when(step == 0)
    def _():
        for made in x_copies:
            made.start()
        scalars = [side_long, side_long, mid_long, 4 * mp, 4 * mp + 1, 2 + mp, 3 - mp, *table, mp, 1 + mp, 2 - 2 * mp]
        for n, value in enumerate(scalars):
            sc[n] = value
        b_mine[...] = jnp.zeros_like(b_mine)
        b_mine[:3, :half] = b_own[...].astype(f32)
        b_mine[3:4, :] = wide(b_up)
        barrier = pltpu.get_barrier_semaphore()
        for dev in (across, core, side):
            pl.semaphore_signal(barrier, inc=1, device_id=dev, device_id_type=pl.DeviceIdType.MESH)
        pl.semaphore_wait(barrier, 3)
        w_across.start()
        b_across.start()
        for made in x_copies:
            made.wait()
        for i in range(4):
            rows = slice(i * BLK, (i + 1) * BLK)
            normed, _ = normalize(x_all[rows, :].astype(f32))
            fresh = (normed * wide(gain) + wide(shift)).astype(bf16)
            hidden[rows, :] = fresh
            ht[:, rows] = fresh.T
        ht_copy.start()
        w_copies[0].start()
        near_cos[...], near_sin[...] = table_rows(2)
        w = jnp.concatenate([w_own[s, : first * GROUP, :] for s in range(3)], 0)
        project(w, b_mine[:3, : first * GROUP], 0, first)
        for made in early:
            made.start()

    @pl.when(step == 2)
    def _():
        by_across[0].start()

    @pl.when(step == 3)
    def _():
        w_across.wait()
        w_core.start()
        b_across.wait()
        by_across[1].start()

    @pl.when(step == 3 * first)
    def _():
        w_core.wait()
        w_copies[1].start()
        tail = first * GROUP
        w = jnp.concatenate([part for s in range(3) for part in (w_own[s, tail:, :], w_in[s])], 0)
        bias = jnp.concatenate([b_mine[:3, tail:half], b_in[:3, :half]], 1)
        project(w, bias, first, groups)
        for made in late:
            made.start()

    @pl.when(step == 3 * first + 1)
    def _():
        for n in range(2):
            by_across[n].wait()
            by_side[n].start()
        out_across.start()

    @pl.when(step == 3 * first + 6)
    def _():
        by_side[0].wait()
        for made in by_core[:2]:
            made.start()

    @pl.when(step == 3 * groups - 1)
    def _():
        by_side[1].wait()
        for made in by_core[2:]:
            made.start()

    keys = pl.ds(pl.multiple_of(b // 2 * LONG, LONG), LONG)
    q = q_all[g, pl.ds(pl.multiple_of(b * BLK, BLK), BLK), :]
    refs = (q, k_all.at[g, keys, :], v_all.at[g, keys, :], o_ref, l_ref, e_ref, store)
    off = lambda allowed: jnp.where(allowed, 0.0, -1e30).astype(f32)

    @pl.when(b != 2)
    def _():
        attend_body(*refs, [off((b == n) | (side_long == 1)) for n in range(2)])

    @pl.when(b == 2)
    def _():
        attend_body(*refs, [off(True), off(mid_long == 1)])

    @pl.when(step == 3 * groups - 1)
    def _():
        b_all[:, : b_mine.shape[1]] = b_mine[3:4, :]
        b_all[:, b_mine.shape[1] :] = b_in[3:4, :]
        out_across.wait()
        for made in by_core:
            made.wait()
        for made in (*early, *late, *w_copies, ht_copy):
            made.wait()


def front(lengths, gain, shift, b_own, b_up, cos, sin, w_own, tokens, w_out, w_up, w_down):
    d = tokens.shape[1]
    groups = d // GROUP
    heads = GROUP // HD
    half = w_own.shape[1]
    own, rows = 3 * BLK, 4 * BLK
    one = pl.Buffered(buffer_count=1)
    whole = lambda a: pl.BlockSpec(a.shape, lambda g, b: (0,) * a.ndim, pipeline_mode=one)
    os = pl.BlockSpec((None, BLK, GROUP), lambda g, b: (g, b, 0))
    es = pl.BlockSpec((heads, LONG, BLK), lambda g, b: (g * 3 + b, 0, 0))
    hbm = pl.BlockSpec(memory_space=pl.ANY)
    held = jax.ShapeDtypeStruct((groups, rows, GROUP), bf16)
    copies = 2 + 2 + 2 + 2 + 4
    return pl.pallas_call(
        functools.partial(front_kernel, half // GROUP),
        grid=(groups, 3),
        in_specs=[pl.BlockSpec(memory_space=pltpu.SMEM)]
        + [whole(a) for a in (gain, shift, b_own, b_up, cos, sin, w_own)]
        + [hbm] * 4,
        out_specs=[os, os, es]
        + [hbm] * 8
        + [pl.BlockSpec((1, 2 * b_up.shape[0]), lambda g, b: (0, 0)), pl.BlockSpec(memory_space=pltpu.SMEM)]
        + [pl.BlockSpec((BLK, GROUP), lambda g, b: (0, 0))] * 2,
        out_shape=[
            jax.ShapeDtypeStruct((groups, own, GROUP), bf16),
            jax.ShapeDtypeStruct((groups, own, GROUP), f32),
            jax.ShapeDtypeStruct((groups * 3 * heads, LONG, BLK), bf16),
            held,
            held,
            held,
            jax.ShapeDtypeStruct((d, rows), bf16),
            jax.ShapeDtypeStruct((3, 2 * half, d), bf16),
            jax.ShapeDtypeStruct(w_out.shape, bf16),
            jax.ShapeDtypeStruct(w_up.shape, bf16),
            jax.ShapeDtypeStruct(w_down.shape, bf16),
            jax.ShapeDtypeStruct((1, 2 * b_up.shape[0]), f32),
            jax.ShapeDtypeStruct((14,), jnp.int32),
            jax.ShapeDtypeStruct((BLK, GROUP), f32),
            jax.ShapeDtypeStruct((BLK, GROUP), f32),
        ],
        scratch_shapes=[
            pltpu.VMEM((2, LONG, BLK), f32),
            pltpu.VMEM((rows, d), bf16),
            pltpu.VMEM((rows, d), bf16),
            pltpu.VMEM((groups, rows, GROUP), bf16),
            pltpu.VMEM((groups, rows, GROUP), bf16),
            pltpu.VMEM((groups, rows, GROUP), bf16),
            pltpu.VMEM((d, rows), bf16),
            pltpu.VMEM(w_own.shape, bf16),
            pltpu.VMEM((8, b_up.shape[0]), f32),
            pltpu.VMEM((8, b_up.shape[0]), f32),
            pltpu.SemaphoreType.DMA((12,)),
            pltpu.SemaphoreType.DMA((copies,)),
            pltpu.SemaphoreType.DMA((copies,)),
        ],
        compiler_params=pltpu.CompilerParams(
            vmem_limit_bytes=VMEM_LIMIT, collective_id=1, has_side_effects=True
        ),
        cost_estimate=pl.CostEstimate(
            flops=50_000_000_000, bytes_accessed=100_000_000, transcendentals=31_000_000
        ),
        name="front",
    )(lengths, gain, shift, b_own, b_up, cos, sin, w_own, tokens, w_out, w_up, w_down)


def attend_back_body(
    q_ref, k_ref, v_ref, do_ref, o_ref, l_ref, e_ref, prod, dk_sum, dv_sum, start, count
):
    lane = lax.broadcasted_iota(jnp.int32, (1, GROUP), 1) // HD
    heads = GROUP // HD
    q = q_ref[...]
    do = (do_ref[...].astype(f32) * l_ref[...]).astype(bf16)
    both = do.astype(f32) * o_ref[...].astype(f32)
    upper = both.astype(bf16)
    lower = (both - upper.astype(f32)).astype(bf16)
    pick = (
        lax.broadcasted_iota(jnp.int32, (8, GROUP), 0)
        == lax.broadcasted_iota(jnp.int32, (8, GROUP), 1) // HD
    )
    pick = pick.astype(f32).astype(bf16)
    delta = dot(pick, upper, NT) + dot(pick, lower, NT)
    keys_t = k_ref[pl.ds(start, count), :].T
    chunks = count // BLK
    tiles = [(h, c) for h in range(heads) for c in range(chunks)]

    def grad_probs(i):
        h, c = tiles[i]
        values = v_ref[pl.ds(start + c * BLK, BLK), :]
        prod[i % 2] = dot(jnp.where(lane == h, values, jnp.zeros_like(values)), do, NT)

    grad_probs(0)
    dq_t = [None] * heads
    for i, (h, c) in enumerate(tiles):
        if i + 1 < len(tiles):
            grad_probs(i + 1)
        rows = pl.ds(start + c * BLK, BLK)
        expo = e_ref[h, rows, :]
        ds = (expo.astype(f32) * (prod[i % 2] - delta[h : h + 1])).astype(bf16)
        dv_sum[rows, :] += dot(expo, jnp.where(lane == h, do, jnp.zeros_like(do)))
        dk_sum[rows, :] += dot(ds, jnp.where(lane == h, q, jnp.zeros_like(q)))
        part = dot(keys_t[HD * h : HD * (h + 1), c * BLK : (c + 1) * BLK], ds)
        dq_t[h] = part if dq_t[h] is None else dq_t[h] + part
    return jnp.concatenate(dq_t, 0).T


def window_back(dq, dk_sum, dv_sum, tables, w_ref, ht_ref, dh_sum):
    parts = [] if dq is None else [dq]
    dk = dk_sum[...] * ln_2
    rotated = []
    for n, (cos, sin) in enumerate(tables):
        rotated.append(rotate_back(dk[n * BLK : (n + 1) * BLK], cos[...], sin[...]))
    parts.append(jnp.concatenate(rotated, 0).astype(bf16))
    parts.append(dv_sum[...].astype(bf16))
    both = jnp.concatenate(parts, 1)
    w = jnp.concatenate([w_ref[s] for s in range(3 - len(parts), 3)], 0)
    for n in range(len(tables)):
        rows = slice(n * BLK, (n + 1) * BLK)
        dh_sum[rows, :] += dot(both[rows], w)
    return dot(ht_ref[...], both), jnp.sum(both.astype(f32), 0, keepdims=True)


def back_kernel(
    mode, sc, q_ref, k_ref, v_ref, do_ref, o_ref, l_ref, e_ref, cos, sin, cos0, sin0, cos1, sin1, w_ref, ht_ref,
    *rest,
):
    g = pl.program_id(0)
    last_g = pl.num_programs(0) - 1
    step = pl.program_id(1)
    if mode == "whole":
        x_ref, gain, mid_ref, g_ref, gb_ref, out_ref, small, dq_cat, prod, dk_sum, dv_sum, dh_sum = rest
    elif mode == "far":
        before, before_b, g_ref, gb_ref, dq_out, part_ref, prod, dk_sum, dv_sum, dh_sum = rest
    else:
        before, before_b, dq_in, g_ref, gb_ref, own_ref, prod, dk_sum, dv_sum, dh_sum = rest
    refs = (q_ref, k_ref, v_ref, do_ref, o_ref, l_ref, e_ref, prod, dk_sum, dv_sum)
    own_tables = (cos0, sin0), (cos1, sin1)
    finish_q = lambda dq: rotate_back(dq * (HD ** (-0.5)), cos[...], sin[...]).astype(bf16)

    @pl.when(step == 0)
    def _():
        dk_sum[...] = jnp.zeros_like(dk_sum)
        dv_sum[...] = jnp.zeros_like(dv_sum)

    @pl.when((step == 0) & (g == 0))
    def _():
        dh_sum[...] = jnp.zeros_like(dh_sum)

    if mode == "whole":
        place = pl.ds(pl.multiple_of(step * BLK, BLK), BLK)

        @pl.when(sc[FLAG] == 1)
        def _():
            dq_cat[place, :] = finish_q(attend_back_body(*refs, 0, LONG))

        @pl.when(sc[FLAG] == 0)
        def _():
            dq_cat[place, :] = finish_q(attend_back_body(*refs, pl.multiple_of(step * BLK, BLK), BLK))

        @pl.when(step == 1)
        def _():
            g_ref[...], gb_ref[...] = window_back(
                dq_cat[...], dk_sum, dv_sum, own_tables, w_ref, ht_ref, dh_sum
            )

        @pl.when((step == 1) & (g == last_g))
        def _():
            sums = [None, None]
            for rows in (slice(0, BLK), slice(BLK, LONG)):
                out, *terms = finish_rows(x_ref[rows, :], wide(gain), mid_ref[rows, :], dh_sum[rows, :])
                out_ref[rows, :] = out
                for n, term in enumerate(terms):
                    sums[n] = term if sums[n] is None else sums[n] + term
            small[...] = jnp.concatenate(sums + [jnp.zeros_like(sums[0])] * 6, 0)

    elif mode == "far":

        @pl.when(sc[FLAG + 2] == 1)
        def _():
            dq_out[...] = attend_back_body(*refs, 0, BLK)

        @pl.when(sc[FLAG + 2] == 0)
        def _():
            dq_out[...] = jnp.zeros_like(dq_out)

        weight, bias = window_back(None, dk_sum, dv_sum, own_tables[:1], w_ref, ht_ref, dh_sum)
        g_ref[:, :GROUP] = before[:, :GROUP]
        g_ref[:, GROUP:] = before[:, GROUP:] + weight
        gb_ref[:, :GROUP] = before_b[:, :GROUP]
        gb_ref[:, GROUP:] = before_b[:, GROUP:] + bias

        @pl.when(g == last_g)
        def _():
            part_ref[...] = dh_sum[...].astype(bf16)

    else:
        dq = finish_q(attend_back_body(*refs, 0, BLK) + dq_in[...])
        weight, bias = window_back(dq, dk_sum, dv_sum, own_tables[:1], w_ref, ht_ref, dh_sum)
        weight = weight + before[...]
        gb_ref[...] = bias + before_b[...]
        g_ref[...] = weight.astype(bf16)

        @pl.when(g == last_g)
        def _():
            own_ref[...] = dh_sum[...]


def back(mode, sc, q, k, v, do, o, inverse, expo, cos, sin, w, hidden_t, more):
    groups = o.shape[0]
    d = w.shape[2]
    heads = GROUP // HD
    blocks = 2 if mode == "whole" else 1
    query = 0 if mode == "whole" else 2
    key = {"whole": 0, "far": 3, "near": 2}[mode]
    keys = LONG if mode == "whole" else BLK
    one = pl.Buffered(buffer_count=1)
    qs = pl.BlockSpec((None, BLK, GROUP), lambda g, b, s: (g, b + query, 0))
    ks = pl.BlockSpec((None, keys, GROUP), lambda g, b, s: (g, key, 0))
    os = pl.BlockSpec((None, BLK, GROUP), lambda g, b, s: (g, b + query, 0))
    es = pl.BlockSpec((heads, keys, BLK), lambda g, b, s: (g * 3 + b + query, 1 if mode == "far" else 0, 0))
    tq = pl.BlockSpec((BLK, GROUP), lambda g, b, s: (s[TABLE + b + query], 0))
    t0 = pl.BlockSpec((BLK, GROUP), lambda g, b, s: (s[TABLE + key], 0))
    t1 = pl.BlockSpec((BLK, GROUP), lambda g, b, s: (s[TABLE + key + (blocks - 1)], 0))
    weight = pl.BlockSpec((None, d, 3 * GROUP), lambda g, b, s: (g, 0, 0))
    bias = pl.BlockSpec((None, 1, 3 * GROUP), lambda g, b, s: (g, 0, 0))
    dq_part = pl.BlockSpec((None, BLK, GROUP), lambda g, b, s: (g, 0, 0))
    whole = lambda *shape: pl.BlockSpec(shape, lambda g, b, s: (0, 0))
    in_specs = [qs, ks, ks, os, os, os, es, tq, tq, t0, t0, t1, t1]
    in_specs += [
        pl.BlockSpec((3, GROUP, d), lambda g, b, s: (0, g, 0)),
        pl.BlockSpec((d, keys), lambda g, b, s: (0, key), pipeline_mode=one),
    ]
    bias_shape = jax.ShapeDtypeStruct((groups, 1, 3 * GROUP), f32)
    scratch = [
        pltpu.VMEM((2, BLK, BLK), f32),
        pltpu.VMEM((keys, GROUP), f32),
        pltpu.VMEM((keys, GROUP), f32),
        pltpu.VMEM((keys, d), f32),
    ]
    if mode == "whole":
        in_specs += [
            pl.BlockSpec((LONG, d), lambda g, b, s: (s[BLOCK] // 2, 0), pipeline_mode=one),
            pl.BlockSpec((d,), lambda g, b, s: (0,)),
            pl.BlockSpec((LONG, d), lambda g, b, s: (0, 0), pipeline_mode=one),
        ]
        out_specs = [weight, bias, whole(LONG, d), whole(8, d)]
        out_shape = [
            jax.ShapeDtypeStruct((groups, d, 3 * GROUP), f32),
            bias_shape,
            jax.ShapeDtypeStruct((LONG, d), bf16),
            jax.ShapeDtypeStruct((8, d), f32),
        ]
        scratch = [pltpu.VMEM((LONG, GROUP), bf16)] + scratch
    elif mode == "far":
        in_specs += [weight, bias]
        out_specs = [weight, bias, dq_part, whole(BLK, d)]
        out_shape = [
            jax.ShapeDtypeStruct((groups, d, 3 * GROUP), f32),
            bias_shape,
            jax.ShapeDtypeStruct((groups, BLK, GROUP), f32),
            jax.ShapeDtypeStruct((BLK, d), bf16),
        ]
    else:
        in_specs += [weight, bias, dq_part]
        out_specs = [weight, bias, whole(BLK, d)]
        out_shape = [
            jax.ShapeDtypeStruct((groups, d, 3 * GROUP), bf16),
            bias_shape,
            jax.ShapeDtypeStruct((BLK, d), f32),
        ]
    return pl.pallas_call(
        functools.partial(back_kernel, mode),
        grid_spec=pltpu.PrefetchScalarGridSpec(
            num_scalar_prefetch=1,
            grid=(groups, blocks),
            in_specs=in_specs,
            out_specs=out_specs,
            scratch_shapes=scratch,
        ),
        out_shape=out_shape,
        compiler_params=pltpu.CompilerParams(vmem_limit_bytes=VMEM_LIMIT),
        cost_estimate=pl.CostEstimate(
            flops=groups * blocks * keys * 5_000_000, bytes_accessed=groups * blocks * 6_000_000, transcendentals=0
        ),
        name="back_" + mode,
    )(sc, q, k, v, do, o, inverse, expo, cos, sin, cos, sin, cos, sin, w, hidden_t, *more)


def gelu_parts(z):
    density = jnp.exp2(z * z * (-0.5 * log2_e)) * 0.3989422804014327
    t = 1.0 / (1.0 + 0.2316419 * jnp.abs(z))
    poly = t * (
        0.319381530
        + t * (-0.356563782 + t * (1.781477937 + t * (-1.821255978 + t * 1.330274429)))
    )
    tail = density * poly
    cdf = jnp.where(z >= 0, 1.0 - tail, tail)
    return z * cdf, cdf + z * density


def middle_kernel(
    sc, tokens, cotangent, o_hbm, w_out_own, w_out_other, b_out, gain, shift,
    up_a, up_b, up_c, up_d, b_up, down_a, down_b, down_c, down_d, b_down,
    out_hbm, mid_hbm, do_hbm, g_ref, g_out, g_bup, g_small,
    w_out, r1, h2, h2t, dy, dyt, acc, back, x_ref, o_ref, out_ref, do_ref, arrive, leave,
):
    i = pl.program_id(0)
    last = pl.num_programs(0) - 1
    blocks = [slice(j * BLK, (j + 1) * BLK) for j in range(3)]
    groups = o_ref.shape[0]
    block = lambda at: pl.ds(pl.multiple_of(at * BLK, BLK), BLK)
    o_in = [pltpu.make_async_copy(o_hbm.at[:, rows, :], o_ref.at[:, rows, :], arrive.at[j]) for j, rows in enumerate(blocks)]
    x_in = [
        pltpu.make_async_copy(tokens.at[block(sc[BLOCK + j]), :], x_ref.at[rows, :], arrive.at[3 + j])
        for j, rows in enumerate(blocks)
    ]
    y_in = [
        pltpu.make_async_copy(cotangent.at[block(sc[BLOCK + j]), :], dy.at[rows, :], arrive.at[6 + j])
        for j, rows in enumerate(blocks)
    ]
    leaving = [
        (
            pltpu.make_async_copy(out_ref.at[rows, :], out_hbm.at[block(sc[PLACE + j]), :], leave.at[j]),
            pltpu.make_async_copy(r1.at[rows, :], mid_hbm.at[rows, :], leave.at[3 + j]),
            pltpu.make_async_copy(do_ref.at[:, rows, :], do_hbm.at[:, rows, :], leave.at[6 + j]),
        )
        for j, rows in enumerate(blocks)
    ]
    heads_of = lambda rows: jnp.concatenate([o_ref[g, rows, :] for g in range(groups)], 1)

    @pl.when(i == 0)
    def _():
        for made in [m for pair in zip(o_in, x_in) for m in pair] + y_in:
            made.start()
        w_out[: w_out_own.shape[0], :] = w_out_own[...]
        w_out[w_out_own.shape[0] :, :] = w_out_other[...]
        for j, rows in enumerate(blocks):
            o_in[j].wait()
            x_in[j].wait()
            mixed = dot(heads_of(rows), w_out[...]) + wide(b_out) + x_ref[rows, :].astype(f32)
            r1[rows, :] = mixed
            normed, _ = normalize(mixed)
            hidden = (normed * wide(gain) + wide(shift)).astype(bf16)
            h2[rows, :] = hidden
            h2t[:, rows] = hidden.T
            acc[rows, :] = jnp.zeros_like(mixed)
            back[rows, :] = jnp.zeros_like(mixed)
        for j, rows in enumerate(blocks):
            y_in[j].wait()
            dyt[:, rows] = dy[rows, :].T

    @pl.when(i < last)
    def _():
        first, second = 2 * i < last, 2 * i + 1 < last
        w_up = jnp.concatenate(
            [jnp.where(first, up_a[...], up_c[...]), jnp.where(second, up_b[...], up_d[...])], 1
        )
        w_down = jnp.concatenate(
            [jnp.where(first, down_a[...], down_c[...]), jnp.where(second, down_b[...], down_d[...])], 0
        )
        bias = b_up[...]
        width = up_a.shape[1]
        total = dy.shape[0]
        parts = [slice(j, j + 256) for j in range(0, total, BLK // 2)]
        count = len(parts)
        actives, grads = [None] * count, [None] * count
        ups, downs = [None] * count, [None] * count
        col_sum = None

        def ahead(j):
            ups[j] = dot(h2[parts[j], :], w_up) + bias
            downs[j] = dot(dy[parts[j], :], w_down, NT)

        ahead(0)
        for j, rows in enumerate(parts):
            if j + 1 < count:
                ahead(j + 1)
            active, slope = gelu_parts(ups[j])
            actives[j] = active.astype(bf16)
            grads[j] = (downs[j] * slope).astype(bf16)
            s = jnp.sum(grads[j].astype(f32), 0, keepdims=True)
            col_sum = s if col_sum is None else col_sum + s
            acc[rows, :] += dot(actives[j], w_down)
            back[rows, :] += dot(grads[j], w_up, NT)
        g_bup[...] = col_sum
        g_up = dot(h2t[...], jnp.concatenate(grads, 0)).astype(bf16)
        g_down = dot(dyt[...], jnp.concatenate(actives, 0)).astype(bf16)
        for n in range(2):
            cols = slice(n * width, (n + 1) * width)
            g_ref[:, 2 * n * width : (2 * n + 1) * width] = g_up[:, cols]
            g_ref[:, (2 * n + 1) * width : (2 * n + 2) * width] = g_down[:, cols]

    @pl.when(i == last)
    def _():
        sums = [None] * 4
        lows = []
        for j, rows in enumerate(blocks):
            mixed = r1[rows, :]
            out_ref[rows, :] = (acc[rows, :] + wide(b_down) + mixed).astype(bf16)
            normed, inverse = normalize(mixed)
            top = dy[rows, :].astype(f32)
            dh = back[rows, :]
            dr = top + normalize_back(normed, inverse, dh * wide(gain))
            r1[rows, :] = dr
            low = dr.astype(bf16)
            lows.append(low)
            do = dot(low, w_out[...], NT).astype(bf16)
            for g in range(groups):
                do_ref[g, rows, :] = do[:, g * GROUP : (g + 1) * GROUP]
            for made in leaving[j]:
                made.start()
            for n, term in enumerate((dh * normed, dh, dr, top)):
                s = jnp.sum(term, 0, keepdims=True)
                sums[n] = s if sums[n] is None else sums[n] + s
        g_out[...] = dot(jnp.concatenate(lows, 0).T, heads_of(slice(0, 3 * BLK))).astype(bf16)
        g_small[...] = jnp.concatenate(sums + [jnp.zeros_like(sums[0])] * 4, 0)
        for parts in leaving:
            for made in parts:
                made.wait()


def middle(sc, tokens, cotangent, o, w_out_own, w_out_other, b_out, gain, shift, up_own, down_own, up_other, down_other, b_up, b_down):
    d = tokens.shape[1]
    groups = o.shape[0]
    own = 3 * BLK
    half = up_own.shape[1]
    piece = 256
    per = half // piece
    steps = per + 1
    one = pl.Buffered(buffer_count=1)
    whole = lambda *shape: pl.BlockSpec(shape, lambda i, s: (0,) * len(shape), pipeline_mode=one)
    hbm = pl.BlockSpec(memory_space=pl.ANY)
    fixed = lambda *shape: pl.BlockSpec(shape, lambda i, s: (0,) * len(shape))
    at = lambda i: jnp.minimum(i, per - 1)
    places = [
        lambda i: jnp.minimum(2 * i, per - 1),
        lambda i: jnp.minimum(2 * i + 1, per - 1),
        lambda i: jnp.clip(2 * i - per, 0, per - 1),
        lambda i: jnp.clip(2 * i + 1 - per, 0, per - 1),
    ]
    ups = [pl.BlockSpec((d, piece), functools.partial(lambda p, i, s: (0, p(i)), p)) for p in places]
    downs = [pl.BlockSpec((piece, d), functools.partial(lambda p, i, s: (p(i), 0), p)) for p in places]
    return pl.pallas_call(
        middle_kernel,
        grid_spec=pltpu.PrefetchScalarGridSpec(
            num_scalar_prefetch=1,
            grid=(steps,),
            in_specs=[hbm, hbm, hbm]
            + [
                whole(*w_out_own.shape),
                whole(*w_out_other.shape),
                whole(d),
                whole(d),
                whole(d),
                *ups,
                pl.BlockSpec((1, 2 * piece), lambda i, s: (0, at(i))),
                *downs,
                whole(d),
            ],
            out_specs=[
                hbm,
                hbm,
                hbm,
                pl.BlockSpec((d, 4 * piece), lambda i, s: (0, at(i))),
                fixed(d, d),
                pl.BlockSpec((1, 2 * piece), lambda i, s: (0, at(i))),
                fixed(8, d),
            ],
            scratch_shapes=[
                pltpu.VMEM((d, d), bf16),
                pltpu.VMEM((own, d), f32),
                pltpu.VMEM((own, d), bf16),
                pltpu.VMEM((d, own), bf16),
                pltpu.VMEM((own, d), bf16),
                pltpu.VMEM((d, own), bf16),
                pltpu.VMEM((own, d), f32),
                pltpu.VMEM((own, d), f32),
                pltpu.VMEM((own, d), bf16),
                pltpu.VMEM((groups, own, GROUP), bf16),
                pltpu.VMEM((own, d), bf16),
                pltpu.VMEM((groups, own, GROUP), bf16),
                pltpu.SemaphoreType.DMA((9,)),
                pltpu.SemaphoreType.DMA((9,)),
            ],
        ),
        out_shape=[
            jax.ShapeDtypeStruct((own, d), bf16),
            jax.ShapeDtypeStruct((own, d), f32),
            jax.ShapeDtypeStruct((groups, own, GROUP), bf16),
            jax.ShapeDtypeStruct((d, 4 * half), bf16),
            jax.ShapeDtypeStruct((d, d), bf16),
            jax.ShapeDtypeStruct((1, 2 * half), f32),
            jax.ShapeDtypeStruct((8, d), f32),
        ],
        compiler_params=pltpu.CompilerParams(vmem_limit_bytes=VMEM_LIMIT),
        cost_estimate=pl.CostEstimate(
            flops=2 * own * d * (3 * d + 12 * half), bytes_accessed=40_000_000, transcendentals=8_000_000
        ),
        name="middle",
    )(sc, tokens, cotangent, o, w_out_own, w_out_other, b_out, gain, shift,
      *[up_own] * 2, *[up_other] * 2, b_up, *[down_own] * 2, *[down_other] * 2, b_down)


def finish_rows(x, gain, mid, dh):
    normed, inverse = normalize(x.astype(f32))
    out = (mid + normalize_back(normed, inverse, dh * gain)).astype(bf16)
    return out, jnp.sum(dh * normed, 0, keepdims=True), jnp.sum(dh, 0, keepdims=True)


def lines(v):
    return jnp.concatenate([v[:, j * GROUP : (j + 1) * GROUP] for j in range(v.shape[1] // GROUP)], 0)


def last_kernel(
    q_ref, k_ref, v_ref, do_ref, o_ref, l_ref, e_ref, cos, sin, w_ref, ht_ref, before, before_b, dq_in, gout_ref,
    part_ref, tokens, gain, mid, small_w, small_two, gup_ref, early_ref,
    sum_out, theirs_out, small_out, small_theirs_out, rows_out, rows_theirs_out, early_out,
    prod, dk_sum, dv_sum, dh_sum, gb_sum, g_all, part_in, x_ref, mid_ref, early_part, early_in,
    r1, a1, r2, a2, r3, sums, theirs, rows_ref, rows_in, s0, s1, s2, s3, q1, q2, q3, q4, send, recv, local,
):
    g = pl.program_id(0)
    groups = g_all.shape[3]
    here = lax.axis_index("dp")
    mp = lax.axis_index("mp")
    c = here % 2
    x = (here // 2) % 2
    z = here // 4
    core = (here + 1 - 2 * c, mp)
    side = (here + 2 - 4 * x, mp)
    across = (here, 1 - mp)
    line = [((z + n) % 4, ((z + n) % 4 * 4 + here % 4, mp)) for n in (1, 2, 3)]

    numbers = {}

    def copy(name, src, dst, dev):
        n = numbers.setdefault(name, len(numbers))
        return pltpu.make_async_remote_copy(
            src_ref=src,
            dst_ref=dst,
            send_sem=send.at[n],
            recv_sem=recv.at[n],
            device_id=dev,
            device_id_type=pl.DeviceIdType.MESH,
        )

    part_copy = copy("part", part_ref, part_in, across)
    early_copy = copy("early", early_part, early_in, across)
    rows_copy = copy("rows", rows_ref, rows_in, across)
    by_core = [copy(("c", n), g_all.at[:, :, 1 - c, n], r1.at[:, :, n], core) for n in range(groups)]
    by_side = [copy(("x", n), a1.at[:, 1 - x, n], r2.at[:, n], side) for n in range(groups)]
    by_line = [
        [copy(("z", n, m), a2.at[at, n], r3.at[m, n], dev) for m, (at, dev) in enumerate(line)]
        for n in range(groups)
    ]
    by_across = [copy(("y", n), sums.at[n], theirs.at[n], across) for n in range(groups)]
    small_core = copy("sc", s0, q1, core)
    small_side = copy("sx", s1, q2, side)
    small_line = [copy(("sz", m), s2, q3.at[z], dev) for m, (_, dev) in enumerate(line)]
    small_across = copy("sy", s3, q4, across)
    rows = pl.ds(pl.multiple_of((2 + mp) * BLK, BLK), BLK)
    x_copy = pltpu.make_async_copy(tokens.at[rows, :], x_ref, local.at[0])
    mid_copy = pltpu.make_async_copy(mid.at[2 * BLK : 3 * BLK, :], mid_ref, local.at[1])

    @pl.when(g == 0)
    def _():
        barrier = pltpu.get_barrier_semaphore()
        partners = [core, side, across] + [dev for _, dev in line]
        for dev in partners:
            pl.semaphore_signal(barrier, inc=1, device_id=dev, device_id_type=pl.DeviceIdType.MESH)
        pl.semaphore_wait(barrier, len(partners))
        part_copy.start()
        x_copy.start()
        mid_copy.start()
        dh_sum[...] = jnp.zeros_like(dh_sum)
        share, width = early_ref.shape[0], early_part.shape[1]
        start = gup_ref.shape[1]
        early_part[share:, :] = jnp.zeros((early_part.shape[0] - share, width), bf16)
        early_part[:share, :] = early_ref[:, start : start + width]
        early_copy.start()

    dk_sum[...] = jnp.zeros_like(dk_sum)
    dv_sum[...] = jnp.zeros_like(dv_sum)
    refs = (q_ref, k_ref, v_ref, do_ref, o_ref, l_ref, e_ref, prod, dk_sum, dv_sum)
    dq = (attend_back_body(*refs, 0, BLK) + dq_in[...]) * (HD ** (-0.5))
    dq = rotate_back(dq, cos[...], sin[...]).astype(bf16)
    weight, bias = window_back(dq, dk_sum, dv_sum, ((cos, sin),), w_ref, ht_ref, dh_sum)
    weight = weight + before[...]
    gb_sum[g] = bias + before_b[...]
    share = early_ref.shape[0]
    held_rows = 4 * share
    fill = jnp.zeros((g_all.shape[4] - held_rows, GROUP), f32)
    weight = jnp.concatenate([weight, gout_ref[...].astype(f32)], 1)
    for n in range(16):
        part = weight[n * share : (n + 1) * share]
        pieces = [part[:, s * GROUP : (s + 1) * GROUP] for s in range(4)]
        pieces = pieces + [fill] if fill.shape[0] else pieces
        g_all[n // 4, n // 2 % 2, n % 2, g] = jnp.concatenate(pieces, 0).astype(bf16)

    def second(n):
        by_core[n].wait()
        a1[:, :, n] = (g_all[:, :, c, n].astype(f32) + r1[:, :, n].astype(f32)).astype(bf16)
        by_side[n].start()

    def third(n):
        by_side[n].wait()
        a2[:, n] = (a1[:, x, n].astype(f32) + r2[:, n].astype(f32)).astype(bf16)
        for made in by_line[n]:
            made.start()

    def fourth(n):
        for made in by_line[n]:
            made.wait()
        total = a2[z, n].astype(f32)
        for m in range(3):
            total = total + r3[m, n].astype(f32)
        sums[n] = total.astype(bf16)
        by_across[n].start()

    for n in range(groups):

        @pl.when(g == n)
        def _(n=n):
            by_core[n].start()
            if n == groups - 1:
                return
            for late, stage in ((1, second), (2, third), (3, fourth)):
                if n >= late:
                    stage(n - late)

    @pl.when(g == groups - 1)
    def _():
        x_copy.wait()
        mid_copy.wait()
        part_copy.wait()
        out, one, two = finish_rows(x_ref[...], wide(gain), mid_ref[...], dh_sum[...] + part_in[...].astype(f32))
        rows_ref[...] = out
        rows_copy.start()
        n = groups - 1
        second(n - 1)
        third(n - 2)
        held = [lines(small_w[0:1, :] + one), lines(small_w[1:2, :] + two)]
        held += [lines(small_two[m : m + 1, :]) for m in range(4)]
        held += [gb_sum[m, :, s * GROUP : (s + 1) * GROUP] for s in range(3) for m in range(groups)]
        held.append(lines(gup_ref[...]))
        held = jnp.concatenate(held, 0)
        s0[...] = jnp.concatenate([held, jnp.zeros((s0.shape[0] - held.shape[0], GROUP), f32)], 0)
        small_core.start()
        second(n)
        fourth(n - 3)
        third(n - 1)
        small_core.wait()
        s1[...] = s0[...] + q1[...]
        small_side.start()
        fourth(n - 2)
        third(n)
        small_side.wait()
        s2[...] = s1[...] + q2[...]
        for made in small_line:
            made.start()
        fourth(n - 1)
        for made in small_line:
            made.wait()
        q3[z] = s2[...]
        s3[...] = (q3[0] + q3[1]) + (q3[2] + q3[3])
        small_across.start()
        fourth(n)
        early_copy.wait()
        early_out[...] = early_in[...]
        small_out[...] = s3[...]
        sum_out[...] = sums[...]
        rows_out[...] = rows_ref[...]
        rows_copy.wait()
        rows_theirs_out[...] = rows_in[...]
        small_across.wait()
        small_theirs_out[...] = q4[...]
        for made in by_across:
            made.wait()
        theirs_out[...] = theirs[...]


def last(q, k, v, do, o, inverse, expo, cos, sin, w, hidden_t, g_sum, gb_sum, dq_far, g_out, part, tokens, gain, mid,
         small_w, small_two, g_bup, early):
    groups = o.shape[0]
    d = w.shape[2]
    heads = GROUP // HD
    share = early.shape[0]
    held = -(-4 * share // 16) * 16
    block = (groups, held, GROUP)
    count = 6 * d // GROUP + groups * 3 + g_bup.shape[1] // GROUP
    small = (-(-count // 8) * 8, GROUP)
    early_part = (-(-share // 16) * 16, g_bup.shape[1])
    copies = 3 + 6 * groups + 6
    one = pl.Buffered(buffer_count=1)
    hbm = pl.BlockSpec(memory_space=pl.ANY)
    whole = lambda a: pl.BlockSpec(a.shape, lambda g: (0,) * a.ndim, pipeline_mode=one)
    fixed = lambda shape: pl.BlockSpec(shape, lambda g: (0,) * len(shape))
    qs = pl.BlockSpec((None, BLK, GROUP), lambda g: (g, 2, 0))
    os = pl.BlockSpec((None, BLK, GROUP), lambda g: (g, 2, 0))
    outs = [(block, bf16), (block, bf16), (small, f32), (small, f32), ((BLK, d), bf16), ((BLK, d), bf16)]
    outs.append((early_part, bf16))
    return pl.pallas_call(
        last_kernel,
        grid=(groups,),
        in_specs=[qs, qs, qs, os, os, os]
        + [
            pl.BlockSpec((heads, BLK, BLK), lambda g: (g * 3 + 2, 0, 0)),
            whole(cos),
            whole(sin),
            pl.BlockSpec((3, GROUP, d), lambda g: (0, g, 0)),
            pl.BlockSpec((d, BLK), lambda g: (0, 2), pipeline_mode=one),
            pl.BlockSpec((None, d, 3 * GROUP), lambda g: (g, 0, 0)),
            pl.BlockSpec((None, 1, 3 * GROUP), lambda g: (g, 0, 0)),
            pl.BlockSpec((None, BLK, GROUP), lambda g: (g, 0, 0)),
            pl.BlockSpec((d, GROUP), lambda g: (0, g)),
            whole(part),
            hbm,
            whole(gain),
            hbm,
            whole(small_w),
            whole(small_two),
            whole(g_bup),
            whole(early),
        ],
        out_specs=[fixed(shape) for shape, _ in outs],
        out_shape=[jax.ShapeDtypeStruct(*spec) for spec in outs],
        scratch_shapes=[
            pltpu.VMEM((2, BLK, BLK), f32),
            pltpu.VMEM((BLK, GROUP), f32),
            pltpu.VMEM((BLK, GROUP), f32),
            pltpu.VMEM((BLK, d), f32),
            pltpu.VMEM((groups, 1, 3 * GROUP), f32),
            pltpu.VMEM((4, 2, 2, *block), bf16),
            pltpu.VMEM((BLK, d), bf16),
            pltpu.VMEM((BLK, d), bf16),
            pltpu.VMEM((BLK, d), f32),
            pltpu.VMEM(early_part, bf16),
            pltpu.VMEM(early_part, bf16),
            pltpu.VMEM((4, 2, *block), bf16),
            pltpu.VMEM((4, 2, *block), bf16),
            pltpu.VMEM((4, *block), bf16),
            pltpu.VMEM((4, *block), bf16),
            pltpu.VMEM((3, *block), bf16),
            pltpu.VMEM(block, bf16),
            pltpu.VMEM(block, bf16),
            pltpu.VMEM((BLK, d), bf16),
            pltpu.VMEM((BLK, d), bf16),
            pltpu.VMEM(small, f32),
            pltpu.VMEM(small, f32),
            pltpu.VMEM(small, f32),
            pltpu.VMEM(small, f32),
            pltpu.VMEM(small, f32),
            pltpu.VMEM(small, f32),
            pltpu.VMEM((4, *small), f32),
            pltpu.VMEM(small, f32),
            pltpu.SemaphoreType.DMA((copies,)),
            pltpu.SemaphoreType.DMA((copies,)),
            pltpu.SemaphoreType.DMA((2,)),
        ],
        compiler_params=pltpu.CompilerParams(
            vmem_limit_bytes=VMEM_LIMIT, collective_id=0, has_side_effects=True
        ),
        cost_estimate=pl.CostEstimate(flops=30_000_000_000, bytes_accessed=100_000_000, transcendentals=0),
        name="last",
    )(q, k, v, do, o, inverse, expo, cos, sin, w, hidden_t, g_sum, gb_sum, dq_far, g_out, part, tokens, gain, mid,
      small_w, small_two, g_bup, early)


def finish_kernel(x_ref, gain, mid_ref, own_ref, part_ref, out_ref, small):
    out, first, second = finish_rows(
        x_ref[...], wide(gain), mid_ref[...], own_ref[...] + part_ref[...].astype(f32)
    )
    out_ref[...] = out
    small[...] = jnp.concatenate([lines(first), lines(second)], 0)


def finish(x, gain, mid, own, part):
    d = x.shape[1]
    return pl.pallas_call(
        finish_kernel,
        out_shape=[jax.ShapeDtypeStruct(x.shape, bf16), jax.ShapeDtypeStruct((2 * d // GROUP, GROUP), f32)],
        compiler_params=pltpu.CompilerParams(vmem_limit_bytes=VMEM_LIMIT),
        name="finish",
    )(x, gain, mid, own, part)


def place_pieces(places, pieces, out_ref, sem):
    mp = lax.axis_index("mp")
    copies = []
    for n, (piece, (zero, one)) in enumerate(zip(pieces, places)):
        start = pl.multiple_of((zero + (one - zero) * mp) * BLK, BLK)
        copies.append(pltpu.make_async_copy(piece, out_ref.at[pl.ds(start, piece.shape[0]), :], sem.at[n]))
        copies[-1].start()
    return copies


def assemble_kernel(places, *rest):
    count = len(places)
    for made in place_pieces(places, rest[:count], rest[count], rest[-1]):
        made.wait()


def assemble(places, pieces, rows):
    count = len(pieces)
    return pl.pallas_call(
        functools.partial(assemble_kernel, places),
        in_specs=[pl.BlockSpec(memory_space=pltpu.VMEM)] * count,
        out_specs=pl.BlockSpec(memory_space=pl.ANY),
        out_shape=jax.ShapeDtypeStruct((rows, pieces[0].shape[1]), pieces[0].dtype),
        scratch_shapes=[pltpu.SemaphoreType.DMA((count,))],
        compiler_params=pltpu.CompilerParams(vmem_limit_bytes=VMEM_LIMIT),
        cost_estimate=pl.CostEstimate(flops=0, bytes_accessed=8_000_000, transcendentals=0),
        name="assemble",
    )(*pieces)


def one_line(v):
    return jnp.concatenate([v[j : j + 1] for j in range(v.shape[0])], 1)


def conclude_kernel(
    share, half, hidden, places, late, late_theirs, early, early_theirs, small, small_theirs, p0, p1, p2, p3,
    g_qkv, g_up, g_down, g_out, g_bqkv, g_bup, grad, *rest,
):
    vectors, sem = rest[:-1], rest[-1]
    copies = place_pieces(places, (p0, p1, p2, p3), grad, sem)
    groups = late.shape[0]
    d = groups * GROUP
    whole = half // GROUP
    for s in range(4):
        rows = slice(s * share, (s + 1) * share)
        mine = [late[g].astype(f32)[rows] for g in range(whole + 1)]
        other = [late_theirs[g].astype(f32)[rows] for g in range(whole, groups)]
        both = jnp.concatenate(mine, 1)[:, :half] + jnp.concatenate(other, 1)[:, half - whole * GROUP :]
        if s < 3:
            g_qkv[s] = both
        else:
            g_out[...] = both
    width = 256
    for c in range(hidden // width):
        mine = early[:, 2 * c * width : 2 * (c + 1) * width].astype(f32)
        other = early_theirs[:share, 2 * c * width : 2 * (c + 1) * width].astype(f32)
        both = mine + other
        cols = slice(c * width, (c + 1) * width)
        g_up[:, cols] = both[:, :width]
        g_down[:, cols] = both[:, width:]
    per = d // GROUP
    for n, ref in enumerate(vectors):
        ref[...] = one_line(small[n * per : (n + 1) * per] + small_theirs[n * per : (n + 1) * per])[0]
    base = 6 * per
    for s in range(3):
        rows = slice(base + s * per, base + (s + 1) * per)
        g_bqkv[s : s + 1, :] = one_line(small[rows])[:, :half] + one_line(small_theirs[rows])[:, half:]
    base += 3 * per
    count = hidden // GROUP
    g_bup[...] = one_line(small[base : base + count] + small_theirs[base + count : base + 2 * count])[0]
    for made in copies:
        made.wait()


def conclude(share, half, hidden, places, args, pieces, rows):
    d = 2 * half
    vmem = pl.BlockSpec(memory_space=pltpu.VMEM)
    return pl.pallas_call(
        functools.partial(conclude_kernel, share, half, hidden, places),
        in_specs=[vmem] * (len(args) + len(pieces)),
        out_specs=[vmem] * 6 + [pl.BlockSpec(memory_space=pl.ANY)] + [vmem] * 6,
        out_shape=[
            jax.ShapeDtypeStruct((3, share, half), f32),
            jax.ShapeDtypeStruct((share, hidden), f32),
            jax.ShapeDtypeStruct((share, hidden), f32),
            jax.ShapeDtypeStruct((share, half), f32),
            jax.ShapeDtypeStruct((3, half), f32),
            jax.ShapeDtypeStruct((hidden,), f32),
            jax.ShapeDtypeStruct((rows, d), bf16),
        ]
        + [jax.ShapeDtypeStruct((d,), f32)] * 6,
        scratch_shapes=[pltpu.SemaphoreType.DMA((len(pieces),))],
        compiler_params=pltpu.CompilerParams(vmem_limit_bytes=VMEM_LIMIT),
        cost_estimate=pl.CostEstimate(flops=1_000_000, bytes_accessed=12_000_000, transcendentals=0),
        name="conclude",
    )(*args, *pieces)


def on_device(
    tokens, lengths, gain_one, shift_one, w_qkv, b_qkv, w_out, b_out, gain_two, shift_two, w_up, b_up, w_down, b_down,
    cotangent,
):
    d = tokens.shape[1]
    n_dp = lax.axis_size("dp")
    swap = [(0, 1), (1, 0)]
    half = w_qkv.shape[2]
    hidden = w_up.shape[1]

    groups = d // GROUP
    share = d // n_dp
    by_hand = n_dp == 16
    tables = tuple(jnp.asarray(t) for t in rope_tables())
    *attended, q, k, v, hidden_t, w_all, w_out_other, up_other, down_other, b_up_all, sc, near_cos, near_sin = front(
        lengths, gain_one, shift_one, b_qkv, b_up, *tables, jnp.transpose(w_qkv, (0, 2, 1)), tokens, w_out, w_up, w_down
    )
    qkv = (q, k, v)
    out_own, grad_mid, do, g_early, g_out, g_bup, small_two = middle(
        sc, tokens, cotangent, attended[0], w_out, w_out_other, b_out, gain_two, shift_two,
        w_up, w_down, up_other, down_other, b_up_all, b_down,
    )
    early = lax.psum_scatter(g_early, "dp", scatter_dimension=0, tiled=True)

    theirs = lax.ppermute(out_own, "mp", swap)
    out_tokens = assemble(((0, 3), (3, 0)), [out_own, theirs], 6 * BLK)
    args = (sc, *qkv, do, *attended, *tables, w_all, hidden_t)
    g_sum, gb_sum, grad_whole, small_w = back("whole", *args, (tokens, gain_one, grad_mid))
    whole_theirs = lax.ppermute(grad_whole, "mp", swap)
    g_sum, gb_sum, dq_far, part = back("far", *args, (g_sum, gb_sum))
    if by_hand:
        part, out_tokens, whole_theirs, early = lax.optimization_barrier((part, out_tokens, whole_theirs, early))
        late, late_theirs, small, small_theirs, shared, shared_theirs, early_theirs = last(
            *args[1:8], near_cos, near_sin, *args[10:], g_sum, gb_sum, dq_far, g_out, part, tokens, gain_one, grad_mid,
            small_w, small_two, g_bup, early,
        )
    else:
        arrived = lax.ppermute(part, "mp", swap)
        g_qkv, g_bqkv, own = back("near", *args, (g_sum, gb_sum, dq_far))
        x_shared = lax.dynamic_slice_in_dim(tokens, sc[BLOCK + 2] * BLK, BLK, 0)
        shared, last_sums = finish(x_shared, gain_one, grad_mid[2 * BLK :], own, arrived)
        g_bqkv = g_bqkv.reshape(groups, 3, GROUP).transpose(1, 0, 2)
        small = jnp.concatenate(
            [
                small_w[:2].reshape(-1, GROUP) + last_sums,
                small_two[:4].reshape(-1, GROUP),
                g_bqkv.reshape(-1, GROUP),
                g_bup.reshape(-1, GROUP),
            ]
        )
        n_small = small.shape[0]
        shared_theirs = lax.ppermute(shared, "mp", swap)
        g_qkv = g_qkv.reshape(groups, d, 3, GROUP).transpose(2, 1, 0, 3).reshape(3, d, d)
        late = lax.psum_scatter(g_qkv, "dp", scatter_dimension=1, tiled=True)
        late_theirs = lax.ppermute(late, "mp", swap)
        small = lax.psum(small, "dp")
        small_theirs = lax.ppermute(small, "mp", swap)
        early_theirs = lax.ppermute(early[:, 2 * hidden :], "mp", swap)
    places = ((0, 4), (2, 3), (3, 2), (4, 0))
    pieces = [grad_whole, shared, shared_theirs, whole_theirs]

    if by_hand:
        g_w, g_up, g_down, g_out, g_bq, g_bu, grad_tokens, *vectors = conclude(
            share, half, hidden, places,
            (late, late_theirs, early, early_theirs, small, small_theirs), pieces, 6 * BLK,
        )
        g_down, g_out = g_down.T, g_out.T
    else:
        grad_tokens = assemble(places, pieces, 6 * BLK)
        mlp = early[:, : 2 * hidden].astype(f32) + early_theirs[:, : 2 * hidden].astype(f32)
        mlp = mlp.reshape(share, hidden // 256, 2, 256)
        g_up = mlp[:, :, 0].reshape(share, hidden)
        g_down = mlp[:, :, 1].reshape(share, hidden).T
        g_out = lax.psum_scatter(g_out, "dp", scatter_dimension=0, tiled=True)
        out_theirs = lax.ppermute(g_out[:, half:], "mp", swap)
        g_out = (g_out[:, :half].astype(f32) + out_theirs.astype(f32)).T
        g_w = late[:, :, :half].astype(f32) + late_theirs[:, :, half:].astype(f32)
        mine, others = small[:n_small].reshape(-1), small_theirs[:n_small].reshape(-1)
        vectors = list((mine[: 6 * d] + others[: 6 * d]).reshape(6, d))
        pair = lambda v, lo, n, w: v[lo : lo + 2 * n * w].reshape(n, 2, w)
        g_bq = pair(mine, 6 * d, 3, half)[:, 0] + pair(others, 6 * d, 3, half)[:, 1]
        g_bu = pair(mine, 9 * d, 1, hidden)[0, 0] + pair(others, 9 * d, 1, hidden)[0, 1]
    return (
        out_tokens,
        grad_tokens,
        vectors[0],
        vectors[1],
        g_w,
        g_bq,
        g_out,
        vectors[4],
        vectors[2],
        vectors[3],
        g_up,
        g_bu,
        g_down,
        vectors[5],
    )


def solution(mesh):
    in_specs = (
        P("dp", None),
        P("dp", None),
        P(),
        P(),
        P(None, None, "mp"),
        P(None, "mp"),
        P("mp", None),
        P(),
        P(),
        P(),
        P(None, "mp"),
        P("mp"),
        P("mp", None),
        P(),
        P("dp", None),
    )
    out_specs = (
        P("dp", None),
        P("dp", None),
        P(),
        P(),
        P(None, "dp", "mp"),
        P(None, "mp"),
        P("mp", "dp"),
        P(),
        P(),
        P(),
        P("dp", "mp"),
        P("mp"),
        P("mp", "dp"),
        P(),
    )
    return jax.shard_map(on_device, mesh=mesh, in_specs=in_specs, out_specs=out_specs, check_vma=False)
```

```python
import functools

import jax
import jax.numpy as jnp
import numpy as np
from jax import lax
from jax.experimental import pallas as pl
from jax.experimental.pallas import tpu as pltpu
from jax.sharding import PartitionSpec as P

HD = 32
LONG = 1024
BLK = 512
GROUP = 128
epsilon = 1e-05
rotary_base = 10000.0
log2_e = 1.4426950408889634
ln_2 = 0.6931471805599453

f32 = jnp.float32
bf16 = jnp.bfloat16
NT = (((1,), (1,)), ((), ()))
NN = (((1,), (0,)), ((), ()))
TN = (((0,), (0,)), ((), ()))
VMEM_LIMIT = 60 << 20


def dot(a, b, dims=NN):
    return lax.dot_general(a, b, dims, preferred_element_type=f32)


def rope_tables():
    place = np.arange(LONG, dtype=np.float64)[:, None]
    frequency = rotary_base ** (-np.arange(HD // 2, dtype=np.float64) * 2.0 / HD)
    angles = place * frequency[None, :]
    cosines = np.concatenate([np.cos(angles), np.cos(angles)], 1)
    sines = np.concatenate([-np.sin(angles), np.sin(angles)], 1)
    repeat = GROUP // HD
    return (
        np.tile(cosines, (1, repeat)).astype(np.float32),
        np.tile(sines, (1, repeat)).astype(np.float32),
    )


def swap_halves(x):
    lane = lax.broadcasted_iota(jnp.int32, (1, GROUP), 1)
    low = (lane // (HD // 2)) % 2 == 0
    return jnp.where(low, pltpu.roll(x, GROUP - HD // 2, 1), pltpu.roll(x, HD // 2, 1))


def rotate(x, cosines, sines):
    return x * cosines + swap_halves(x) * sines


def rotate_back(x, cosines, sines):
    return x * cosines - swap_halves(x) * sines


def normalize(values):
    centred = values - jnp.mean(values, -1, keepdims=True)
    inverse = lax.rsqrt(jnp.mean(centred * centred, -1, keepdims=True) + epsilon)
    return (centred * inverse, inverse)


def normalize_back(normed, inverse, grad_normed):
    mean_grad = jnp.mean(grad_normed, -1, keepdims=True)
    mean_proj = jnp.mean(grad_normed * normed, -1, keepdims=True)
    return inverse * (grad_normed - mean_grad - normed * mean_proj)


FLAG, BLOCK, TABLE, PLACE = 0, 3, 7, 11


def wide(ref):
    return ref[...].astype(f32)[None]


def attend_body(q, k_ref, v_ref, o_ref, l_ref, e_ref, store, bias):
    lane = lax.broadcasted_iota(jnp.int32, (1, GROUP), 1) // HD
    heads = GROUP // HD
    count = k_ref.shape[0]
    chunks = count // BLK
    values_t = v_ref[...].T
    ones = jnp.ones((16, count), bf16)
    outs, inverses = [], []

    def score(h, c):
        keys = k_ref[c * BLK : (c + 1) * BLK, :]
        scores = dot(jnp.where(lane == h, keys, jnp.zeros_like(keys)), q, NT)
        store[h % 2, c * BLK : (c + 1) * BLK, :] = scores
        return jnp.max(scores.reshape(BLK // 8, 8, BLK), axis=0) + bias[c]

    def score_max(h, c, so_far):
        found = score(h, c)
        return found if so_far is None else jnp.maximum(so_far, found)

    top = None
    for c in range(chunks):
        top = score_max(0, c, top)
    row_max = jnp.max(top, axis=0, keepdims=True)
    for h in range(heads):
        top = None
        total = None
        stacked = jnp.concatenate([values_t[HD * h : HD * (h + 1)], ones], 0)
        for c in range(chunks):
            if h + 1 < heads:
                top = score_max(h + 1, c, top)
            rows = slice(c * BLK, (c + 1) * BLK)
            expo = jnp.exp2(store[h % 2, rows, :] - (row_max - bias[c])).astype(bf16)
            e_ref[h, rows, :] = expo
            part = dot(stacked[:, rows], expo)
            total = part if total is None else total + part
        inverse = 1.0 / total[HD : HD + 1]
        outs.append(total[:HD] * inverse)
        inverses.append(jnp.broadcast_to(inverse, (HD, BLK)))
        if h + 1 < heads:
            row_max = jnp.max(top, axis=0, keepdims=True)
    o_ref[...] = jnp.concatenate(outs, 0).T.astype(bf16)
    l_ref[...] = jnp.concatenate(inverses, 0).T


def front_kernel(
    first, lengths, gain, shift, b_own, b_up, cos, sin, w_own, tokens, w_out, w_up, w_down,
    o_ref, l_ref, e_ref, q_out, k_out, v_out, ht_out, w_all, out_other, up_other, down_other, b_all, sc, near_cos, near_sin,
    store, x_all, hidden, q_all, k_all, v_all, ht, w_in, b_mine, b_in, local, send, recv,
):
    g, b = pl.program_id(0), pl.program_id(1)
    step = 3 * g + b
    here = lax.axis_index("dp")
    mp = lax.axis_index("mp")
    c = here % 2
    x = (here // 2) % 2
    core = (here + 1 - 2 * c, mp)
    side = (here + 2 - 4 * x, mp)
    across = (here, 1 - mp)
    groups = q_all.shape[0]
    half = w_own.shape[1]
    side_long = (lengths[0, 4 * mp] == LONG).astype(jnp.int32)
    mid_long = (lengths[0, 2] == LONG).astype(jnp.int32)
    table = [0, side_long, mp * mid_long, (1 - mp) * mid_long]
    numbers = {}

    def copy(name, src, dst, dev):
        n = numbers.setdefault(name, len(numbers))
        return pltpu.make_async_remote_copy(
            src_ref=src,
            dst_ref=dst,
            send_sem=send.at[n],
            recv_sem=recv.at[n],
            device_id=dev,
            device_id_type=pl.DeviceIdType.MESH,
        )

    def quarter(ref, n):
        size = ref.shape[0] // 4
        return ref.at[pl.ds(pl.multiple_of(n * size, size), size), :]

    share = half // 2
    mine = pl.ds(pl.multiple_of(c * share, share), share)
    w_across = copy("w", w_own.at[:, mine, :], w_in.at[:, mine, :], across)
    w_core = copy("wc", w_in.at[:, mine, :], w_in.at[:, mine, :], core)
    b_across = copy("b", b_mine, b_in, across)
    out_across = copy("o", w_out, out_other, across)
    n_mine, n_side = 2 * x + c, 2 * (1 - x) + c
    pairs = ((w_up, up_other), (w_down, down_other))
    by_across = [copy(("y", n), quarter(a, n_mine), quarter(to, n_mine), across) for n, (a, to) in enumerate(pairs)]
    by_side = [copy(("x", n), quarter(to, n_mine), quarter(to, n_mine), side) for n, (_, to) in enumerate(pairs)]
    by_core = [
        copy(("c", n, m), quarter(to, at), quarter(to, at), core)
        for n, (_, to) in enumerate(pairs)
        for m, at in enumerate((n_mine, n_side))
    ]
    block = lambda at, count: pl.ds(pl.multiple_of(at * BLK, BLK), count * BLK)
    x_copies = [
        pltpu.make_async_copy(tokens.at[block(at, count), :], x_all.at[to * BLK : (to + count) * BLK, :], local.at[n])
        for n, (at, to, count) in enumerate(((4 * mp, 0, 2), (2 + mp, 2, 1), (3 - mp, 3, 1)))
    ]
    w_copies = [
        pltpu.make_async_copy(w_own, w_all.at[:, :half, :], local.at[3]),
        pltpu.make_async_copy(w_in, w_all.at[:, half:, :], local.at[4]),
    ]
    ht_copy = pltpu.make_async_copy(ht, ht_out, local.at[5])

    def qkv_copies(lo, hi, n):
        return [
            pltpu.make_async_copy(a.at[lo:hi], out.at[lo:hi], local.at[n + m])
            for m, (a, out) in enumerate(((q_all, q_out), (k_all, k_out), (v_all, v_out)))
        ]

    early, late = qkv_copies(0, first, 6), qkv_copies(first, groups, 9)

    def table_rows(i):
        chosen = jnp.full((1, GROUP), table[i], jnp.int32) > 0
        return jnp.where(chosen, cos[BLK:, :], cos[:BLK, :]), jnp.where(chosen, sin[BLK:, :], sin[:BLK, :])

    def project(w, bias, lo, hi):
        count = hi - lo
        for i in range(4):
            rows = slice(i * BLK, (i + 1) * BLK)
            out = dot(hidden[rows, :], w, NT)
            cosines, sines = table_rows(i)
            for s in range(3):
                for n in range(count):
                    at = (s * count + n) * GROUP
                    part = out[:, at : at + GROUP] + bias[s : s + 1, n * GROUP : (n + 1) * GROUP]
                    if s == 0:
                        part = rotate(part, cosines, sines) * (HD ** (-0.5) * log2_e)
                        q_all[lo + n, rows, :] = part.astype(bf16)
                    elif s == 1:
                        k_all[lo + n, rows, :] = rotate(part, cosines, sines).astype(bf16)
                    else:
                        v_all[lo + n, rows, :] = part.astype(bf16)

    @pl.when(step == 0)
    def _():
        for made in x_copies:
            made.start()
        scalars = [side_long, side_long, mid_long, 4 * mp, 4 * mp + 1, 2 + mp, 3 - mp, *table, mp, 1 + mp, 2 - 2 * mp]
        for n, value in enumerate(scalars):
            sc[n] = value
        b_mine[...] = jnp.zeros_like(b_mine)
        b_mine[:3, :half] = b_own[...].astype(f32)
        b_mine[3:4, :] = wide(b_up)
        barrier = pltpu.get_barrier_semaphore()
        for dev in (across, core, side):
            pl.semaphore_signal(barrier, inc=1, device_id=dev, device_id_type=pl.DeviceIdType.MESH)
        pl.semaphore_wait(barrier, 3)
        w_across.start()
        b_across.start()
        for made in x_copies:
            made.wait()
        for i in range(4):
            rows = slice(i * BLK, (i + 1) * BLK)
            normed, _ = normalize(x_all[rows, :].astype(f32))
            fresh = (normed * wide(gain) + wide(shift)).astype(bf16)
            hidden[rows, :] = fresh
            ht[:, rows] = fresh.T
        ht_copy.start()
        w_copies[0].start()
        near_cos[...], near_sin[...] = table_rows(2)
        w = jnp.concatenate([w_own[s, : first * GROUP, :] for s in range(3)], 0)
        project(w, b_mine[:3, : first * GROUP], 0, first)
        for made in early:
            made.start()

    @pl.when(step == 3)
    def _():
        w_across.wait()
        w_core.start()
        b_across.wait()
        by_across[0].start()

    @pl.when(step == 3 * first)
    def _():
        by_across[1].start()
        w_core.wait()
        w_copies[1].start()
        tail = first * GROUP
        w = jnp.concatenate([part for s in range(3) for part in (w_own[s, tail:, :], w_in[s])], 0)
        bias = jnp.concatenate([b_mine[:3, tail:half], b_in[:3, :half]], 1)
        project(w, bias, first, groups)
        for made in late:
            made.start()

    @pl.when(step == 3 * first + 1)
    def _():
        by_across[0].wait()
        by_side[0].start()

    @pl.when(step == 3 * first + 2)
    def _():
        by_across[1].wait()
        by_side[1].start()
        out_across.start()

    @pl.when(step == 3 * first + 6)
    def _():
        by_side[0].wait()
        for made in by_core[:2]:
            made.start()

    @pl.when(step == 3 * groups - 1)
    def _():
        by_side[1].wait()
        for made in by_core[2:]:
            made.start()

    keys = pl.ds(pl.multiple_of(b // 2 * LONG, LONG), LONG)
    q = q_all[g, pl.ds(pl.multiple_of(b * BLK, BLK), BLK), :]
    refs = (q, k_all.at[g, keys, :], v_all.at[g, keys, :], o_ref, l_ref, e_ref, store)
    off = lambda allowed: jnp.where(allowed, 0.0, -1e30).astype(f32)

    @pl.when(b != 2)
    def _():
        attend_body(*refs, [off((b == n) | (side_long == 1)) for n in range(2)])

    @pl.when(b == 2)
    def _():
        attend_body(*refs, [off(True), off(mid_long == 1)])

    @pl.when(step == 3 * groups - 1)
    def _():
        b_all[:, : b_mine.shape[1]] = b_mine[3:4, :]
        b_all[:, b_mine.shape[1] :] = b_in[3:4, :]
        out_across.wait()
        for made in by_core:
            made.wait()
        for made in (*early, *late, *w_copies, ht_copy):
            made.wait()


def front(lengths, gain, shift, b_own, b_up, cos, sin, w_own, tokens, w_out, w_up, w_down):
    d = tokens.shape[1]
    groups = d // GROUP
    heads = GROUP // HD
    half = w_own.shape[1]
    own, rows = 3 * BLK, 4 * BLK
    one = pl.Buffered(buffer_count=1)
    whole = lambda a: pl.BlockSpec(a.shape, lambda g, b: (0,) * a.ndim, pipeline_mode=one)
    os = pl.BlockSpec((None, BLK, GROUP), lambda g, b: (g, b, 0))
    es = pl.BlockSpec((heads, LONG, BLK), lambda g, b: (g * 3 + b, 0, 0))
    hbm = pl.BlockSpec(memory_space=pl.ANY)
    held = jax.ShapeDtypeStruct((groups, rows, GROUP), bf16)
    copies = 2 + 2 + 2 + 2 + 4
    return pl.pallas_call(
        functools.partial(front_kernel, half // GROUP),
        grid=(groups, 3),
        in_specs=[pl.BlockSpec(memory_space=pltpu.SMEM)]
        + [whole(a) for a in (gain, shift, b_own, b_up, cos, sin, w_own)]
        + [hbm] * 4,
        out_specs=[os, os, es]
        + [hbm] * 8
        + [pl.BlockSpec((1, 2 * b_up.shape[0]), lambda g, b: (0, 0)), pl.BlockSpec(memory_space=pltpu.SMEM)]
        + [pl.BlockSpec((BLK, GROUP), lambda g, b: (0, 0))] * 2,
        out_shape=[
            jax.ShapeDtypeStruct((groups, own, GROUP), bf16),
            jax.ShapeDtypeStruct((groups, own, GROUP), f32),
            jax.ShapeDtypeStruct((groups * 3 * heads, LONG, BLK), bf16),
            held,
            held,
            held,
            jax.ShapeDtypeStruct((d, rows), bf16),
            jax.ShapeDtypeStruct((3, 2 * half, d), bf16),
            jax.ShapeDtypeStruct(w_out.shape, bf16),
            jax.ShapeDtypeStruct(w_up.shape, bf16),
            jax.ShapeDtypeStruct(w_down.shape, bf16),
            jax.ShapeDtypeStruct((1, 2 * b_up.shape[0]), f32),
            jax.ShapeDtypeStruct((14,), jnp.int32),
            jax.ShapeDtypeStruct((BLK, GROUP), f32),
            jax.ShapeDtypeStruct((BLK, GROUP), f32),
        ],
        scratch_shapes=[
            pltpu.VMEM((2, LONG, BLK), f32),
            pltpu.VMEM((rows, d), bf16),
            pltpu.VMEM((rows, d), bf16),
            pltpu.VMEM((groups, rows, GROUP), bf16),
            pltpu.VMEM((groups, rows, GROUP), bf16),
            pltpu.VMEM((groups, rows, GROUP), bf16),
            pltpu.VMEM((d, rows), bf16),
            pltpu.VMEM(w_own.shape, bf16),
            pltpu.VMEM((8, b_up.shape[0]), f32),
            pltpu.VMEM((8, b_up.shape[0]), f32),
            pltpu.SemaphoreType.DMA((12,)),
            pltpu.SemaphoreType.DMA((copies,)),
            pltpu.SemaphoreType.DMA((copies,)),
        ],
        compiler_params=pltpu.CompilerParams(
            vmem_limit_bytes=VMEM_LIMIT, collective_id=1, has_side_effects=True
        ),
        cost_estimate=pl.CostEstimate(
            flops=50_000_000_000, bytes_accessed=100_000_000, transcendentals=31_000_000
        ),
        name="front",
    )(lengths, gain, shift, b_own, b_up, cos, sin, w_own, tokens, w_out, w_up, w_down)


def attend_back_body(
    q_ref, k_ref, v_ref, do_ref, o_ref, l_ref, e_ref, prod, dk_sum, dv_sum, start, count
):
    lane = lax.broadcasted_iota(jnp.int32, (1, GROUP), 1) // HD
    heads = GROUP // HD
    q = q_ref[...]
    do = (do_ref[...].astype(f32) * l_ref[...]).astype(bf16)
    both = do.astype(f32) * o_ref[...].astype(f32)
    upper = both.astype(bf16)
    lower = (both - upper.astype(f32)).astype(bf16)
    pick = (
        lax.broadcasted_iota(jnp.int32, (8, GROUP), 0)
        == lax.broadcasted_iota(jnp.int32, (8, GROUP), 1) // HD
    )
    pick = pick.astype(f32).astype(bf16)
    delta = dot(pick, upper, NT) + dot(pick, lower, NT)
    keys_t = k_ref[pl.ds(start, count), :].T
    chunks = count // BLK
    tiles = [(h, c) for h in range(heads) for c in range(chunks)]

    def grad_probs(i):
        h, c = tiles[i]
        values = v_ref[pl.ds(start + c * BLK, BLK), :]
        prod[i % 2] = dot(jnp.where(lane == h, values, jnp.zeros_like(values)), do, NT)

    grad_probs(0)
    dq_t = [None] * heads
    for i, (h, c) in enumerate(tiles):
        if i + 1 < len(tiles):
            grad_probs(i + 1)
        rows = pl.ds(start + c * BLK, BLK)
        expo = e_ref[h, rows, :]
        ds = (expo.astype(f32) * (prod[i % 2] - delta[h : h + 1])).astype(bf16)
        dv_sum[rows, :] += dot(expo, jnp.where(lane == h, do, jnp.zeros_like(do)))
        dk_sum[rows, :] += dot(ds, jnp.where(lane == h, q, jnp.zeros_like(q)))
        part = dot(keys_t[HD * h : HD * (h + 1), c * BLK : (c + 1) * BLK], ds)
        dq_t[h] = part if dq_t[h] is None else dq_t[h] + part
    return jnp.concatenate(dq_t, 0).T


def window_back(dq, dk_sum, dv_sum, tables, w_ref, ht_ref, dh_sum):
    parts = [] if dq is None else [dq]
    dk = dk_sum[...] * ln_2
    rotated = []
    for n, (cos, sin) in enumerate(tables):
        rotated.append(rotate_back(dk[n * BLK : (n + 1) * BLK], cos[...], sin[...]))
    parts.append(jnp.concatenate(rotated, 0).astype(bf16))
    parts.append(dv_sum[...].astype(bf16))
    both = jnp.concatenate(parts, 1)
    w = jnp.concatenate([w_ref[s] for s in range(3 - len(parts), 3)], 0)
    for n in range(len(tables)):
        rows = slice(n * BLK, (n + 1) * BLK)
        dh_sum[rows, :] += dot(both[rows], w)
    return dot(ht_ref[...], both), jnp.sum(both.astype(f32), 0, keepdims=True)


def back_kernel(
    mode, sc, q_ref, k_ref, v_ref, do_ref, o_ref, l_ref, e_ref, cos, sin, cos0, sin0, cos1, sin1, w_ref, ht_ref,
    *rest,
):
    g = pl.program_id(0)
    last_g = pl.num_programs(0) - 1
    step = pl.program_id(1)
    if mode == "whole":
        x_ref, gain, mid_ref, g_ref, gb_ref, out_ref, small, dq_cat, prod, dk_sum, dv_sum, dh_sum = rest
    elif mode == "far":
        before, before_b, g_ref, gb_ref, dq_out, part_ref, prod, dk_sum, dv_sum, dh_sum = rest
    else:
        before, before_b, dq_in, g_ref, gb_ref, own_ref, prod, dk_sum, dv_sum, dh_sum = rest
    refs = (q_ref, k_ref, v_ref, do_ref, o_ref, l_ref, e_ref, prod, dk_sum, dv_sum)
    own_tables = (cos0, sin0), (cos1, sin1)
    finish_q = lambda dq: rotate_back(dq * (HD ** (-0.5)), cos[...], sin[...]).astype(bf16)

    @pl.when(step == 0)
    def _():
        dk_sum[...] = jnp.zeros_like(dk_sum)
        dv_sum[...] = jnp.zeros_like(dv_sum)

    @pl.when((step == 0) & (g == 0))
    def _():
        dh_sum[...] = jnp.zeros_like(dh_sum)

    if mode == "whole":
        place = pl.ds(pl.multiple_of(step * BLK, BLK), BLK)

        @pl.when(sc[FLAG] == 1)
        def _():
            dq_cat[place, :] = finish_q(attend_back_body(*refs, 0, LONG))

        @pl.when(sc[FLAG] == 0)
        def _():
            dq_cat[place, :] = finish_q(attend_back_body(*refs, pl.multiple_of(step * BLK, BLK), BLK))

        @pl.when(step == 1)
        def _():
            g_ref[...], gb_ref[...] = window_back(
                dq_cat[...], dk_sum, dv_sum, own_tables, w_ref, ht_ref, dh_sum
            )

        @pl.when((step == 1) & (g == last_g))
        def _():
            sums = [None, None]
            for rows in (slice(0, BLK), slice(BLK, LONG)):
                out, *terms = finish_rows(x_ref[rows, :], wide(gain), mid_ref[rows, :], dh_sum[rows, :])
                out_ref[rows, :] = out
                for n, term in enumerate(terms):
                    sums[n] = term if sums[n] is None else sums[n] + term
            small[...] = jnp.concatenate(sums + [jnp.zeros_like(sums[0])] * 6, 0)

    elif mode == "far":

        @pl.when(sc[FLAG + 2] == 1)
        def _():
            dq_out[...] = attend_back_body(*refs, 0, BLK)

        @pl.when(sc[FLAG + 2] == 0)
        def _():
            dq_out[...] = jnp.zeros_like(dq_out)

        weight, bias = window_back(None, dk_sum, dv_sum, own_tables[:1], w_ref, ht_ref, dh_sum)
        g_ref[:, :GROUP] = before[:, :GROUP]
        g_ref[:, GROUP:] = before[:, GROUP:] + weight
        gb_ref[:, :GROUP] = before_b[:, :GROUP]
        gb_ref[:, GROUP:] = before_b[:, GROUP:] + bias

        @pl.when(g == last_g)
        def _():
            part_ref[...] = dh_sum[...].astype(bf16)

    else:
        dq = finish_q(attend_back_body(*refs, 0, BLK) + dq_in[...])
        weight, bias = window_back(dq, dk_sum, dv_sum, own_tables[:1], w_ref, ht_ref, dh_sum)
        weight = weight + before[...]
        gb_ref[...] = bias + before_b[...]
        g_ref[...] = weight.astype(bf16)

        @pl.when(g == last_g)
        def _():
            own_ref[...] = dh_sum[...]


def back(mode, sc, q, k, v, do, o, inverse, expo, cos, sin, w, hidden_t, more):
    groups = o.shape[0]
    d = w.shape[2]
    heads = GROUP // HD
    blocks = 2 if mode == "whole" else 1
    query = 0 if mode == "whole" else 2
    key = {"whole": 0, "far": 3, "near": 2}[mode]
    keys = LONG if mode == "whole" else BLK
    one = pl.Buffered(buffer_count=1)
    qs = pl.BlockSpec((None, BLK, GROUP), lambda g, b, s: (g, b + query, 0))
    ks = pl.BlockSpec((None, keys, GROUP), lambda g, b, s: (g, key, 0))
    os = pl.BlockSpec((None, BLK, GROUP), lambda g, b, s: (g, b + query, 0))
    es = pl.BlockSpec((heads, keys, BLK), lambda g, b, s: (g * 3 + b + query, 1 if mode == "far" else 0, 0))
    tq = pl.BlockSpec((BLK, GROUP), lambda g, b, s: (s[TABLE + b + query], 0))
    t0 = pl.BlockSpec((BLK, GROUP), lambda g, b, s: (s[TABLE + key], 0))
    t1 = pl.BlockSpec((BLK, GROUP), lambda g, b, s: (s[TABLE + key + (blocks - 1)], 0))
    weight = pl.BlockSpec((None, d, 3 * GROUP), lambda g, b, s: (g, 0, 0))
    bias = pl.BlockSpec((None, 1, 3 * GROUP), lambda g, b, s: (g, 0, 0))
    dq_part = pl.BlockSpec((None, BLK, GROUP), lambda g, b, s: (g, 0, 0))
    whole = lambda *shape: pl.BlockSpec(shape, lambda g, b, s: (0, 0))
    in_specs = [qs, ks, ks, os, os, os, es, tq, tq, t0, t0, t1, t1]
    in_specs += [
        pl.BlockSpec((3, GROUP, d), lambda g, b, s: (0, g, 0)),
        pl.BlockSpec((d, keys), lambda g, b, s: (0, key), pipeline_mode=one),
    ]
    bias_shape = jax.ShapeDtypeStruct((groups, 1, 3 * GROUP), f32)
    scratch = [
        pltpu.VMEM((2, BLK, BLK), f32),
        pltpu.VMEM((keys, GROUP), f32),
        pltpu.VMEM((keys, GROUP), f32),
        pltpu.VMEM((keys, d), f32),
    ]
    if mode == "whole":
        in_specs += [
            pl.BlockSpec((LONG, d), lambda g, b, s: (s[BLOCK] // 2, 0), pipeline_mode=one),
            pl.BlockSpec((d,), lambda g, b, s: (0,)),
            pl.BlockSpec((LONG, d), lambda g, b, s: (0, 0), pipeline_mode=one),
        ]
        out_specs = [weight, bias, whole(LONG, d), whole(8, d)]
        out_shape = [
            jax.ShapeDtypeStruct((groups, d, 3 * GROUP), f32),
            bias_shape,
            jax.ShapeDtypeStruct((LONG, d), bf16),
            jax.ShapeDtypeStruct((8, d), f32),
        ]
        scratch = [pltpu.VMEM((LONG, GROUP), bf16)] + scratch
    elif mode == "far":
        in_specs += [weight, bias]
        out_specs = [weight, bias, dq_part, whole(BLK, d)]
        out_shape = [
            jax.ShapeDtypeStruct((groups, d, 3 * GROUP), f32),
            bias_shape,
            jax.ShapeDtypeStruct((groups, BLK, GROUP), f32),
            jax.ShapeDtypeStruct((BLK, d), bf16),
        ]
    else:
        in_specs += [weight, bias, dq_part]
        out_specs = [weight, bias, whole(BLK, d)]
        out_shape = [
            jax.ShapeDtypeStruct((groups, d, 3 * GROUP), bf16),
            bias_shape,
            jax.ShapeDtypeStruct((BLK, d), f32),
        ]
    return pl.pallas_call(
        functools.partial(back_kernel, mode),
        grid_spec=pltpu.PrefetchScalarGridSpec(
            num_scalar_prefetch=1,
            grid=(groups, blocks),
            in_specs=in_specs,
            out_specs=out_specs,
            scratch_shapes=scratch,
        ),
        out_shape=out_shape,
        compiler_params=pltpu.CompilerParams(vmem_limit_bytes=VMEM_LIMIT),
        cost_estimate=pl.CostEstimate(
            flops=groups * blocks * keys * 5_000_000, bytes_accessed=groups * blocks * 6_000_000, transcendentals=0
        ),
        name="back_" + mode,
    )(sc, q, k, v, do, o, inverse, expo, cos, sin, cos, sin, cos, sin, w, hidden_t, *more)


def gelu_parts(z):
    density = jnp.exp2(z * z * (-0.5 * log2_e)) * 0.3989422804014327
    t = 1.0 / (1.0 + 0.2316419 * jnp.abs(z))
    poly = t * (
        0.319381530
        + t * (-0.356563782 + t * (1.781477937 + t * (-1.821255978 + t * 1.330274429)))
    )
    tail = density * poly
    cdf = jnp.where(z >= 0, 1.0 - tail, tail)
    return z * cdf, cdf + z * density


def middle_kernel(
    sc, tokens, cotangent, o_hbm, w_out_own, w_out_other, b_out, gain, shift,
    up_a, up_b, up_c, up_d, b_up, down_a, down_b, down_c, down_d, b_down,
    out_hbm, mid_hbm, do_hbm, g_ref, g_out, g_bup, g_small,
    w_out, r1, h2, h2t, dy, dyt, acc, back, x_ref, o_ref, out_ref, do_ref, arrive, leave,
):
    i = pl.program_id(0)
    last = pl.num_programs(0) - 1
    blocks = [slice(j * BLK, (j + 1) * BLK) for j in range(3)]
    groups = o_ref.shape[0]
    block = lambda at: pl.ds(pl.multiple_of(at * BLK, BLK), BLK)
    o_in = [pltpu.make_async_copy(o_hbm.at[:, rows, :], o_ref.at[:, rows, :], arrive.at[j]) for j, rows in enumerate(blocks)]
    x_in = [
        pltpu.make_async_copy(tokens.at[block(sc[BLOCK + j]), :], x_ref.at[rows, :], arrive.at[3 + j])
        for j, rows in enumerate(blocks)
    ]
    y_in = [
        pltpu.make_async_copy(cotangent.at[block(sc[BLOCK + j]), :], dy.at[rows, :], arrive.at[6 + j])
        for j, rows in enumerate(blocks)
    ]
    leaving = [
        (
            pltpu.make_async_copy(out_ref.at[rows, :], out_hbm.at[block(sc[PLACE + j]), :], leave.at[j]),
            pltpu.make_async_copy(r1.at[rows, :], mid_hbm.at[rows, :], leave.at[3 + j]),
            pltpu.make_async_copy(do_ref.at[:, rows, :], do_hbm.at[:, rows, :], leave.at[6 + j]),
        )
        for j, rows in enumerate(blocks)
    ]
    heads_of = lambda rows: jnp.concatenate([o_ref[g, rows, :] for g in range(groups)], 1)

    @pl.when(i == 0)
    def _():
        for made in [m for pair in zip(o_in, x_in) for m in pair] + y_in:
            made.start()
        w_out[: w_out_own.shape[0], :] = w_out_own[...]
        w_out[w_out_own.shape[0] :, :] = w_out_other[...]
        for j, rows in enumerate(blocks):
            o_in[j].wait()
            x_in[j].wait()
            mixed = dot(heads_of(rows), w_out[...]) + wide(b_out) + x_ref[rows, :].astype(f32)
            r1[rows, :] = mixed
            normed, _ = normalize(mixed)
            hidden = (normed * wide(gain) + wide(shift)).astype(bf16)
            h2[rows, :] = hidden
            h2t[:, rows] = hidden.T
            acc[rows, :] = jnp.zeros_like(mixed)
            back[rows, :] = jnp.zeros_like(mixed)
        for j, rows in enumerate(blocks):
            y_in[j].wait()
            dyt[:, rows] = dy[rows, :].T

    @pl.when(i < last)
    def _():
        first, second = 2 * i < last, 2 * i + 1 < last
        w_up = jnp.concatenate(
            [jnp.where(first, up_a[...], up_c[...]), jnp.where(second, up_b[...], up_d[...])], 1
        )
        w_down = jnp.concatenate(
            [jnp.where(first, down_a[...], down_c[...]), jnp.where(second, down_b[...], down_d[...])], 0
        )
        bias = b_up[...]
        width = up_a.shape[1]
        total = dy.shape[0]
        parts = [slice(j, j + 256) for j in range(0, total, BLK // 2)]
        count = len(parts)
        actives, grads = [None] * count, [None] * count
        ups, downs = [None] * count, [None] * count
        col_sum = None

        def ahead(j):
            ups[j] = dot(h2[parts[j], :], w_up) + bias
            downs[j] = dot(dy[parts[j], :], w_down, NT)

        ahead(0)
        for j, rows in enumerate(parts):
            if j + 1 < count:
                ahead(j + 1)
            active, slope = gelu_parts(ups[j])
            actives[j] = active.astype(bf16)
            grads[j] = (downs[j] * slope).astype(bf16)
            s = jnp.sum(grads[j].astype(f32), 0, keepdims=True)
            col_sum = s if col_sum is None else col_sum + s
            acc[rows, :] += dot(actives[j], w_down)
            back[rows, :] += dot(grads[j], w_up, NT)
        g_bup[...] = col_sum
        g_up = dot(h2t[...], jnp.concatenate(grads, 0)).astype(bf16)
        g_down = dot(dyt[...], jnp.concatenate(actives, 0)).astype(bf16)
        for n in range(2):
            cols = slice(n * width, (n + 1) * width)
            g_ref[:, 2 * n * width : (2 * n + 1) * width] = g_up[:, cols]
            g_ref[:, (2 * n + 1) * width : (2 * n + 2) * width] = g_down[:, cols]

    @pl.when(i == last)
    def _():
        sums = [None] * 4
        lows = []
        for j, rows in enumerate(blocks):
            mixed = r1[rows, :]
            out_ref[rows, :] = (acc[rows, :] + wide(b_down) + mixed).astype(bf16)
            normed, inverse = normalize(mixed)
            top = dy[rows, :].astype(f32)
            dh = back[rows, :]
            dr = top + normalize_back(normed, inverse, dh * wide(gain))
            r1[rows, :] = dr
            low = dr.astype(bf16)
            lows.append(low)
            do = dot(low, w_out[...], NT).astype(bf16)
            for g in range(groups):
                do_ref[g, rows, :] = do[:, g * GROUP : (g + 1) * GROUP]
            for made in leaving[j]:
                made.start()
            for n, term in enumerate((dh * normed, dh, dr, top)):
                s = jnp.sum(term, 0, keepdims=True)
                sums[n] = s if sums[n] is None else sums[n] + s
        g_out[...] = dot(jnp.concatenate(lows, 0).T, heads_of(slice(0, 3 * BLK))).astype(bf16)
        g_small[...] = jnp.concatenate(sums + [jnp.zeros_like(sums[0])] * 4, 0)
        for parts in leaving:
            for made in parts:
                made.wait()


def middle(sc, tokens, cotangent, o, w_out_own, w_out_other, b_out, gain, shift, up_own, down_own, up_other, down_other, b_up, b_down):
    d = tokens.shape[1]
    groups = o.shape[0]
    own = 3 * BLK
    half = up_own.shape[1]
    piece = 256
    per = half // piece
    steps = per + 1
    one = pl.Buffered(buffer_count=1)
    whole = lambda *shape: pl.BlockSpec(shape, lambda i, s: (0,) * len(shape), pipeline_mode=one)
    hbm = pl.BlockSpec(memory_space=pl.ANY)
    fixed = lambda *shape: pl.BlockSpec(shape, lambda i, s: (0,) * len(shape))
    at = lambda i: jnp.minimum(i, per - 1)
    places = [
        lambda i: jnp.minimum(2 * i, per - 1),
        lambda i: jnp.minimum(2 * i + 1, per - 1),
        lambda i: jnp.clip(2 * i - per, 0, per - 1),
        lambda i: jnp.clip(2 * i + 1 - per, 0, per - 1),
    ]
    ups = [pl.BlockSpec((d, piece), functools.partial(lambda p, i, s: (0, p(i)), p)) for p in places]
    downs = [pl.BlockSpec((piece, d), functools.partial(lambda p, i, s: (p(i), 0), p)) for p in places]
    return pl.pallas_call(
        middle_kernel,
        grid_spec=pltpu.PrefetchScalarGridSpec(
            num_scalar_prefetch=1,
            grid=(steps,),
            in_specs=[hbm, hbm, hbm]
            + [
                whole(*w_out_own.shape),
                whole(*w_out_other.shape),
                whole(d),
                whole(d),
                whole(d),
                *ups,
                pl.BlockSpec((1, 2 * piece), lambda i, s: (0, at(i))),
                *downs,
                whole(d),
            ],
            out_specs=[
                hbm,
                hbm,
                hbm,
                pl.BlockSpec((d, 4 * piece), lambda i, s: (0, at(i))),
                fixed(d, d),
                pl.BlockSpec((1, 2 * piece), lambda i, s: (0, at(i))),
                fixed(8, d),
            ],
            scratch_shapes=[
                pltpu.VMEM((d, d), bf16),
                pltpu.VMEM((own, d), f32),
                pltpu.VMEM((own, d), bf16),
                pltpu.VMEM((d, own), bf16),
                pltpu.VMEM((own, d), bf16),
                pltpu.VMEM((d, own), bf16),
                pltpu.VMEM((own, d), f32),
                pltpu.VMEM((own, d), f32),
                pltpu.VMEM((own, d), bf16),
                pltpu.VMEM((groups, own, GROUP), bf16),
                pltpu.VMEM((own, d), bf16),
                pltpu.VMEM((groups, own, GROUP), bf16),
                pltpu.SemaphoreType.DMA((9,)),
                pltpu.SemaphoreType.DMA((9,)),
            ],
        ),
        out_shape=[
            jax.ShapeDtypeStruct((own, d), bf16),
            jax.ShapeDtypeStruct((own, d), f32),
            jax.ShapeDtypeStruct((groups, own, GROUP), bf16),
            jax.ShapeDtypeStruct((d, 4 * half), bf16),
            jax.ShapeDtypeStruct((d, d), bf16),
            jax.ShapeDtypeStruct((1, 2 * half), f32),
            jax.ShapeDtypeStruct((8, d), f32),
        ],
        compiler_params=pltpu.CompilerParams(vmem_limit_bytes=VMEM_LIMIT),
        cost_estimate=pl.CostEstimate(
            flops=2 * own * d * (3 * d + 12 * half), bytes_accessed=40_000_000, transcendentals=8_000_000
        ),
        name="middle",
    )(sc, tokens, cotangent, o, w_out_own, w_out_other, b_out, gain, shift,
      *[up_own] * 2, *[up_other] * 2, b_up, *[down_own] * 2, *[down_other] * 2, b_down)


def finish_rows(x, gain, mid, dh):
    normed, inverse = normalize(x.astype(f32))
    out = (mid + normalize_back(normed, inverse, dh * gain)).astype(bf16)
    return out, jnp.sum(dh * normed, 0, keepdims=True), jnp.sum(dh, 0, keepdims=True)


def lines(v):
    return jnp.concatenate([v[:, j * GROUP : (j + 1) * GROUP] for j in range(v.shape[1] // GROUP)], 0)


def last_kernel(
    q_ref, k_ref, v_ref, do_ref, o_ref, l_ref, e_ref, cos, sin, w_ref, ht_ref, before, before_b, dq_in, gout_ref,
    part_ref, tokens, gain, mid, small_w, small_two, gup_ref, early_ref,
    sum_out, theirs_out, small_out, small_theirs_out, rows_out, rows_theirs_out, early_out,
    prod, dk_sum, dv_sum, dh_sum, gb_sum, g_all, part_in, x_ref, mid_ref, early_part,
    r1, a1, r2, a2, r3, sums, theirs, rows_ref, row_ends, s0, s1, s2, s3, q1, q2, q3, q4, send, recv, local,
):
    g = pl.program_id(0)
    groups = g_all.shape[3]
    here = lax.axis_index("dp")
    mp = lax.axis_index("mp")
    c = here % 2
    x = (here // 2) % 2
    z = here // 4
    core = (here + 1 - 2 * c, mp)
    side = (here + 2 - 4 * x, mp)
    across = (here, 1 - mp)
    line = [((z + n) % 4, ((z + n) % 4 * 4 + here % 4, mp)) for n in (1, 2, 3)]

    numbers = {}

    def copy(name, src, dst, dev):
        n = numbers.setdefault(name, len(numbers))
        return pltpu.make_async_remote_copy(
            src_ref=src,
            dst_ref=dst,
            send_sem=send.at[n],
            recv_sem=recv.at[n],
            device_id=dev,
            device_id_type=pl.DeviceIdType.MESH,
        )

    part_copy = copy("part", part_ref, part_in, across)
    early_copy = copy("early", early_part, early_out, across)
    halves = [slice(n, n + BLK // 2) for n in range(0, BLK, BLK // 2)]
    rows_copies = [copy(("r", n), rows_ref.at[h, :], rows_theirs_out.at[h, :], across) for n, h in enumerate(halves)]
    rows_keep = pltpu.make_async_copy(rows_ref, rows_out, local.at[2])
    by_core = [copy(("c", n), g_all.at[:, :, 1 - c, n], r1.at[:, :, n], core) for n in range(groups)]
    by_side = [copy(("x", n), a1.at[:, 1 - x, n], r2.at[:, n], side) for n in range(groups)]
    by_line = [
        [copy(("z", n, m), a2.at[at, n], r3.at[m, n], dev) for m, (at, dev) in enumerate(line)]
        for n in range(groups)
    ]
    by_across = [copy(("y", n), sums.at[n], theirs.at[n], across) for n in range(groups)]
    small_core = copy("sc", s0, q1, core)
    small_side = copy("sx", s1, q2, side)
    small_line = [copy(("sz", m), s2, q3.at[z], dev) for m, (_, dev) in enumerate(line)]
    small_across = copy("sy", s3, q4, across)
    rows = pl.ds(pl.multiple_of((2 + mp) * BLK, BLK), BLK)
    x_copy = pltpu.make_async_copy(tokens.at[rows, :], x_ref, local.at[0])
    mid_copy = pltpu.make_async_copy(mid.at[2 * BLK : 3 * BLK, :], mid_ref, local.at[1])

    partners = [core, side, across] + [dev for _, dev in line]

    @pl.when(g == 0)
    def _():
        barrier = pltpu.get_barrier_semaphore()
        for dev in partners:
            pl.semaphore_signal(barrier, inc=1, device_id=dev, device_id_type=pl.DeviceIdType.MESH)
        x_copy.start()
        mid_copy.start()
        dh_sum[...] = jnp.zeros_like(dh_sum)
        share, width = early_ref.shape[0], early_part.shape[1]
        start = gup_ref.shape[1]
        early_part[share:, :] = jnp.zeros((early_part.shape[0] - share, width), bf16)
        early_part[:share, :] = early_ref[:, start : start + width]

    def second(n):
        by_core[n].wait()
        a1[:, :, n] = (g_all[:, :, c, n].astype(f32) + r1[:, :, n].astype(f32)).astype(bf16)
        by_side[n].start()

    def third(n):
        by_side[n].wait()
        a2[:, n] = (a1[:, x, n].astype(f32) + r2[:, n].astype(f32)).astype(bf16)
        for made in by_line[n]:
            made.start()

    def fourth(n):
        for made in by_line[n]:
            made.wait()
        total = a2[z, n].astype(f32)
        for m in range(3):
            total = total + r3[m, n].astype(f32)
        sums[n] = total.astype(bf16)
        by_across[n].start()

    dk_sum[...] = jnp.zeros_like(dk_sum)
    dv_sum[...] = jnp.zeros_like(dv_sum)
    refs = (q_ref, k_ref, v_ref, do_ref, o_ref, l_ref, e_ref, prod, dk_sum, dv_sum)
    dq = (attend_back_body(*refs, 0, BLK) + dq_in[...]) * (HD ** (-0.5))

    @pl.when(g == 0)
    def _():
        pl.semaphore_wait(pltpu.get_barrier_semaphore(), len(partners))
        part_copy.start()
        early_copy.start()

    for n in range(1, groups):

        @pl.when(g == n)
        def _(n=n):
            for late, stage in ((1, second), (2, third), (3, fourth)):
                if n >= late:
                    stage(n - late)

    dq = rotate_back(dq, cos[...], sin[...]).astype(bf16)
    weight, bias = window_back(dq, dk_sum, dv_sum, ((cos, sin),), w_ref, ht_ref, dh_sum)
    gb_sum[g] = bias + before_b[...]

    @pl.when(g == groups - 1)
    def _():
        x_copy.wait()
        mid_copy.wait()
        part_copy.wait()
        ends = [0.0, 0.0]
        for n, h in enumerate(halves):
            out, *terms = finish_rows(x_ref[h, :], wide(gain), mid_ref[h, :], dh_sum[h, :] + part_in[h, :].astype(f32))
            rows_ref[h, :] = out
            rows_copies[n].start()
            ends = [a + b for a, b in zip(ends, terms)]
        rows_keep.start()
        row_ends[0:1, :] = ends[0]
        row_ends[1:2, :] = ends[1]

    weight = weight + before[...]
    share = early_ref.shape[0]
    held_rows = 4 * share
    fill = jnp.zeros((g_all.shape[4] - held_rows, GROUP), f32)
    weight = jnp.concatenate([weight, gout_ref[...].astype(f32)], 1)
    for n in range(16):
        part = weight[n * share : (n + 1) * share]
        pieces = [part[:, s * GROUP : (s + 1) * GROUP] for s in range(4)]
        pieces = pieces + [fill] if fill.shape[0] else pieces
        g_all[n // 4, n // 2 % 2, n % 2, g] = jnp.concatenate(pieces, 0).astype(bf16)

    for n in range(groups):

        @pl.when(g == n)
        def _(n=n):
            by_core[n].start()

    @pl.when(g == groups - 1)
    def _():
        n = groups - 1
        held = [lines(small_w[m : m + 1, :] + row_ends[m : m + 1, :]) for m in range(2)]
        held += [lines(small_two[m : m + 1, :]) for m in range(4)]
        held += [gb_sum[m, :, s * GROUP : (s + 1) * GROUP] for s in range(3) for m in range(groups)]
        held.append(lines(gup_ref[...]))
        held = jnp.concatenate(held, 0)
        s0[...] = jnp.concatenate([held, jnp.zeros((s0.shape[0] - held.shape[0], GROUP), f32)], 0)
        small_core.start()
        second(n)
        third(n - 1)
        fourth(n - 2)
        small_core.wait()
        s1[...] = s0[...] + q1[...]
        small_side.start()
        third(n)
        small_side.wait()
        s2[...] = s1[...] + q2[...]
        for made in small_line:
            made.start()
        fourth(n - 1)
        for made in small_line:
            made.wait()
        q3[z] = s2[...]
        s3[...] = (q3[0] + q3[1]) + (q3[2] + q3[3])
        small_across.start()
        fourth(n)
        early_copy.wait()
        small_out[...] = s3[...]
        sum_out[...] = sums[...]
        rows_keep.wait()
        for made in rows_copies:
            made.wait()
        small_across.wait()
        small_theirs_out[...] = q4[...]
        for made in by_across:
            made.wait()
        theirs_out[...] = theirs[...]


def last(q, k, v, do, o, inverse, expo, cos, sin, w, hidden_t, g_sum, gb_sum, dq_far, g_out, part, tokens, gain, mid,
         small_w, small_two, g_bup, early):
    groups = o.shape[0]
    d = w.shape[2]
    heads = GROUP // HD
    share = early.shape[0]
    held = -(-4 * share // 16) * 16
    block = (groups, held, GROUP)
    count = 6 * d // GROUP + groups * 3 + g_bup.shape[1] // GROUP
    small = (-(-count // 8) * 8, GROUP)
    early_part = (-(-share // 16) * 16, g_bup.shape[1])
    copies = 4 + 6 * groups + 6
    one = pl.Buffered(buffer_count=1)
    hbm = pl.BlockSpec(memory_space=pl.ANY)
    whole = lambda a: pl.BlockSpec(a.shape, lambda g: (0,) * a.ndim, pipeline_mode=one)
    fixed = lambda shape: pl.BlockSpec(shape, lambda g: (0,) * len(shape))
    qs = pl.BlockSpec((None, BLK, GROUP), lambda g: (g, 2, 0))
    os = pl.BlockSpec((None, BLK, GROUP), lambda g: (g, 2, 0))
    outs = [(block, bf16), (block, bf16), (small, f32), (small, f32), ((BLK, d), bf16), ((BLK, d), bf16)]
    outs.append((early_part, bf16))
    return pl.pallas_call(
        last_kernel,
        grid=(groups,),
        in_specs=[qs, qs, qs, os, os, os]
        + [
            pl.BlockSpec((heads, BLK, BLK), lambda g: (g * 3 + 2, 0, 0)),
            whole(cos),
            whole(sin),
            pl.BlockSpec((3, GROUP, d), lambda g: (0, g, 0)),
            pl.BlockSpec((d, BLK), lambda g: (0, 2), pipeline_mode=one),
            pl.BlockSpec((None, d, 3 * GROUP), lambda g: (g, 0, 0)),
            pl.BlockSpec((None, 1, 3 * GROUP), lambda g: (g, 0, 0)),
            pl.BlockSpec((None, BLK, GROUP), lambda g: (g, 0, 0)),
            pl.BlockSpec((d, GROUP), lambda g: (0, g)),
            whole(part),
            hbm,
            whole(gain),
            hbm,
            whole(small_w),
            whole(small_two),
            whole(g_bup),
            whole(early),
        ],
        out_specs=[fixed(shape) for shape, _ in outs[:4]] + [hbm] * 3,
        out_shape=[jax.ShapeDtypeStruct(*spec) for spec in outs],
        scratch_shapes=[
            pltpu.VMEM((2, BLK, BLK), f32),
            pltpu.VMEM((BLK, GROUP), f32),
            pltpu.VMEM((BLK, GROUP), f32),
            pltpu.VMEM((BLK, d), f32),
            pltpu.VMEM((groups, 1, 3 * GROUP), f32),
            pltpu.VMEM((4, 2, 2, *block), bf16),
            pltpu.VMEM((BLK, d), bf16),
            pltpu.VMEM((BLK, d), bf16),
            pltpu.VMEM((BLK, d), f32),
            pltpu.VMEM(early_part, bf16),
            pltpu.VMEM((4, 2, *block), bf16),
            pltpu.VMEM((4, 2, *block), bf16),
            pltpu.VMEM((4, *block), bf16),
            pltpu.VMEM((4, *block), bf16),
            pltpu.VMEM((3, *block), bf16),
            pltpu.VMEM(block, bf16),
            pltpu.VMEM(block, bf16),
            pltpu.VMEM((BLK, d), bf16),
            pltpu.VMEM((8, d), f32),
            pltpu.VMEM(small, f32),
            pltpu.VMEM(small, f32),
            pltpu.VMEM(small, f32),
            pltpu.VMEM(small, f32),
            pltpu.VMEM(small, f32),
            pltpu.VMEM(small, f32),
            pltpu.VMEM((4, *small), f32),
            pltpu.VMEM(small, f32),
            pltpu.SemaphoreType.DMA((copies,)),
            pltpu.SemaphoreType.DMA((copies,)),
            pltpu.SemaphoreType.DMA((3,)),
        ],
        compiler_params=pltpu.CompilerParams(
            vmem_limit_bytes=VMEM_LIMIT, collective_id=0, has_side_effects=True
        ),
        cost_estimate=pl.CostEstimate(flops=30_000_000_000, bytes_accessed=100_000_000, transcendentals=0),
        name="last",
    )(q, k, v, do, o, inverse, expo, cos, sin, w, hidden_t, g_sum, gb_sum, dq_far, g_out, part, tokens, gain, mid,
      small_w, small_two, g_bup, early)


def finish_kernel(x_ref, gain, mid_ref, own_ref, part_ref, out_ref, small):
    out, first, second = finish_rows(
        x_ref[...], wide(gain), mid_ref[...], own_ref[...] + part_ref[...].astype(f32)
    )
    out_ref[...] = out
    small[...] = jnp.concatenate([lines(first), lines(second)], 0)


def finish(x, gain, mid, own, part):
    d = x.shape[1]
    return pl.pallas_call(
        finish_kernel,
        out_shape=[jax.ShapeDtypeStruct(x.shape, bf16), jax.ShapeDtypeStruct((2 * d // GROUP, GROUP), f32)],
        compiler_params=pltpu.CompilerParams(vmem_limit_bytes=VMEM_LIMIT),
        name="finish",
    )(x, gain, mid, own, part)


def place_pieces(places, pieces, out_ref, sem):
    mp = lax.axis_index("mp")
    copies = []
    for n, (piece, (zero, one)) in enumerate(zip(pieces, places)):
        start = pl.multiple_of((zero + (one - zero) * mp) * BLK, BLK)
        copies.append(pltpu.make_async_copy(piece, out_ref.at[pl.ds(start, piece.shape[0]), :], sem.at[n]))
        copies[-1].start()
    return copies


def assemble_kernel(places, *rest):
    count = len(places)
    for made in place_pieces(places, rest[:count], rest[count], rest[-1]):
        made.wait()


def assemble(places, pieces, rows):
    count = len(pieces)
    return pl.pallas_call(
        functools.partial(assemble_kernel, places),
        in_specs=[pl.BlockSpec(memory_space=pltpu.VMEM)] * count,
        out_specs=pl.BlockSpec(memory_space=pl.ANY),
        out_shape=jax.ShapeDtypeStruct((rows, pieces[0].shape[1]), pieces[0].dtype),
        scratch_shapes=[pltpu.SemaphoreType.DMA((count,))],
        compiler_params=pltpu.CompilerParams(vmem_limit_bytes=VMEM_LIMIT),
        cost_estimate=pl.CostEstimate(flops=0, bytes_accessed=8_000_000, transcendentals=0),
        name="assemble",
    )(*pieces)


def one_line(v):
    return jnp.concatenate([v[j : j + 1] for j in range(v.shape[0])], 1)


def conclude_kernel(
    share, half, hidden, places, late, late_theirs, early, early_theirs, small, small_theirs, p0, p1, p2, p3,
    g_qkv, g_up, g_down, g_out, g_bqkv, g_bup, grad, *rest,
):
    vectors, sem = rest[:-1], rest[-1]
    copies = place_pieces(places, (p0, p1, p2, p3), grad, sem)
    groups = late.shape[0]
    d = groups * GROUP
    whole = half // GROUP
    for s in range(4):
        rows = slice(s * share, (s + 1) * share)
        mine = [late[g].astype(f32)[rows] for g in range(whole + 1)]
        other = [late_theirs[g].astype(f32)[rows] for g in range(whole, groups)]
        both = jnp.concatenate(mine, 1)[:, :half] + jnp.concatenate(other, 1)[:, half - whole * GROUP :]
        if s < 3:
            g_qkv[s] = both
        else:
            g_out[...] = both
    width = 256
    for c in range(hidden // width):
        mine = early[:, 2 * c * width : 2 * (c + 1) * width].astype(f32)
        other = early_theirs[:share, 2 * c * width : 2 * (c + 1) * width].astype(f32)
        both = mine + other
        cols = slice(c * width, (c + 1) * width)
        g_up[:, cols] = both[:, :width]
        g_down[:, cols] = both[:, width:]
    per = d // GROUP
    for n, ref in enumerate(vectors):
        ref[...] = one_line(small[n * per : (n + 1) * per] + small_theirs[n * per : (n + 1) * per])[0]
    base = 6 * per
    for s in range(3):
        rows = slice(base + s * per, base + (s + 1) * per)
        g_bqkv[s : s + 1, :] = one_line(small[rows])[:, :half] + one_line(small_theirs[rows])[:, half:]
    base += 3 * per
    count = hidden // GROUP
    g_bup[...] = one_line(small[base : base + count] + small_theirs[base + count : base + 2 * count])[0]
    for made in copies:
        made.wait()


def conclude(share, half, hidden, places, args, pieces, rows):
    d = 2 * half
    vmem = pl.BlockSpec(memory_space=pltpu.VMEM)
    return pl.pallas_call(
        functools.partial(conclude_kernel, share, half, hidden, places),
        in_specs=[vmem] * (len(args) + len(pieces)),
        out_specs=[vmem] * 6 + [pl.BlockSpec(memory_space=pl.ANY)] + [vmem] * 6,
        out_shape=[
            jax.ShapeDtypeStruct((3, share, half), f32),
            jax.ShapeDtypeStruct((share, hidden), f32),
            jax.ShapeDtypeStruct((share, hidden), f32),
            jax.ShapeDtypeStruct((share, half), f32),
            jax.ShapeDtypeStruct((3, half), f32),
            jax.ShapeDtypeStruct((hidden,), f32),
            jax.ShapeDtypeStruct((rows, d), bf16),
        ]
        + [jax.ShapeDtypeStruct((d,), f32)] * 6,
        scratch_shapes=[pltpu.SemaphoreType.DMA((len(pieces),))],
        compiler_params=pltpu.CompilerParams(vmem_limit_bytes=VMEM_LIMIT),
        cost_estimate=pl.CostEstimate(flops=1_000_000, bytes_accessed=12_000_000, transcendentals=0),
        name="conclude",
    )(*args, *pieces)


def on_device(
    tokens, lengths, gain_one, shift_one, w_qkv, b_qkv, w_out, b_out, gain_two, shift_two, w_up, b_up, w_down, b_down,
    cotangent,
):
    d = tokens.shape[1]
    n_dp = lax.axis_size("dp")
    swap = [(0, 1), (1, 0)]
    half = w_qkv.shape[2]
    hidden = w_up.shape[1]

    groups = d // GROUP
    share = d // n_dp
    by_hand = n_dp == 16
    tables = tuple(jnp.asarray(t) for t in rope_tables())
    *attended, q, k, v, hidden_t, w_all, w_out_other, up_other, down_other, b_up_all, sc, near_cos, near_sin = front(
        lengths, gain_one, shift_one, b_qkv, b_up, *tables, jnp.transpose(w_qkv, (0, 2, 1)), tokens, w_out, w_up, w_down
    )
    qkv = (q, k, v)
    out_own, grad_mid, do, g_early, g_out, g_bup, small_two = middle(
        sc, tokens, cotangent, attended[0], w_out, w_out_other, b_out, gain_two, shift_two,
        w_up, w_down, up_other, down_other, b_up_all, b_down,
    )
    early = lax.psum_scatter(g_early, "dp", scatter_dimension=0, tiled=True)

    theirs = lax.ppermute(out_own, "mp", swap)
    out_tokens = assemble(((0, 3), (3, 0)), [out_own, theirs], 6 * BLK)
    args = (sc, *qkv, do, *attended, *tables, w_all, hidden_t)
    g_sum, gb_sum, grad_whole, small_w = back("whole", *args, (tokens, gain_one, grad_mid))
    whole_theirs = lax.ppermute(grad_whole, "mp", swap)
    g_sum, gb_sum, dq_far, part = back("far", *args, (g_sum, gb_sum))
    if by_hand:
        part, out_tokens, whole_theirs, early = lax.optimization_barrier((part, out_tokens, whole_theirs, early))
        late, late_theirs, small, small_theirs, shared, shared_theirs, early_theirs = last(
            *args[1:8], near_cos, near_sin, *args[10:], g_sum, gb_sum, dq_far, g_out, part, tokens, gain_one, grad_mid,
            small_w, small_two, g_bup, early,
        )
    else:
        arrived = lax.ppermute(part, "mp", swap)
        g_qkv, g_bqkv, own = back("near", *args, (g_sum, gb_sum, dq_far))
        x_shared = lax.dynamic_slice_in_dim(tokens, sc[BLOCK + 2] * BLK, BLK, 0)
        shared, last_sums = finish(x_shared, gain_one, grad_mid[2 * BLK :], own, arrived)
        g_bqkv = g_bqkv.reshape(groups, 3, GROUP).transpose(1, 0, 2)
        small = jnp.concatenate(
            [
                small_w[:2].reshape(-1, GROUP) + last_sums,
                small_two[:4].reshape(-1, GROUP),
                g_bqkv.reshape(-1, GROUP),
                g_bup.reshape(-1, GROUP),
            ]
        )
        n_small = small.shape[0]
        shared_theirs = lax.ppermute(shared, "mp", swap)
        g_qkv = g_qkv.reshape(groups, d, 3, GROUP).transpose(2, 1, 0, 3).reshape(3, d, d)
        late = lax.psum_scatter(g_qkv, "dp", scatter_dimension=1, tiled=True)
        late_theirs = lax.ppermute(late, "mp", swap)
        small = lax.psum(small, "dp")
        small_theirs = lax.ppermute(small, "mp", swap)
        early_theirs = lax.ppermute(early[:, 2 * hidden :], "mp", swap)
    places = ((0, 4), (2, 3), (3, 2), (4, 0))
    pieces = [grad_whole, shared, shared_theirs, whole_theirs]

    if by_hand:
        g_w, g_up, g_down, g_out, g_bq, g_bu, grad_tokens, *vectors = conclude(
            share, half, hidden, places,
            (late, late_theirs, early, early_theirs, small, small_theirs), pieces, 6 * BLK,
        )
        g_down, g_out = g_down.T, g_out.T
    else:
        grad_tokens = assemble(places, pieces, 6 * BLK)
        mlp = early[:, : 2 * hidden].astype(f32) + early_theirs[:, : 2 * hidden].astype(f32)
        mlp = mlp.reshape(share, hidden // 256, 2, 256)
        g_up = mlp[:, :, 0].reshape(share, hidden)
        g_down = mlp[:, :, 1].reshape(share, hidden).T
        g_out = lax.psum_scatter(g_out, "dp", scatter_dimension=0, tiled=True)
        out_theirs = lax.ppermute(g_out[:, half:], "mp", swap)
        g_out = (g_out[:, :half].astype(f32) + out_theirs.astype(f32)).T
        g_w = late[:, :, :half].astype(f32) + late_theirs[:, :, half:].astype(f32)
        mine, others = small[:n_small].reshape(-1), small_theirs[:n_small].reshape(-1)
        vectors = list((mine[: 6 * d] + others[: 6 * d]).reshape(6, d))
        pair = lambda v, lo, n, w: v[lo : lo + 2 * n * w].reshape(n, 2, w)
        g_bq = pair(mine, 6 * d, 3, half)[:, 0] + pair(others, 6 * d, 3, half)[:, 1]
        g_bu = pair(mine, 9 * d, 1, hidden)[0, 0] + pair(others, 9 * d, 1, hidden)[0, 1]
    return (
        out_tokens,
        grad_tokens,
        vectors[0],
        vectors[1],
        g_w,
        g_bq,
        g_out,
        vectors[4],
        vectors[2],
        vectors[3],
        g_up,
        g_bu,
        g_down,
        vectors[5],
    )


def solution(mesh):
    in_specs = (
        P("dp", None),
        P("dp", None),
        P(),
        P(),
        P(None, None, "mp"),
        P(None, "mp"),
        P("mp", None),
        P(),
        P(),
        P(),
        P(None, "mp"),
        P("mp"),
        P("mp", None),
        P(),
        P("dp", None),
    )
    out_specs = (
        P("dp", None),
        P("dp", None),
        P(),
        P(),
        P(None, "dp", "mp"),
        P(None, "mp"),
        P("mp", "dp"),
        P(),
        P(),
        P(),
        P("dp", "mp"),
        P("mp"),
        P("mp", "dp"),
        P(),
    )
    return jax.shard_map(on_device, mesh=mesh, in_specs=in_specs, out_specs=out_specs, check_vma=False)
```

```python
import functools

import jax
import jax.numpy as jnp
import numpy as np
from jax import lax
from jax.experimental import pallas as pl
from jax.experimental.pallas import tpu as pltpu
from jax.sharding import PartitionSpec as P

HD = 32
LONG = 1024
BLK = 512
GROUP = 128
epsilon = 1e-05
rotary_base = 10000.0
log2_e = 1.4426950408889634
ln_2 = 0.6931471805599453

f32 = jnp.float32
bf16 = jnp.bfloat16
NT = (((1,), (1,)), ((), ()))
NN = (((1,), (0,)), ((), ()))
TN = (((0,), (0,)), ((), ()))
VMEM_LIMIT = 60 << 20


def dot(a, b, dims=NN):
    return lax.dot_general(a, b, dims, preferred_element_type=f32)


def rope_tables():
    place = np.arange(LONG, dtype=np.float64)[:, None]
    frequency = rotary_base ** (-np.arange(HD // 2, dtype=np.float64) * 2.0 / HD)
    angles = place * frequency[None, :]
    cosines = np.concatenate([np.cos(angles), np.cos(angles)], 1)
    sines = np.concatenate([-np.sin(angles), np.sin(angles)], 1)
    repeat = GROUP // HD
    return (
        np.tile(cosines, (1, repeat)).astype(np.float32),
        np.tile(sines, (1, repeat)).astype(np.float32),
    )


def swap_pieces_of_rows(x):
    lane = lax.broadcasted_iota(jnp.int32, (1, GROUP), 1)
    low = (lane // (HD // 2)) % 2 == 0
    return jnp.where(low, pltpu.roll(x, GROUP - HD // 2, 1), pltpu.roll(x, HD // 2, 1))


def rotate(x, cosines, sines):
    return x * cosines + swap_pieces_of_rows(x) * sines


def rotate_back(x, cosines, sines):
    return x * cosines - swap_pieces_of_rows(x) * sines


def normalize(values):
    centred = values - jnp.mean(values, -1, keepdims=True)
    inverse = lax.rsqrt(jnp.mean(centred * centred, -1, keepdims=True) + epsilon)
    return (centred * inverse, inverse)


def normalize_back(normed, inverse, grad_normed):
    mean_grad = jnp.mean(grad_normed, -1, keepdims=True)
    mean_proj = jnp.mean(grad_normed * normed, -1, keepdims=True)
    return inverse * (grad_normed - mean_grad - normed * mean_proj)


FLAG, BLOCK, TABLE, PLACE = 0, 3, 7, 11


def wide(ref):
    return ref[...].astype(f32)[None]


def attend_body(q, k_ref, v_ref, o_ref, l_ref, e_ref, store, bias):
    lane = lax.broadcasted_iota(jnp.int32, (1, GROUP), 1) // HD
    heads = GROUP // HD
    count = k_ref.shape[0]
    chunks = count // BLK
    values_t = v_ref[...].T
    ones = jnp.ones((16, count), bf16)
    outs, inverses = [], []

    def score(h, c):
        keys = k_ref[c * BLK : (c + 1) * BLK, :]
        scores = dot(jnp.where(lane == h, keys, jnp.zeros_like(keys)), q, NT)
        store[h % 2, c * BLK : (c + 1) * BLK, :] = scores
        return jnp.max(scores.reshape(BLK // 8, 8, BLK), axis=0) + bias[c]

    def score_max(h, c, so_far):
        found = score(h, c)
        return found if so_far is None else jnp.maximum(so_far, found)

    top = None
    for c in range(chunks):
        top = score_max(0, c, top)
    row_max = jnp.max(top, axis=0, keepdims=True)
    for h in range(heads):
        top = None
        total = None
        stacked = jnp.concatenate([values_t[HD * h : HD * (h + 1)], ones], 0)
        for c in range(chunks):
            if h + 1 < heads:
                top = score_max(h + 1, c, top)
            rows = slice(c * BLK, (c + 1) * BLK)
            expo = jnp.exp2(store[h % 2, rows, :] - (row_max - bias[c])).astype(bf16)
            e_ref[h, rows, :] = expo
            part = dot(stacked[:, rows], expo)
            total = part if total is None else total + part
        inverse = 1.0 / total[HD : HD + 1]
        outs.append(total[:HD] * inverse)
        inverses.append(jnp.broadcast_to(inverse, (HD, BLK)))
        if h + 1 < heads:
            row_max = jnp.max(top, axis=0, keepdims=True)
    o_ref[...] = jnp.concatenate(outs, 0).T.astype(bf16)
    l_ref[...] = jnp.concatenate(inverses, 0).T


def front_kernel(
    first, lengths, gain, shift, b_own, b_up, cos, sin, w_own, tokens, w_out, w_up, w_down,
    o_ref, l_ref, e_ref, q_out, k_out, v_out, ht_out, w_all, out_other, up_other, down_other, b_all, sc, near_cos, near_sin,
    store, x_all, hidden, q_all, k_all, v_all, ht, w_in, b_mine, b_in, local, send, recv,
):
    g, b = pl.program_id(0), pl.program_id(1)
    step = 3 * g + b
    here = lax.axis_index("dp")
    mp = lax.axis_index("mp")
    c = here % 2
    x = (here // 2) % 2
    core = (here + 1 - 2 * c, mp)
    side = (here + 2 - 4 * x, mp)
    across = (here, 1 - mp)
    groups = q_all.shape[0]
    half = w_own.shape[1]
    side_long = (lengths[0, 4 * mp] == LONG).astype(jnp.int32)
    mid_long = (lengths[0, 2] == LONG).astype(jnp.int32)
    table = [0, side_long, mp * mid_long, (1 - mp) * mid_long]
    numbers = {}

    def copy(name, src, dst, dev):
        n = numbers.setdefault(name, len(numbers))
        return pltpu.make_async_remote_copy(
            src_ref=src,
            dst_ref=dst,
            send_sem=send.at[n],
            recv_sem=recv.at[n],
            device_id=dev,
            device_id_type=pl.DeviceIdType.MESH,
        )

    def quarter(ref, n):
        size = ref.shape[0] // 4
        return ref.at[pl.ds(pl.multiple_of(n * size, size), size), :]

    share = half // 2
    mine = pl.ds(pl.multiple_of(c * share, share), share)
    w_across = copy("w", w_own.at[:, mine, :], w_in.at[:, mine, :], across)
    w_core = copy("wc", w_in.at[:, mine, :], w_in.at[:, mine, :], core)
    b_across = copy("b", b_mine, b_in, across)
    out_across = copy("o", w_out, out_other, across)
    n_mine, n_side = 2 * x + c, 2 * (1 - x) + c
    pairs = ((w_up, up_other), (w_down, down_other))
    by_across = [copy(("y", n), quarter(a, n_mine), quarter(to, n_mine), across) for n, (a, to) in enumerate(pairs)]
    by_side = [copy(("x", n), quarter(to, n_mine), quarter(to, n_mine), side) for n, (_, to) in enumerate(pairs)]
    by_core = [
        copy(("c", n, m), quarter(to, at), quarter(to, at), core)
        for n, (_, to) in enumerate(pairs)
        for m, at in enumerate((n_mine, n_side))
    ]
    block = lambda at, count: pl.ds(pl.multiple_of(at * BLK, BLK), count * BLK)
    x_copies = [
        pltpu.make_async_copy(tokens.at[block(at, count), :], x_all.at[to * BLK : (to + count) * BLK, :], local.at[n])
        for n, (at, to, count) in enumerate(((4 * mp, 0, 2), (2 + mp, 2, 1), (3 - mp, 3, 1)))
    ]
    w_copies = [
        pltpu.make_async_copy(w_own, w_all.at[:, :half, :], local.at[3]),
        pltpu.make_async_copy(w_in, w_all.at[:, half:, :], local.at[4]),
    ]
    ht_copy = pltpu.make_async_copy(ht, ht_out, local.at[5])

    def qkv_copies(lo, hi, n):
        return [
            pltpu.make_async_copy(a.at[lo:hi], out.at[lo:hi], local.at[n + m])
            for m, (a, out) in enumerate(((q_all, q_out), (k_all, k_out), (v_all, v_out)))
        ]

    early, late = qkv_copies(0, first, 6), qkv_copies(first, groups, 9)

    def table_rows(i):
        chosen = jnp.full((1, GROUP), table[i], jnp.int32) > 0
        return jnp.where(chosen, cos[BLK:, :], cos[:BLK, :]), jnp.where(chosen, sin[BLK:, :], sin[:BLK, :])

    def project(w, bias, lo, hi):
        count = hi - lo
        for i in range(4):
            rows = slice(i * BLK, (i + 1) * BLK)
            out = dot(hidden[rows, :], w, NT)
            cosines, sines = table_rows(i)
            for s in range(3):
                for n in range(count):
                    at = (s * count + n) * GROUP
                    part = out[:, at : at + GROUP] + bias[s : s + 1, n * GROUP : (n + 1) * GROUP]
                    if s == 0:
                        part = rotate(part, cosines, sines) * (HD ** (-0.5) * log2_e)
                        q_all[lo + n, rows, :] = part.astype(bf16)
                    elif s == 1:
                        k_all[lo + n, rows, :] = rotate(part, cosines, sines).astype(bf16)
                    else:
                        v_all[lo + n, rows, :] = part.astype(bf16)

    @pl.when(step == 0)
    def _():
        for made in x_copies:
            made.start()
        scalars = [side_long, side_long, mid_long, 4 * mp, 4 * mp + 1, 2 + mp, 3 - mp, *table, mp, 1 + mp, 2 - 2 * mp]
        for n, value in enumerate(scalars):
            sc[n] = value
        b_mine[...] = jnp.zeros_like(b_mine)
        b_mine[:3, :half] = b_own[...].astype(f32)
        b_mine[3:4, :] = wide(b_up)
        barrier = pltpu.get_barrier_semaphore()
        for dev in (across, core, side):
            pl.semaphore_signal(barrier, inc=1, device_id=dev, device_id_type=pl.DeviceIdType.MESH)
        pl.semaphore_wait(barrier, 3)
        w_across.start()
        b_across.start()
        for made in x_copies:
            made.wait()
        for i in range(4):
            rows = slice(i * BLK, (i + 1) * BLK)
            normed, _ = normalize(x_all[rows, :].astype(f32))
            fresh = (normed * wide(gain) + wide(shift)).astype(bf16)
            hidden[rows, :] = fresh
            ht[:, rows] = fresh.T
        ht_copy.start()
        w_copies[0].start()
        near_cos[...], near_sin[...] = table_rows(2)
        w = jnp.concatenate([w_own[s, : first * GROUP, :] for s in range(3)], 0)
        project(w, b_mine[:3, : first * GROUP], 0, first)
        for made in early:
            made.start()

    @pl.when(step == 3)
    def _():
        w_across.wait()
        w_core.start()
        b_across.wait()
        by_across[0].start()

    @pl.when(step == 3 * first)
    def _():
        by_across[1].start()
        w_core.wait()
        w_copies[1].start()
        tail = first * GROUP
        w = jnp.concatenate([part for s in range(3) for part in (w_own[s, tail:, :], w_in[s])], 0)
        bias = jnp.concatenate([b_mine[:3, tail:half], b_in[:3, :half]], 1)
        project(w, bias, first, groups)
        for made in late:
            made.start()

    @pl.when(step == 3 * first + 1)
    def _():
        by_across[0].wait()
        by_side[0].start()

    @pl.when(step == 3 * first + 2)
    def _():
        by_across[1].wait()
        by_side[1].start()
        out_across.start()

    @pl.when(step == 3 * first + 6)
    def _():
        by_side[0].wait()
        for made in by_core[:2]:
            made.start()

    @pl.when(step == 3 * groups - 1)
    def _():
        by_side[1].wait()
        for made in by_core[2:]:
            made.start()

    keys = pl.ds(pl.multiple_of(b // 2 * LONG, LONG), LONG)
    q = q_all[g, pl.ds(pl.multiple_of(b * BLK, BLK), BLK), :]
    refs = (q, k_all.at[g, keys, :], v_all.at[g, keys, :], o_ref, l_ref, e_ref, store)
    off = lambda allowed: jnp.where(allowed, 0.0, -1e30).astype(f32)

    @pl.when(b != 2)
    def _():
        attend_body(*refs, [off((b == n) | (side_long == 1)) for n in range(2)])

    @pl.when(b == 2)
    def _():
        attend_body(*refs, [off(True), off(mid_long == 1)])

    @pl.when(step == 3 * groups - 1)
    def _():
        b_all[:, : b_mine.shape[1]] = b_mine[3:4, :]
        b_all[:, b_mine.shape[1] :] = b_in[3:4, :]
        out_across.wait()
        for made in by_core:
            made.wait()
        for made in (*early, *late, *w_copies, ht_copy):
            made.wait()


def front(lengths, gain, shift, b_own, b_up, cos, sin, w_own, tokens, w_out, w_up, w_down):
    d = tokens.shape[1]
    groups = d // GROUP
    heads = GROUP // HD
    half = w_own.shape[1]
    own, rows = 3 * BLK, 4 * BLK
    one = pl.Buffered(buffer_count=1)
    whole = lambda a: pl.BlockSpec(a.shape, lambda g, b: (0,) * a.ndim, pipeline_mode=one)
    os = pl.BlockSpec((None, BLK, GROUP), lambda g, b: (g, b, 0))
    es = pl.BlockSpec((heads, LONG, BLK), lambda g, b: (g * 3 + b, 0, 0))
    hbm = pl.BlockSpec(memory_space=pl.ANY)
    held = jax.ShapeDtypeStruct((groups, rows, GROUP), bf16)
    copies = 2 + 2 + 2 + 2 + 4
    return pl.pallas_call(
        functools.partial(front_kernel, half // GROUP),
        grid=(groups, 3),
        in_specs=[pl.BlockSpec(memory_space=pltpu.SMEM)]
        + [whole(a) for a in (gain, shift, b_own, b_up, cos, sin, w_own)]
        + [hbm] * 4,
        out_specs=[os, os, es]
        + [hbm] * 8
        + [pl.BlockSpec((1, 2 * b_up.shape[0]), lambda g, b: (0, 0)), pl.BlockSpec(memory_space=pltpu.SMEM)]
        + [pl.BlockSpec((BLK, GROUP), lambda g, b: (0, 0))] * 2,
        out_shape=[
            jax.ShapeDtypeStruct((groups, own, GROUP), bf16),
            jax.ShapeDtypeStruct((groups, own, GROUP), f32),
            jax.ShapeDtypeStruct((groups * 3 * heads, LONG, BLK), bf16),
            held,
            held,
            held,
            jax.ShapeDtypeStruct((d, rows), bf16),
            jax.ShapeDtypeStruct((3, 2 * half, d), bf16),
            jax.ShapeDtypeStruct(w_out.shape, bf16),
            jax.ShapeDtypeStruct(w_up.shape, bf16),
            jax.ShapeDtypeStruct(w_down.shape, bf16),
            jax.ShapeDtypeStruct((1, 2 * b_up.shape[0]), f32),
            jax.ShapeDtypeStruct((14,), jnp.int32),
            jax.ShapeDtypeStruct((BLK, GROUP), f32),
            jax.ShapeDtypeStruct((BLK, GROUP), f32),
        ],
        scratch_shapes=[
            pltpu.VMEM((2, LONG, BLK), f32),
            pltpu.VMEM((rows, d), bf16),
            pltpu.VMEM((rows, d), bf16),
            pltpu.VMEM((groups, rows, GROUP), bf16),
            pltpu.VMEM((groups, rows, GROUP), bf16),
            pltpu.VMEM((groups, rows, GROUP), bf16),
            pltpu.VMEM((d, rows), bf16),
            pltpu.VMEM(w_own.shape, bf16),
            pltpu.VMEM((8, b_up.shape[0]), f32),
            pltpu.VMEM((8, b_up.shape[0]), f32),
            pltpu.SemaphoreType.DMA((12,)),
            pltpu.SemaphoreType.DMA((copies,)),
            pltpu.SemaphoreType.DMA((copies,)),
        ],
        compiler_params=pltpu.CompilerParams(
            vmem_limit_bytes=VMEM_LIMIT, collective_id=1, has_side_effects=True
        ),
        cost_estimate=pl.CostEstimate(
            flops=50_000_000_000, bytes_accessed=100_000_000, transcendentals=31_000_000
        ),
        name="front",
    )(lengths, gain, shift, b_own, b_up, cos, sin, w_own, tokens, w_out, w_up, w_down)


def attend_back_body(
    q_ref, k_ref, v_ref, do_ref, o_ref, l_ref, e_ref, prod, dk_sum, dv_sum, start, count
):
    lane = lax.broadcasted_iota(jnp.int32, (1, GROUP), 1) // HD
    heads = GROUP // HD
    q = q_ref[...]
    do = (do_ref[...].astype(f32) * l_ref[...]).astype(bf16)
    both = do.astype(f32) * o_ref[...].astype(f32)
    upper = both.astype(bf16)
    lower = (both - upper.astype(f32)).astype(bf16)
    pick = (
        lax.broadcasted_iota(jnp.int32, (8, GROUP), 0)
        == lax.broadcasted_iota(jnp.int32, (8, GROUP), 1) // HD
    )
    pick = pick.astype(f32).astype(bf16)
    delta = dot(pick, upper, NT) + dot(pick, lower, NT)
    keys_t = k_ref[pl.ds(start, count), :].T
    chunks = count // BLK
    tiles = [(h, c) for h in range(heads) for c in range(chunks)]

    def grad_probs(i):
        h, c = tiles[i]
        values = v_ref[pl.ds(start + c * BLK, BLK), :]
        prod[i % 2] = dot(jnp.where(lane == h, values, jnp.zeros_like(values)), do, NT)

    grad_probs(0)
    dq_t = [None] * heads
    for i, (h, c) in enumerate(tiles):
        if i + 1 < len(tiles):
            grad_probs(i + 1)
        rows = pl.ds(start + c * BLK, BLK)
        expo = e_ref[h, rows, :]
        ds = (expo.astype(f32) * (prod[i % 2] - delta[h : h + 1])).astype(bf16)
        dv_sum[rows, :] += dot(expo, jnp.where(lane == h, do, jnp.zeros_like(do)))
        dk_sum[rows, :] += dot(ds, jnp.where(lane == h, q, jnp.zeros_like(q)))
        part = dot(keys_t[HD * h : HD * (h + 1), c * BLK : (c + 1) * BLK], ds)
        dq_t[h] = part if dq_t[h] is None else dq_t[h] + part
    return jnp.concatenate(dq_t, 0).T


def window_back(dq, dk_sum, dv_sum, tables, w_ref, ht_ref, dh_sum):
    parts = [] if dq is None else [dq]
    dk = dk_sum[...] * ln_2
    rotated = []
    for n, (cos, sin) in enumerate(tables):
        rotated.append(rotate_back(dk[n * BLK : (n + 1) * BLK], cos[...], sin[...]))
    parts.append(jnp.concatenate(rotated, 0).astype(bf16))
    parts.append(dv_sum[...].astype(bf16))
    both = jnp.concatenate(parts, 1)
    w = jnp.concatenate([w_ref[s] for s in range(3 - len(parts), 3)], 0)
    for n in range(len(tables)):
        rows = slice(n * BLK, (n + 1) * BLK)
        dh_sum[rows, :] += dot(both[rows], w)
    return dot(ht_ref[...], both), jnp.sum(both.astype(f32), 0, keepdims=True)


def back_kernel(
    mode, sc, q_ref, k_ref, v_ref, do_ref, o_ref, l_ref, e_ref, cos, sin, cos0, sin0, cos1, sin1, w_ref, ht_ref,
    *rest,
):
    g = pl.program_id(0)
    last_g = pl.num_programs(0) - 1
    step = pl.program_id(1)
    if mode == "whole":
        x_ref, gain, mid_ref, g_ref, gb_ref, out_ref, small, dq_cat, prod, dk_sum, dv_sum, dh_sum = rest
    elif mode == "far":
        before, before_b, g_ref, gb_ref, dq_out, part_ref, prod, dk_sum, dv_sum, dh_sum = rest
    else:
        before, before_b, dq_in, g_ref, gb_ref, own_ref, prod, dk_sum, dv_sum, dh_sum = rest
    refs = (q_ref, k_ref, v_ref, do_ref, o_ref, l_ref, e_ref, prod, dk_sum, dv_sum)
    own_tables = (cos0, sin0), (cos1, sin1)
    finish_q = lambda dq: rotate_back(dq * (HD ** (-0.5)), cos[...], sin[...]).astype(bf16)

    @pl.when(step == 0)
    def _():
        dk_sum[...] = jnp.zeros_like(dk_sum)
        dv_sum[...] = jnp.zeros_like(dv_sum)

    @pl.when((step == 0) & (g == 0))
    def _():
        dh_sum[...] = jnp.zeros_like(dh_sum)

    if mode == "whole":
        place = pl.ds(pl.multiple_of(step * BLK, BLK), BLK)

        @pl.when(sc[FLAG] == 1)
        def _():
            dq_cat[place, :] = finish_q(attend_back_body(*refs, 0, LONG))

        @pl.when(sc[FLAG] == 0)
        def _():
            dq_cat[place, :] = finish_q(attend_back_body(*refs, pl.multiple_of(step * BLK, BLK), BLK))

        @pl.when(step == 1)
        def _():
            g_ref[...], gb_ref[...] = window_back(
                dq_cat[...], dk_sum, dv_sum, own_tables, w_ref, ht_ref, dh_sum
            )

        @pl.when((step == 1) & (g == last_g))
        def _():
            sums = [None, None]
            for rows in (slice(0, BLK), slice(BLK, LONG)):
                out, *terms = finish_rows(x_ref[rows, :], wide(gain), mid_ref[rows, :], dh_sum[rows, :])
                out_ref[rows, :] = out
                for n, term in enumerate(terms):
                    sums[n] = term if sums[n] is None else sums[n] + term
            small[...] = jnp.concatenate(sums + [jnp.zeros_like(sums[0])] * 6, 0)

    elif mode == "far":

        @pl.when(sc[FLAG + 2] == 1)
        def _():
            dq_out[...] = attend_back_body(*refs, 0, BLK)

        @pl.when(sc[FLAG + 2] == 0)
        def _():
            dq_out[...] = jnp.zeros_like(dq_out)

        weight, bias = window_back(None, dk_sum, dv_sum, own_tables[:1], w_ref, ht_ref, dh_sum)
        g_ref[:, :GROUP] = before[:, :GROUP]
        g_ref[:, GROUP:] = before[:, GROUP:] + weight
        gb_ref[:, :GROUP] = before_b[:, :GROUP]
        gb_ref[:, GROUP:] = before_b[:, GROUP:] + bias

        @pl.when(g == last_g)
        def _():
            part_ref[...] = dh_sum[...].astype(bf16)

    else:
        dq = finish_q(attend_back_body(*refs, 0, BLK) + dq_in[...])
        weight, bias = window_back(dq, dk_sum, dv_sum, own_tables[:1], w_ref, ht_ref, dh_sum)
        weight = weight + before[...]
        gb_ref[...] = bias + before_b[...]
        g_ref[...] = weight.astype(bf16)

        @pl.when(g == last_g)
        def _():
            own_ref[...] = dh_sum[...]


def back(mode, sc, q, k, v, do, o, inverse, expo, cos, sin, w, hidden_t, more):
    groups = o.shape[0]
    d = w.shape[2]
    heads = GROUP // HD
    blocks = 2 if mode == "whole" else 1
    query = 0 if mode == "whole" else 2
    key = {"whole": 0, "far": 3, "near": 2}[mode]
    keys = LONG if mode == "whole" else BLK
    one = pl.Buffered(buffer_count=1)
    qs = pl.BlockSpec((None, BLK, GROUP), lambda g, b, s: (g, b + query, 0))
    ks = pl.BlockSpec((None, keys, GROUP), lambda g, b, s: (g, key, 0))
    os = pl.BlockSpec((None, BLK, GROUP), lambda g, b, s: (g, b + query, 0))
    es = pl.BlockSpec((heads, keys, BLK), lambda g, b, s: (g * 3 + b + query, 1 if mode == "far" else 0, 0))
    tq = pl.BlockSpec((BLK, GROUP), lambda g, b, s: (s[TABLE + b + query], 0))
    t0 = pl.BlockSpec((BLK, GROUP), lambda g, b, s: (s[TABLE + key], 0))
    t1 = pl.BlockSpec((BLK, GROUP), lambda g, b, s: (s[TABLE + key + (blocks - 1)], 0))
    weight = pl.BlockSpec((None, d, 3 * GROUP), lambda g, b, s: (g, 0, 0))
    bias = pl.BlockSpec((None, 1, 3 * GROUP), lambda g, b, s: (g, 0, 0))
    dq_part = pl.BlockSpec((None, BLK, GROUP), lambda g, b, s: (g, 0, 0))
    whole = lambda *shape: pl.BlockSpec(shape, lambda g, b, s: (0, 0))
    in_specs = [qs, ks, ks, os, os, os, es, tq, tq, t0, t0, t1, t1]
    in_specs += [
        pl.BlockSpec((3, GROUP, d), lambda g, b, s: (0, g, 0)),
        pl.BlockSpec((d, keys), lambda g, b, s: (0, key), pipeline_mode=one),
    ]
    bias_shape = jax.ShapeDtypeStruct((groups, 1, 3 * GROUP), f32)
    scratch = [
        pltpu.VMEM((2, BLK, BLK), f32),
        pltpu.VMEM((keys, GROUP), f32),
        pltpu.VMEM((keys, GROUP), f32),
        pltpu.VMEM((keys, d), f32),
    ]
    if mode == "whole":
        in_specs += [
            pl.BlockSpec((LONG, d), lambda g, b, s: (s[BLOCK] // 2, 0), pipeline_mode=one),
            pl.BlockSpec((d,), lambda g, b, s: (0,)),
            pl.BlockSpec((LONG, d), lambda g, b, s: (0, 0), pipeline_mode=one),
        ]
        out_specs = [weight, bias, whole(LONG, d), whole(8, d)]
        out_shape = [
            jax.ShapeDtypeStruct((groups, d, 3 * GROUP), f32),
            bias_shape,
            jax.ShapeDtypeStruct((LONG, d), bf16),
            jax.ShapeDtypeStruct((8, d), f32),
        ]
        scratch = [pltpu.VMEM((LONG, GROUP), bf16)] + scratch
    elif mode == "far":
        in_specs += [weight, bias]
        out_specs = [weight, bias, dq_part, whole(BLK, d)]
        out_shape = [
            jax.ShapeDtypeStruct((groups, d, 3 * GROUP), f32),
            bias_shape,
            jax.ShapeDtypeStruct((groups, BLK, GROUP), f32),
            jax.ShapeDtypeStruct((BLK, d), bf16),
        ]
    else:
        in_specs += [weight, bias, dq_part]
        out_specs = [weight, bias, whole(BLK, d)]
        out_shape = [
            jax.ShapeDtypeStruct((groups, d, 3 * GROUP), bf16),
            bias_shape,
            jax.ShapeDtypeStruct((BLK, d), f32),
        ]
    return pl.pallas_call(
        functools.partial(back_kernel, mode),
        grid_spec=pltpu.PrefetchScalarGridSpec(
            num_scalar_prefetch=1,
            grid=(groups, blocks),
            in_specs=in_specs,
            out_specs=out_specs,
            scratch_shapes=scratch,
        ),
        out_shape=out_shape,
        compiler_params=pltpu.CompilerParams(vmem_limit_bytes=VMEM_LIMIT),
        cost_estimate=pl.CostEstimate(
            flops=groups * blocks * keys * 5_000_000, bytes_accessed=groups * blocks * 6_000_000, transcendentals=0
        ),
        name="back_" + mode,
    )(sc, q, k, v, do, o, inverse, expo, cos, sin, cos, sin, cos, sin, w, hidden_t, *more)


def gelu_parts(z):
    density = jnp.exp2(z * z * (-0.5 * log2_e)) * 0.3989422804014327
    t = 1.0 / (1.0 + 0.2316419 * jnp.abs(z))
    poly = t * (
        0.319381530
        + t * (-0.356563782 + t * (1.781477937 + t * (-1.821255978 + t * 1.330274429)))
    )
    tail = density * poly
    cdf = jnp.where(z >= 0, 1.0 - tail, tail)
    return z * cdf, cdf + z * density


def middle_kernel(
    sc, tokens, cotangent, o_hbm, w_out_own, w_out_other, b_out, gain, shift,
    up_a, up_b, up_c, up_d, b_up, down_a, down_b, down_c, down_d, b_down,
    out_hbm, mid_hbm, do_hbm, g_ref, g_out, g_bup, g_small,
    w_out, r1, h2, h2t, dy, dyt, acc, back, x_ref, o_ref, out_ref, do_ref, arrive, leave,
):
    i = pl.program_id(0)
    last = pl.num_programs(0) - 1
    blocks = [slice(j * BLK, (j + 1) * BLK) for j in range(3)]
    groups = o_ref.shape[0]
    block = lambda at: pl.ds(pl.multiple_of(at * BLK, BLK), BLK)
    o_in = [pltpu.make_async_copy(o_hbm.at[:, rows, :], o_ref.at[:, rows, :], arrive.at[j]) for j, rows in enumerate(blocks)]
    x_in = [
        pltpu.make_async_copy(tokens.at[block(sc[BLOCK + j]), :], x_ref.at[rows, :], arrive.at[3 + j])
        for j, rows in enumerate(blocks)
    ]
    y_in = [
        pltpu.make_async_copy(cotangent.at[block(sc[BLOCK + j]), :], dy.at[rows, :], arrive.at[6 + j])
        for j, rows in enumerate(blocks)
    ]
    leaving = [
        (
            pltpu.make_async_copy(out_ref.at[rows, :], out_hbm.at[block(sc[PLACE + j]), :], leave.at[j]),
            pltpu.make_async_copy(r1.at[rows, :], mid_hbm.at[rows, :], leave.at[3 + j]),
            pltpu.make_async_copy(do_ref.at[:, rows, :], do_hbm.at[:, rows, :], leave.at[6 + j]),
        )
        for j, rows in enumerate(blocks)
    ]
    heads_of = lambda rows: jnp.concatenate([o_ref[g, rows, :] for g in range(groups)], 1)

    @pl.when(i == 0)
    def _():
        for made in [m for pair in zip(o_in, x_in) for m in pair] + y_in:
            made.start()
        w_out[: w_out_own.shape[0], :] = w_out_own[...]
        w_out[w_out_own.shape[0] :, :] = w_out_other[...]
        for j, rows in enumerate(blocks):
            o_in[j].wait()
            x_in[j].wait()
            mixed = dot(heads_of(rows), w_out[...]) + wide(b_out) + x_ref[rows, :].astype(f32)
            r1[rows, :] = mixed
            normed, _ = normalize(mixed)
            hidden = (normed * wide(gain) + wide(shift)).astype(bf16)
            h2[rows, :] = hidden
            h2t[:, rows] = hidden.T
            acc[rows, :] = jnp.zeros_like(mixed)
            back[rows, :] = jnp.zeros_like(mixed)
        for j, rows in enumerate(blocks):
            y_in[j].wait()
            dyt[:, rows] = dy[rows, :].T

    @pl.when(i < last)
    def _():
        first, second = 2 * i < last, 2 * i + 1 < last
        w_up = jnp.concatenate(
            [jnp.where(first, up_a[...], up_c[...]), jnp.where(second, up_b[...], up_d[...])], 1
        )
        w_down = jnp.concatenate(
            [jnp.where(first, down_a[...], down_c[...]), jnp.where(second, down_b[...], down_d[...])], 0
        )
        bias = b_up[...]
        width = up_a.shape[1]
        total = dy.shape[0]
        parts = [slice(j, j + 256) for j in range(0, total, BLK // 2)]
        count = len(parts)
        actives, grads = [None] * count, [None] * count
        ups, downs = [None] * count, [None] * count
        col_sum = None

        def ahead(j):
            ups[j] = dot(h2[parts[j], :], w_up) + bias
            downs[j] = dot(dy[parts[j], :], w_down, NT)

        ahead(0)
        for j, rows in enumerate(parts):
            if j + 1 < count:
                ahead(j + 1)
            active, slope = gelu_parts(ups[j])
            actives[j] = active.astype(bf16)
            grads[j] = (downs[j] * slope).astype(bf16)
            s = jnp.sum(grads[j].astype(f32), 0, keepdims=True)
            col_sum = s if col_sum is None else col_sum + s
            acc[rows, :] += dot(actives[j], w_down)
            back[rows, :] += dot(grads[j], w_up, NT)
        g_bup[...] = col_sum
        g_up = dot(h2t[...], jnp.concatenate(grads, 0)).astype(bf16)
        g_down = dot(dyt[...], jnp.concatenate(actives, 0)).astype(bf16)
        for n in range(2):
            cols = slice(n * width, (n + 1) * width)
            g_ref[:, 2 * n * width : (2 * n + 1) * width] = g_up[:, cols]
            g_ref[:, (2 * n + 1) * width : (2 * n + 2) * width] = g_down[:, cols]

    @pl.when(i == last)
    def _():
        sums = [None] * 4
        lows = []
        for j, rows in enumerate(blocks):
            mixed = r1[rows, :]
            out_ref[rows, :] = (acc[rows, :] + wide(b_down) + mixed).astype(bf16)
            normed, inverse = normalize(mixed)
            top = dy[rows, :].astype(f32)
            dh = back[rows, :]
            dr = top + normalize_back(normed, inverse, dh * wide(gain))
            r1[rows, :] = dr
            low = dr.astype(bf16)
            lows.append(low)
            do = dot(low, w_out[...], NT).astype(bf16)
            for g in range(groups):
                do_ref[g, rows, :] = do[:, g * GROUP : (g + 1) * GROUP]
            for made in leaving[j]:
                made.start()
            for n, term in enumerate((dh * normed, dh, dr, top)):
                s = jnp.sum(term, 0, keepdims=True)
                sums[n] = s if sums[n] is None else sums[n] + s
        g_out[...] = dot(jnp.concatenate(lows, 0).T, heads_of(slice(0, 3 * BLK))).astype(bf16)
        g_small[...] = jnp.concatenate(sums + [jnp.zeros_like(sums[0])] * 4, 0)
        for parts in leaving:
            for made in parts:
                made.wait()


def middle(sc, tokens, cotangent, o, w_out_own, w_out_other, b_out, gain, shift, up_own, down_own, up_other, down_other, b_up, b_down):
    d = tokens.shape[1]
    groups = o.shape[0]
    own = 3 * BLK
    half = up_own.shape[1]
    piece = 256
    per = half // piece
    steps = per + 1
    one = pl.Buffered(buffer_count=1)
    whole = lambda *shape: pl.BlockSpec(shape, lambda i, s: (0,) * len(shape), pipeline_mode=one)
    hbm = pl.BlockSpec(memory_space=pl.ANY)
    fixed = lambda *shape: pl.BlockSpec(shape, lambda i, s: (0,) * len(shape))
    at = lambda i: jnp.minimum(i, per - 1)
    places = [
        lambda i: jnp.minimum(2 * i, per - 1),
        lambda i: jnp.minimum(2 * i + 1, per - 1),
        lambda i: jnp.clip(2 * i - per, 0, per - 1),
        lambda i: jnp.clip(2 * i + 1 - per, 0, per - 1),
    ]
    ups = [pl.BlockSpec((d, piece), functools.partial(lambda p, i, s: (0, p(i)), p)) for p in places]
    downs = [pl.BlockSpec((piece, d), functools.partial(lambda p, i, s: (p(i), 0), p)) for p in places]
    return pl.pallas_call(
        middle_kernel,
        grid_spec=pltpu.PrefetchScalarGridSpec(
            num_scalar_prefetch=1,
            grid=(steps,),
            in_specs=[hbm, hbm, hbm]
            + [
                whole(*w_out_own.shape),
                whole(*w_out_other.shape),
                whole(d),
                whole(d),
                whole(d),
                *ups,
                pl.BlockSpec((1, 2 * piece), lambda i, s: (0, at(i))),
                *downs,
                whole(d),
            ],
            out_specs=[
                hbm,
                hbm,
                hbm,
                pl.BlockSpec((d, 4 * piece), lambda i, s: (0, at(i))),
                fixed(d, d),
                pl.BlockSpec((1, 2 * piece), lambda i, s: (0, at(i))),
                fixed(8, d),
            ],
            scratch_shapes=[
                pltpu.VMEM((d, d), bf16),
                pltpu.VMEM((own, d), f32),
                pltpu.VMEM((own, d), bf16),
                pltpu.VMEM((d, own), bf16),
                pltpu.VMEM((own, d), bf16),
                pltpu.VMEM((d, own), bf16),
                pltpu.VMEM((own, d), f32),
                pltpu.VMEM((own, d), f32),
                pltpu.VMEM((own, d), bf16),
                pltpu.VMEM((groups, own, GROUP), bf16),
                pltpu.VMEM((own, d), bf16),
                pltpu.VMEM((groups, own, GROUP), bf16),
                pltpu.SemaphoreType.DMA((9,)),
                pltpu.SemaphoreType.DMA((9,)),
            ],
        ),
        out_shape=[
            jax.ShapeDtypeStruct((own, d), bf16),
            jax.ShapeDtypeStruct((own, d), f32),
            jax.ShapeDtypeStruct((groups, own, GROUP), bf16),
            jax.ShapeDtypeStruct((d, 4 * half), bf16),
            jax.ShapeDtypeStruct((d, d), bf16),
            jax.ShapeDtypeStruct((1, 2 * half), f32),
            jax.ShapeDtypeStruct((8, d), f32),
        ],
        compiler_params=pltpu.CompilerParams(vmem_limit_bytes=VMEM_LIMIT),
        cost_estimate=pl.CostEstimate(
            flops=2 * own * d * (3 * d + 12 * half), bytes_accessed=40_000_000, transcendentals=8_000_000
        ),
        name="middle",
    )(sc, tokens, cotangent, o, w_out_own, w_out_other, b_out, gain, shift,
      *[up_own] * 2, *[up_other] * 2, b_up, *[down_own] * 2, *[down_other] * 2, b_down)


def finish_rows(x, gain, mid, dh):
    normed, inverse = normalize(x.astype(f32))
    out = (mid + normalize_back(normed, inverse, dh * gain)).astype(bf16)
    return out, jnp.sum(dh * normed, 0, keepdims=True), jnp.sum(dh, 0, keepdims=True)


def lines(v):
    return jnp.concatenate([v[:, j * GROUP : (j + 1) * GROUP] for j in range(v.shape[1] // GROUP)], 0)


def last_kernel(
    q_ref, k_ref, v_ref, do_ref, o_ref, l_ref, e_ref, cos, sin, w_ref, ht_ref, before, before_b, dq_in, gout_ref,
    part_ref, tokens, gain, mid, small_w, small_two, gup_ref, early_ref,
    sum_out, theirs_out, small_out, small_theirs_out, rows_out, rows_theirs_out, early_out,
    prod, dk_sum, dv_sum, dh_sum, gb_sum, g_all, part_in, x_ref, mid_ref, early_part,
    r1, a1, r2, a2, r3, sums, theirs, rows_ref, row_ends, s0, s1, s2, s3, q1, q2, q3, q4, send, recv, local,
):
    g = pl.program_id(0)
    groups = g_all.shape[3]
    here = lax.axis_index("dp")
    mp = lax.axis_index("mp")
    c = here % 2
    x = (here // 2) % 2
    z = here // 4
    core = (here + 1 - 2 * c, mp)
    side = (here + 2 - 4 * x, mp)
    across = (here, 1 - mp)
    line = [((z + n) % 4, ((z + n) % 4 * 4 + here % 4, mp)) for n in (1, 2, 3)]

    numbers = {}

    def copy(name, src, dst, dev):
        n = numbers.setdefault(name, len(numbers))
        return pltpu.make_async_remote_copy(
            src_ref=src,
            dst_ref=dst,
            send_sem=send.at[n],
            recv_sem=recv.at[n],
            device_id=dev,
            device_id_type=pl.DeviceIdType.MESH,
        )

    part_copy = copy("part", part_ref, part_in, across)
    early_copy = copy("early", early_part, early_out, across)
    pieces_of_rows = [slice(n, n + BLK // 4) for n in range(0, BLK, BLK // 4)]
    rows_copies = [copy(("r", n), rows_ref.at[h, :], rows_theirs_out.at[h, :], across) for n, h in enumerate(pieces_of_rows)]
    rows_keep = pltpu.make_async_copy(rows_ref, rows_out, local.at[2])
    by_core = [copy(("c", n), g_all.at[:, :, 1 - c, n], r1.at[:, :, n], core) for n in range(groups)]
    by_side = [copy(("x", n), a1.at[:, 1 - x, n], r2.at[:, n], side) for n in range(groups)]
    by_line = [
        [copy(("z", n, m), a2.at[at, n], r3.at[m, n], dev) for m, (at, dev) in enumerate(line)]
        for n in range(groups)
    ]
    by_across = [copy(("y", n), sums.at[n], theirs.at[n], across) for n in range(groups)]
    small_core = copy("sc", s0, q1, core)
    small_side = copy("sx", s1, q2, side)
    small_line = [copy(("sz", m), s2, q3.at[z], dev) for m, (_, dev) in enumerate(line)]
    small_across = copy("sy", s3, q4, across)
    rows = pl.ds(pl.multiple_of((2 + mp) * BLK, BLK), BLK)
    x_copy = pltpu.make_async_copy(tokens.at[rows, :], x_ref, local.at[0])
    mid_copy = pltpu.make_async_copy(mid.at[2 * BLK : 3 * BLK, :], mid_ref, local.at[1])

    partners = [core, side, across] + [dev for _, dev in line]

    @pl.when(g == 0)
    def _():
        barrier = pltpu.get_barrier_semaphore()
        for dev in partners:
            pl.semaphore_signal(barrier, inc=1, device_id=dev, device_id_type=pl.DeviceIdType.MESH)
        x_copy.start()
        mid_copy.start()
        dh_sum[...] = jnp.zeros_like(dh_sum)
        share, width = early_ref.shape[0], early_part.shape[1]
        start = gup_ref.shape[1]
        early_part[share:, :] = jnp.zeros((early_part.shape[0] - share, width), bf16)
        early_part[:share, :] = early_ref[:, start : start + width]

    def second(n):
        by_core[n].wait()
        a1[:, :, n] = (g_all[:, :, c, n].astype(f32) + r1[:, :, n].astype(f32)).astype(bf16)
        by_side[n].start()

    def third(n):
        by_side[n].wait()
        a2[:, n] = (a1[:, x, n].astype(f32) + r2[:, n].astype(f32)).astype(bf16)
        for made in by_line[n]:
            made.start()

    def fourth(n):
        for made in by_line[n]:
            made.wait()
        total = a2[z, n].astype(f32)
        for m in range(3):
            total = total + r3[m, n].astype(f32)
        sums[n] = total.astype(bf16)
        by_across[n].start()

    dk_sum[...] = jnp.zeros_like(dk_sum)
    dv_sum[...] = jnp.zeros_like(dv_sum)
    refs = (q_ref, k_ref, v_ref, do_ref, o_ref, l_ref, e_ref, prod, dk_sum, dv_sum)
    dq = (attend_back_body(*refs, 0, BLK) + dq_in[...]) * (HD ** (-0.5))

    @pl.when(g == 0)
    def _():
        pl.semaphore_wait(pltpu.get_barrier_semaphore(), len(partners))
        part_copy.start()
        early_copy.start()

    for n in range(1, groups):

        @pl.when(g == n)
        def _(n=n):
            for late, stage in ((1, second), (2, third), (3, fourth)):
                if n >= late:
                    stage(n - late)

    dq = rotate_back(dq, cos[...], sin[...]).astype(bf16)
    weight, bias = window_back(dq, dk_sum, dv_sum, ((cos, sin),), w_ref, ht_ref, dh_sum)
    gb_sum[g] = bias + before_b[...]

    @pl.when(g == groups - 1)
    def _():
        x_copy.wait()
        mid_copy.wait()
        part_copy.wait()
        ends = [0.0, 0.0]
        for n, h in enumerate(pieces_of_rows):
            out, *terms = finish_rows(x_ref[h, :], wide(gain), mid_ref[h, :], dh_sum[h, :] + part_in[h, :].astype(f32))
            rows_ref[h, :] = out
            rows_copies[n].start()
            ends = [a + b for a, b in zip(ends, terms)]
        rows_keep.start()
        row_ends[0:1, :] = ends[0]
        row_ends[1:2, :] = ends[1]

    weight = weight + before[...]
    share = early_ref.shape[0]
    held_rows = 4 * share
    fill = jnp.zeros((g_all.shape[4] - held_rows, GROUP), f32)
    weight = jnp.concatenate([weight, gout_ref[...].astype(f32)], 1)
    for n in range(16):
        part = weight[n * share : (n + 1) * share]
        pieces = [part[:, s * GROUP : (s + 1) * GROUP] for s in range(4)]
        pieces = pieces + [fill] if fill.shape[0] else pieces
        g_all[n // 4, n // 2 % 2, n % 2, g] = jnp.concatenate(pieces, 0).astype(bf16)

    for n in range(groups):

        @pl.when(g == n)
        def _(n=n):
            by_core[n].start()

    @pl.when(g == groups - 1)
    def _():
        n = groups - 1
        held = [lines(small_w[m : m + 1, :] + row_ends[m : m + 1, :]) for m in range(2)]
        held += [lines(small_two[m : m + 1, :]) for m in range(4)]
        held += [gb_sum[m, :, s * GROUP : (s + 1) * GROUP] for s in range(3) for m in range(groups)]
        held.append(lines(gup_ref[...]))
        held = jnp.concatenate(held, 0)
        s0[...] = jnp.concatenate([held, jnp.zeros((s0.shape[0] - held.shape[0], GROUP), f32)], 0)
        small_core.start()
        second(n)
        third(n - 1)
        fourth(n - 2)
        small_core.wait()
        s1[...] = s0[...] + q1[...]
        small_side.start()
        third(n)
        small_side.wait()
        s2[...] = s1[...] + q2[...]
        for made in small_line:
            made.start()
        fourth(n - 1)
        for made in small_line:
            made.wait()
        q3[z] = s2[...]
        s3[...] = (q3[0] + q3[1]) + (q3[2] + q3[3])
        small_across.start()
        fourth(n)
        early_copy.wait()
        small_out[...] = s3[...]
        sum_out[...] = sums[...]
        rows_keep.wait()
        for made in rows_copies:
            made.wait()
        small_across.wait()
        small_theirs_out[...] = q4[...]
        for made in by_across:
            made.wait()
        theirs_out[...] = theirs[...]


def last(q, k, v, do, o, inverse, expo, cos, sin, w, hidden_t, g_sum, gb_sum, dq_far, g_out, part, tokens, gain, mid,
         small_w, small_two, g_bup, early):
    groups = o.shape[0]
    d = w.shape[2]
    heads = GROUP // HD
    share = early.shape[0]
    held = -(-4 * share // 16) * 16
    block = (groups, held, GROUP)
    count = 6 * d // GROUP + groups * 3 + g_bup.shape[1] // GROUP
    small = (-(-count // 8) * 8, GROUP)
    early_part = (-(-share // 16) * 16, g_bup.shape[1])
    copies = 6 + 6 * groups + 6
    one = pl.Buffered(buffer_count=1)
    hbm = pl.BlockSpec(memory_space=pl.ANY)
    whole = lambda a: pl.BlockSpec(a.shape, lambda g: (0,) * a.ndim, pipeline_mode=one)
    fixed = lambda shape: pl.BlockSpec(shape, lambda g: (0,) * len(shape))
    qs = pl.BlockSpec((None, BLK, GROUP), lambda g: (g, 2, 0))
    os = pl.BlockSpec((None, BLK, GROUP), lambda g: (g, 2, 0))
    outs = [(block, bf16), (block, bf16), (small, f32), (small, f32), ((BLK, d), bf16), ((BLK, d), bf16)]
    outs.append((early_part, bf16))
    return pl.pallas_call(
        last_kernel,
        grid=(groups,),
        in_specs=[qs, qs, qs, os, os, os]
        + [
            pl.BlockSpec((heads, BLK, BLK), lambda g: (g * 3 + 2, 0, 0)),
            whole(cos),
            whole(sin),
            pl.BlockSpec((3, GROUP, d), lambda g: (0, g, 0)),
            pl.BlockSpec((d, BLK), lambda g: (0, 2), pipeline_mode=one),
            pl.BlockSpec((None, d, 3 * GROUP), lambda g: (g, 0, 0)),
            pl.BlockSpec((None, 1, 3 * GROUP), lambda g: (g, 0, 0)),
            pl.BlockSpec((None, BLK, GROUP), lambda g: (g, 0, 0)),
            pl.BlockSpec((d, GROUP), lambda g: (0, g)),
            whole(part),
            hbm,
            whole(gain),
            hbm,
            whole(small_w),
            whole(small_two),
            whole(g_bup),
            whole(early),
        ],
        out_specs=[fixed(shape) for shape, _ in outs[:4]] + [hbm] * 3,
        out_shape=[jax.ShapeDtypeStruct(*spec) for spec in outs],
        scratch_shapes=[
            pltpu.VMEM((2, BLK, BLK), f32),
            pltpu.VMEM((BLK, GROUP), f32),
            pltpu.VMEM((BLK, GROUP), f32),
            pltpu.VMEM((BLK, d), f32),
            pltpu.VMEM((groups, 1, 3 * GROUP), f32),
            pltpu.VMEM((4, 2, 2, *block), bf16),
            pltpu.VMEM((BLK, d), bf16),
            pltpu.VMEM((BLK, d), bf16),
            pltpu.VMEM((BLK, d), f32),
            pltpu.VMEM(early_part, bf16),
            pltpu.VMEM((4, 2, *block), bf16),
            pltpu.VMEM((4, 2, *block), bf16),
            pltpu.VMEM((4, *block), bf16),
            pltpu.VMEM((4, *block), bf16),
            pltpu.VMEM((3, *block), bf16),
            pltpu.VMEM(block, bf16),
            pltpu.VMEM(block, bf16),
            pltpu.VMEM((BLK, d), bf16),
            pltpu.VMEM((8, d), f32),
            pltpu.VMEM(small, f32),
            pltpu.VMEM(small, f32),
            pltpu.VMEM(small, f32),
            pltpu.VMEM(small, f32),
            pltpu.VMEM(small, f32),
            pltpu.VMEM(small, f32),
            pltpu.VMEM((4, *small), f32),
            pltpu.VMEM(small, f32),
            pltpu.SemaphoreType.DMA((copies,)),
            pltpu.SemaphoreType.DMA((copies,)),
            pltpu.SemaphoreType.DMA((3,)),
        ],
        compiler_params=pltpu.CompilerParams(
            vmem_limit_bytes=VMEM_LIMIT, collective_id=0, has_side_effects=True
        ),
        cost_estimate=pl.CostEstimate(flops=30_000_000_000, bytes_accessed=100_000_000, transcendentals=0),
        name="last",
    )(q, k, v, do, o, inverse, expo, cos, sin, w, hidden_t, g_sum, gb_sum, dq_far, g_out, part, tokens, gain, mid,
      small_w, small_two, g_bup, early)


def finish_kernel(x_ref, gain, mid_ref, own_ref, part_ref, out_ref, small):
    out, first, second = finish_rows(
        x_ref[...], wide(gain), mid_ref[...], own_ref[...] + part_ref[...].astype(f32)
    )
    out_ref[...] = out
    small[...] = jnp.concatenate([lines(first), lines(second)], 0)


def finish(x, gain, mid, own, part):
    d = x.shape[1]
    return pl.pallas_call(
        finish_kernel,
        out_shape=[jax.ShapeDtypeStruct(x.shape, bf16), jax.ShapeDtypeStruct((2 * d // GROUP, GROUP), f32)],
        compiler_params=pltpu.CompilerParams(vmem_limit_bytes=VMEM_LIMIT),
        name="finish",
    )(x, gain, mid, own, part)


def place_pieces(places, pieces, out_ref, sem):
    mp = lax.axis_index("mp")
    copies = []
    for n, (piece, (zero, one)) in enumerate(zip(pieces, places)):
        start = pl.multiple_of((zero + (one - zero) * mp) * BLK, BLK)
        copies.append(pltpu.make_async_copy(piece, out_ref.at[pl.ds(start, piece.shape[0]), :], sem.at[n]))
        copies[-1].start()
    return copies


def assemble_kernel(places, *rest):
    count = len(places)
    for made in place_pieces(places, rest[:count], rest[count], rest[-1]):
        made.wait()


def assemble(places, pieces, rows):
    count = len(pieces)
    return pl.pallas_call(
        functools.partial(assemble_kernel, places),
        in_specs=[pl.BlockSpec(memory_space=pltpu.VMEM)] * count,
        out_specs=pl.BlockSpec(memory_space=pl.ANY),
        out_shape=jax.ShapeDtypeStruct((rows, pieces[0].shape[1]), pieces[0].dtype),
        scratch_shapes=[pltpu.SemaphoreType.DMA((count,))],
        compiler_params=pltpu.CompilerParams(vmem_limit_bytes=VMEM_LIMIT),
        cost_estimate=pl.CostEstimate(flops=0, bytes_accessed=8_000_000, transcendentals=0),
        name="assemble",
    )(*pieces)


def one_line(v):
    return jnp.concatenate([v[j : j + 1] for j in range(v.shape[0])], 1)


def conclude_kernel(
    share, half, hidden, places, late, late_theirs, early, early_theirs, small, small_theirs, p0, p1, p2, p3,
    g_qkv, g_up, g_down, g_out, g_bqkv, g_bup, grad, *rest,
):
    vectors, sem = rest[:-1], rest[-1]
    copies = place_pieces(places, (p0, p1, p2, p3), grad, sem)
    groups = late.shape[0]
    d = groups * GROUP
    whole = half // GROUP
    for s in range(4):
        rows = slice(s * share, (s + 1) * share)
        mine = [late[g].astype(f32)[rows] for g in range(whole + 1)]
        other = [late_theirs[g].astype(f32)[rows] for g in range(whole, groups)]
        both = jnp.concatenate(mine, 1)[:, :half] + jnp.concatenate(other, 1)[:, half - whole * GROUP :]
        if s < 3:
            g_qkv[s] = both
        else:
            g_out[...] = both
    width = 256
    for c in range(hidden // width):
        mine = early[:, 2 * c * width : 2 * (c + 1) * width].astype(f32)
        other = early_theirs[:share, 2 * c * width : 2 * (c + 1) * width].astype(f32)
        both = mine + other
        cols = slice(c * width, (c + 1) * width)
        g_up[:, cols] = both[:, :width]
        g_down[:, cols] = both[:, width:]
    per = d // GROUP
    for n, ref in enumerate(vectors):
        ref[...] = one_line(small[n * per : (n + 1) * per] + small_theirs[n * per : (n + 1) * per])[0]
    base = 6 * per
    for s in range(3):
        rows = slice(base + s * per, base + (s + 1) * per)
        g_bqkv[s : s + 1, :] = one_line(small[rows])[:, :half] + one_line(small_theirs[rows])[:, half:]
    base += 3 * per
    count = hidden // GROUP
    g_bup[...] = one_line(small[base : base + count] + small_theirs[base + count : base + 2 * count])[0]
    for made in copies:
        made.wait()


def conclude(share, half, hidden, places, args, pieces, rows):
    d = 2 * half
    vmem = pl.BlockSpec(memory_space=pltpu.VMEM)
    return pl.pallas_call(
        functools.partial(conclude_kernel, share, half, hidden, places),
        in_specs=[vmem] * (len(args) + len(pieces)),
        out_specs=[vmem] * 6 + [pl.BlockSpec(memory_space=pl.ANY)] + [vmem] * 6,
        out_shape=[
            jax.ShapeDtypeStruct((3, share, half), f32),
            jax.ShapeDtypeStruct((share, hidden), f32),
            jax.ShapeDtypeStruct((share, hidden), f32),
            jax.ShapeDtypeStruct((share, half), f32),
            jax.ShapeDtypeStruct((3, half), f32),
            jax.ShapeDtypeStruct((hidden,), f32),
            jax.ShapeDtypeStruct((rows, d), bf16),
        ]
        + [jax.ShapeDtypeStruct((d,), f32)] * 6,
        scratch_shapes=[pltpu.SemaphoreType.DMA((len(pieces),))],
        compiler_params=pltpu.CompilerParams(vmem_limit_bytes=VMEM_LIMIT),
        cost_estimate=pl.CostEstimate(flops=1_000_000, bytes_accessed=12_000_000, transcendentals=0),
        name="conclude",
    )(*args, *pieces)


def on_device(
    tokens, lengths, gain_one, shift_one, w_qkv, b_qkv, w_out, b_out, gain_two, shift_two, w_up, b_up, w_down, b_down,
    cotangent,
):
    d = tokens.shape[1]
    n_dp = lax.axis_size("dp")
    swap = [(0, 1), (1, 0)]
    half = w_qkv.shape[2]
    hidden = w_up.shape[1]

    groups = d // GROUP
    share = d // n_dp
    by_hand = n_dp == 16
    tables = tuple(jnp.asarray(t) for t in rope_tables())
    *attended, q, k, v, hidden_t, w_all, w_out_other, up_other, down_other, b_up_all, sc, near_cos, near_sin = front(
        lengths, gain_one, shift_one, b_qkv, b_up, *tables, jnp.transpose(w_qkv, (0, 2, 1)), tokens, w_out, w_up, w_down
    )
    qkv = (q, k, v)
    out_own, grad_mid, do, g_early, g_out, g_bup, small_two = middle(
        sc, tokens, cotangent, attended[0], w_out, w_out_other, b_out, gain_two, shift_two,
        w_up, w_down, up_other, down_other, b_up_all, b_down,
    )
    early = lax.psum_scatter(g_early, "dp", scatter_dimension=0, tiled=True)

    theirs = lax.ppermute(out_own, "mp", swap)
    out_tokens = assemble(((0, 3), (3, 0)), [out_own, theirs], 6 * BLK)
    args = (sc, *qkv, do, *attended, *tables, w_all, hidden_t)
    g_sum, gb_sum, grad_whole, small_w = back("whole", *args, (tokens, gain_one, grad_mid))
    whole_theirs = lax.ppermute(grad_whole, "mp", swap)
    g_sum, gb_sum, dq_far, part = back("far", *args, (g_sum, gb_sum))
    if by_hand:
        part, out_tokens, whole_theirs, early = lax.optimization_barrier((part, out_tokens, whole_theirs, early))
        late, late_theirs, small, small_theirs, shared, shared_theirs, early_theirs = last(
            *args[1:8], near_cos, near_sin, *args[10:], g_sum, gb_sum, dq_far, g_out, part, tokens, gain_one, grad_mid,
            small_w, small_two, g_bup, early,
        )
    else:
        arrived = lax.ppermute(part, "mp", swap)
        g_qkv, g_bqkv, own = back("near", *args, (g_sum, gb_sum, dq_far))
        x_shared = lax.dynamic_slice_in_dim(tokens, sc[BLOCK + 2] * BLK, BLK, 0)
        shared, last_sums = finish(x_shared, gain_one, grad_mid[2 * BLK :], own, arrived)
        g_bqkv = g_bqkv.reshape(groups, 3, GROUP).transpose(1, 0, 2)
        small = jnp.concatenate(
            [
                small_w[:2].reshape(-1, GROUP) + last_sums,
                small_two[:4].reshape(-1, GROUP),
                g_bqkv.reshape(-1, GROUP),
                g_bup.reshape(-1, GROUP),
            ]
        )
        n_small = small.shape[0]
        shared_theirs = lax.ppermute(shared, "mp", swap)
        g_qkv = g_qkv.reshape(groups, d, 3, GROUP).transpose(2, 1, 0, 3).reshape(3, d, d)
        late = lax.psum_scatter(g_qkv, "dp", scatter_dimension=1, tiled=True)
        late_theirs = lax.ppermute(late, "mp", swap)
        small = lax.psum(small, "dp")
        small_theirs = lax.ppermute(small, "mp", swap)
        early_theirs = lax.ppermute(early[:, 2 * hidden :], "mp", swap)
    places = ((0, 4), (2, 3), (3, 2), (4, 0))
    pieces = [grad_whole, shared, shared_theirs, whole_theirs]

    if by_hand:
        g_w, g_up, g_down, g_out, g_bq, g_bu, grad_tokens, *vectors = conclude(
            share, half, hidden, places,
            (late, late_theirs, early, early_theirs, small, small_theirs), pieces, 6 * BLK,
        )
        g_down, g_out = g_down.T, g_out.T
    else:
        grad_tokens = assemble(places, pieces, 6 * BLK)
        mlp = early[:, : 2 * hidden].astype(f32) + early_theirs[:, : 2 * hidden].astype(f32)
        mlp = mlp.reshape(share, hidden // 256, 2, 256)
        g_up = mlp[:, :, 0].reshape(share, hidden)
        g_down = mlp[:, :, 1].reshape(share, hidden).T
        g_out = lax.psum_scatter(g_out, "dp", scatter_dimension=0, tiled=True)
        out_theirs = lax.ppermute(g_out[:, half:], "mp", swap)
        g_out = (g_out[:, :half].astype(f32) + out_theirs.astype(f32)).T
        g_w = late[:, :, :half].astype(f32) + late_theirs[:, :, half:].astype(f32)
        mine, others = small[:n_small].reshape(-1), small_theirs[:n_small].reshape(-1)
        vectors = list((mine[: 6 * d] + others[: 6 * d]).reshape(6, d))
        pair = lambda v, lo, n, w: v[lo : lo + 2 * n * w].reshape(n, 2, w)
        g_bq = pair(mine, 6 * d, 3, half)[:, 0] + pair(others, 6 * d, 3, half)[:, 1]
        g_bu = pair(mine, 9 * d, 1, hidden)[0, 0] + pair(others, 9 * d, 1, hidden)[0, 1]
    return (
        out_tokens,
        grad_tokens,
        vectors[0],
        vectors[1],
        g_w,
        g_bq,
        g_out,
        vectors[4],
        vectors[2],
        vectors[3],
        g_up,
        g_bu,
        g_down,
        vectors[5],
    )


def solution(mesh):
    in_specs = (
        P("dp", None),
        P("dp", None),
        P(),
        P(),
        P(None, None, "mp"),
        P(None, "mp"),
        P("mp", None),
        P(),
        P(),
        P(),
        P(None, "mp"),
        P("mp"),
        P("mp", None),
        P(),
        P("dp", None),
    )
    out_specs = (
        P("dp", None),
        P("dp", None),
        P(),
        P(),
        P(None, "dp", "mp"),
        P(None, "mp"),
        P("mp", "dp"),
        P(),
        P(),
        P(),
        P("dp", "mp"),
        P("mp"),
        P("mp", "dp"),
        P(),
    )
    return jax.shard_map(on_device, mesh=mesh, in_specs=in_specs, out_specs=out_specs, check_vma=False)
```
